32 devices in a mesh: groups: 2 (over y), seq: 2 (over x), frame: 4 (over z), cfg: 2 (over core).
Axes of the slice: x: 2, y: 2, z: 4, core: 2. Of those that a mesh axis runs over, the one named last changes fastest.
Arguments:
- qkv: bfloat16 [2, 4096, 3, 4096], P('cfg', ('groups', 'frame', 'seq')), parts along dimension 1, may hold values from -108 to 108, as said below
- timestep: int32 [2], P('groups'), parts along dimension 0, may hold values from 0 to 999
- windows: int32 [32], replicated, may hold values from 0 to 2
- segments: int32 [16], P('groups'), parts along dimension 0, may hold values from 0 to 3, never falling along the last dimension, each value on 1 to 4 neighbouring positions
Outputs:
- guided: bfloat16 [4096, 16, 256], P(('groups', 'frame', 'seq'), 'cfg'), parts along dimension 0
The draws below stay inside these ranges and needn't reach their ends.
There are 2 independent parts, one for each index of `groups`. The reference program is written for one: setup_inputs(seed, part) draws one part's arguments, and reference() takes and returns one part's arrays. A program takes and returns all parts, laid end to end along the dimension named above; an argument that names none is the same for every part. Nothing has to cross between parts.
Inputs may be any that keep to these rules, and one draw needn't show every extreme that they name: Entries of qkv lie in this range. `segments`: shot numbers never fall from one frame to the next.
All inputs are finite; a program needn't handle non-finite values.
Results may differ from the reference program's by a relative error of at most 0.0053.
Values may be sent and summed in bfloat16 or wider, within the bound.
No kernel may reach another device: no remote copies, remote signals or barrier semaphores. Data moves between devices by JAX's collectives and lax.ppermute only.
A program may use at most 128 MiB of HBM per device.

```python
import math
import jax
import jax.numpy as jnp
import numpy as np
from jax import lax

HD = 128
HEADS = 32
P_SIZE = 256
W_MAX = 2
SEGMENTS = 4
FRAMES = 8
TOKENS = 2048
N_SEQ = 2


def draw_qkv(key, part):
    key = jax.random.fold_in(key, 11)
    streams = jax.random.split(key, 1)
    shape = (2, TOKENS, 3, HEADS * HD)
    spreads = jnp.array([2.0, 1.0, 4.0], jnp.float32).reshape(1, 1, 3, 1)
    base = jnp.clip(jax.random.normal(streams[0], shape, jnp.float32), -5.0, 5.0)
    values = base * spreads
    return values.astype(jnp.bfloat16)


def draw_windows(key, part):
    key = jax.random.fold_in(key, 23)
    order = jax.random.permutation(key, HEADS)
    return (order % (W_MAX + 1)).astype(jnp.int32)


def length_profile(amount, total, most, slope):
    loads = [(1 << 20) // math.isqrt(rank ** slope) + 1 for rank in range(2, amount + 1)]
    spare, counts = total - most - (amount - 1), [1] * (amount - 1)
    while spare > 0:
        free = [i for i in range(amount - 1) if counts[i] < most]
        whole, left = sum([loads[i] for i in free]), spare
        for i in free:
            more = min(most - counts[i], max(1, left * loads[i] // whole), spare)
            counts[i] = counts[i] + more
            spare = spare - more
    return np.array([most] + counts)


def ragged(key, amount, total, most, slope):
    if amount == 2:
        one = jax.random.randint(key, (), max(1, total - most), min(most, total - 1) + 1)
        return jnp.stack([one, total - one])
    tallies = jnp.asarray(length_profile(amount, total, most, slope), jnp.int32)
    pairs = (amount - 1) // 2
    giver, taker = tallies[1:1 + 2 * pairs:2], tallies[2:2 + 2 * pairs:2]
    margin = jnp.minimum(giver - 1, most - taker)
    moved = jax.random.randint(jax.random.fold_in(key, 1), (pairs,), 0, 1 << 20) % (margin + 1)
    tallies = tallies.at[1:1 + 2 * pairs:2].set(giver - moved).at[2:2 + 2 * pairs:2].set(taker + moved)
    return tallies[jax.random.permutation(jax.random.fold_in(key, 2), amount)]


def setup_inputs(seed: int = 0, part: int = 0) -> dict:
    keys = jax.random.split(jax.random.key(seed), 5)
    own_keys = jax.random.split(jax.random.fold_in(keys[4], part), 5)
    qkv = draw_qkv(jax.random.fold_in(jax.random.fold_in(keys[4], part), 71), part)
    timestep = jax.random.randint(own_keys[1], (1,), 0, 1000).astype(jnp.int32)
    windows = draw_windows(jax.random.fold_in(keys[4], 71), part)
    segments = jnp.searchsorted(jnp.cumsum(ragged(own_keys[3], SEGMENTS, FRAMES, FRAMES // 2, 1)), jnp.arange(FRAMES), side="right").astype(jnp.int32)
    return {"qkv": qkv, "timestep": timestep, "windows": windows, "segments": segments}


def reference(qkv, timestep, windows, segments):
    scale = 1.0 / (HD ** 0.5)
    blocks = qkv.reshape(2, FRAMES, P_SIZE, 3, HEADS, HD)
    fill = jnp.full((W_MAX,), -1, jnp.int32)
    seg_pad = jnp.concatenate([fill, segments.astype(jnp.int32), fill])
    offsets = jnp.arange(2 * W_MAX + 1, dtype=jnp.int32) - W_MAX
    within_reach = jnp.abs(offsets)[None, :] <= windows.astype(jnp.int32)[:, None]

    def one_frame(frame_number):
        query = lax.dynamic_index_in_dim(blocks, frame_number, 1, keepdims=False)[:, :, 0]
        picks = jnp.clip(frame_number + offsets, 0, FRAMES - 1).astype(jnp.int32)
        near = jnp.take(blocks, picks, axis=1)
        key_rows = near[:, :, :, 1]
        value_rows = near[:, :, :, 2]
        shots = lax.dynamic_slice_in_dim(seg_pad, frame_number, 2 * W_MAX + 1, 0)
        own_shot = lax.dynamic_index_in_dim(seg_pad, frame_number + W_MAX, 0, keepdims=False)
        allowed = within_reach & (shots == own_shot)[None, :]
        scores = jnp.einsum('bthd,bgrhd->bhtgr', query.astype(jnp.float32), key_rows.astype(jnp.float32)) * scale
        scores = jnp.where(allowed[None, :, None, :, None], scores, -1e30)
        highest = jnp.max(scores, axis=(3, 4), keepdims=True)
        expd = jnp.exp(scores - highest)
        totals = jnp.sum(expd, axis=(3, 4))
        weights = expd.astype(jnp.bfloat16)
        mixed = jnp.einsum('bhtgr,bgrhd->bthd', weights.astype(jnp.float32), value_rows.astype(jnp.float32))
        mixed = mixed / jnp.transpose(totals, (0, 2, 1))[..., None]
        return mixed.astype(jnp.bfloat16)

    attended = lax.map(one_frame, jnp.arange(FRAMES, dtype=jnp.int32))
    strength = 1.0 + 4.0 * timestep[0].astype(jnp.float32) / 999.0
    cond = attended[:, 0].astype(jnp.float32)
    uncond = attended[:, 1].astype(jnp.float32)
    guided = (uncond + strength * (cond - uncond)).astype(jnp.bfloat16)
    guided = guided.reshape(TOKENS, N_SEQ, HEADS // N_SEQ, HD)
    guided = jnp.transpose(guided, (0, 2, 1, 3)).reshape(TOKENS, HEADS // N_SEQ, N_SEQ * HD)
    return guided
```

```python
import functools
import math

import jax
import jax.numpy as jnp
from jax import lax
from jax.experimental import pallas as pl
from jax.experimental.pallas import tpu as pltpu
from jax.sharding import PartitionSpec as P

HD = 128
F_DEV = 2
W_MAX = 2


def padded_2(block, sides, width):
    for axis, dim in sides:
        count = lax.axis_size(axis)
        forward = [(i, i + 1) for i in range(count - 1)]
        backward = [(target, source) for source, target in forward]
        low = lax.ppermute(
            lax.slice_in_dim(block, block.shape[dim] - width, None, axis=dim), axis, forward
        )
        high = lax.ppermute(lax.slice_in_dim(block, 0, width, axis=dim), axis, backward)
        block = jnp.concatenate([low, block, high], axis=dim)
    return block


def attend(block, head_windows, seg_pad, first_frame):
    count_blocks = block.shape[0]
    branches = block.shape[1]
    rows_block = block.shape[2]
    columns = block.shape[4]
    heads_here = columns // HD
    per_frame = count_blocks // F_DEV
    reach = W_MAX * per_frame
    span = 2 * W_MAX + 1
    scale = 1.0 / math.sqrt(HD)
    pairs = block[:, :, :, 1:]
    padded = padded_2(pairs, (("frame", 0),), reach)
    queries = block[:, :, :, 0].reshape(count_blocks, branches, rows_block, heads_here, HD)
    offsets = jnp.arange(span, dtype=jnp.int32) - W_MAX
    within_reach = jnp.abs(offsets)[None, None, :] <= head_windows[:, :, None]
    results = []
    for frame_number in range(F_DEV):
        query = queries[frame_number * per_frame : (frame_number + 1) * per_frame]
        window_rows = padded[frame_number * per_frame : frame_number * per_frame + span * per_frame]
        window_rows = window_rows.reshape(span * per_frame, branches, rows_block, 2, heads_here, HD)
        key_rows = window_rows[:, :, :, 0]
        value_rows = window_rows[:, :, :, 1]
        here = first_frame + frame_number
        shots = lax.dynamic_slice_in_dim(seg_pad, here, span, 0)
        own_shot = lax.dynamic_index_in_dim(seg_pad, here + W_MAX, 0, keepdims=False)
        allowed = within_reach & (shots == own_shot)[None, None, :]
        allowed = jnp.repeat(allowed, per_frame, axis=2)
        scores = (
            jnp.einsum("sbthd,ubrhd->bhstur", query, key_rows, preferred_element_type=jnp.float32)
            * scale
        )
        scores = jnp.where(allowed[:, :, None, None, :, None], scores, -1e30)
        highest = jnp.max(scores, axis=(4, 5), keepdims=True)
        expd = jnp.exp(scores - highest)
        totals = jnp.sum(expd, axis=(4, 5))
        weights = expd.astype(jnp.bfloat16)
        mixed = jnp.einsum(
            "bhstur,ubrhd->sbthd", weights, value_rows, preferred_element_type=jnp.float32
        )
        mixed = mixed / jnp.transpose(totals, (2, 0, 3, 1))[..., None]
        results.append(mixed.astype(jnp.bfloat16))
    return jnp.concatenate(results, axis=0)


def body(qkv, timestep, windows, segments):
    first_frame = lax.axis_index("frame") * F_DEV
    fill = jnp.full((W_MAX,), -1, jnp.int32)
    seg_pad = jnp.concatenate([fill, segments, fill])
    strength = 1.0 + 4.0 * timestep[0].astype(jnp.float32) / 999.0
    seq_count = lax.axis_size("seq")
    cfg_count = lax.axis_size("cfg")
    spread = lax.all_to_all(qkv, ("seq", "cfg"), split_axis=3, concat_axis=0, tiled=True)
    columns = spread.shape[3]
    heads_here = columns // HD
    block = spread.reshape(seq_count, cfg_count, spread.shape[1], 3, columns)
    start_head = (lax.axis_index("seq") * cfg_count + lax.axis_index("cfg")) * heads_here
    head_windows = lax.dynamic_slice_in_dim(windows, start_head, heads_here, 0).reshape(
        1, heads_here
    )
    attended = attend(block, head_windows, seg_pad, first_frame)
    cond = attended[:, 0].astype(jnp.float32)
    uncond = attended[:, 1].astype(jnp.float32)
    guided = (uncond + strength * (cond - uncond)).astype(jnp.bfloat16)
    own_rows = lax.all_to_all(guided, "seq", split_axis=0, concat_axis=3, tiled=True)
    return own_rows[0]

LOG2E = 1.4426950408889634
MASKED = -1e30
BF16 = jnp.bfloat16
F32 = jnp.float32
VMEM_BYTES = 32 * 1024 * 1024


def whole(space=pltpu.VMEM):
    return pl.BlockSpec(memory_space=space)


def pack_kernel(planes, count, heads_ref, x_ref, out_ref, sems):
    copies = []
    for j in range(count):
        start = pl.multiple_of(heads_ref[j] * HD, HD)
        for k, plane in enumerate(planes):
            copies.append(
                pltpu.make_async_copy(
                    x_ref.at[plane, :, pl.ds(start, HD)],
                    out_ref.at[j, k],
                    sems.at[j * len(planes) + k],
                )
            )
    for copy in copies:
        copy.start()
    for copy in copies:
        copy.wait()


def pack(x3, heads, planes):
    count = heads.shape[0]
    rows = x3.shape[1]
    return pl.pallas_call(
        functools.partial(pack_kernel, planes, count),
        out_shape=jax.ShapeDtypeStruct((count, len(planes), rows, HD), x3.dtype),
        grid_spec=pltpu.PrefetchScalarGridSpec(
            num_scalar_prefetch=1,
            grid=(1,),
            in_specs=[whole(pl.ANY)],
            out_specs=whole(pl.ANY),
            scratch_shapes=[pltpu.SemaphoreType.DMA((count * len(planes),))],
        ),
        compiler_params=pltpu.CompilerParams(vmem_limit_bytes=VMEM_BYTES),
        cost_estimate=pl.CostEstimate(
            flops=0, bytes_accessed=4 * count * len(planes) * rows * HD, transcendentals=0
        ),
        name="pack_heads",
    )(heads, x3)


def softmax_mix(q, keys, values, biases):
    factor = LOG2E / math.sqrt(HD)
    scores = []
    for key, bias in zip(keys, biases):
        score = lax.dot_general(
            q, key, (((1,), (1,)), ((), ())), preferred_element_type=F32
        )
        scores.append(score if bias is None else score + bias)
    top = functools.reduce(
        jnp.maximum, [jnp.max(score, axis=1, keepdims=True) for score in scores]
    )
    total = None
    mixed = None
    for score, value in zip(scores, values):
        expd = jnp.exp2((score - top) * factor)
        part = jnp.sum(expd, axis=1, keepdims=True)
        prod = jnp.dot(expd.astype(BF16), value, preferred_element_type=F32)
        total = part if total is None else total + part
        mixed = prod if mixed is None else mixed + prod
    return (mixed / total).astype(BF16)


def attend_kernel(count_src, masked, halves, heads_ref, flags_ref, scal_ref, q_ref, *refs):
    slot = pl.program_id(0)
    if masked:
        kv_refs, out_refs = refs[:count_src], refs[count_src:]
        keys = [ref[0, 0] for ref in kv_refs]
        values = [ref[0, 1] for ref in kv_refs]
        biases = [
            jnp.where(flags_ref[slot * count_src + k] != 0, 0.0, MASKED).astype(F32)
            for k in range(count_src)
        ]
    else:
        keys, values, out_refs = [refs[0][0]], [refs[1][0]], refs[2:]
        biases = [None]
    out = softmax_mix(q_ref[0], keys, values, biases)
    if halves:
        half = out.shape[0] // 2
        low, high = out[:half], out[half:]
        first = scal_ref[0] == 0
        out_refs[0][0] = jnp.where(first, low, high)
        out_refs[1][0] = jnp.where(first, high, low)
    else:
        out_refs[0][0] = out


def attend_slots(q, q_is_x3, sources, flags, heads, scal, halves):
    count = heads.shape[0]
    rows = q.shape[1] if q_is_x3 else q.shape[-2]
    if q_is_x3:
        q_spec = pl.BlockSpec((1, rows, HD), lambda i, h, fl, sc: (0, 0, h[i]))
    else:
        q_spec = pl.BlockSpec((1, rows, HD), lambda i, h, fl, sc: (i, 0, 0))
    args = [q]
    specs = [q_spec]
    masked = sources is not None
    if masked:
        count_src = len(sources)
        for array, first in sources:
            args.append(array)
            specs.append(
                pl.BlockSpec(
                    (1, 2, rows, HD), functools.partial(lambda o, i, h, fl, sc: (i + o, 0, 0, 0), first)
                )
            )
    else:
        count_src = 1
        for plane in (1, 2):
            args.append(q)
            specs.append(
                pl.BlockSpec(
                    (1, rows, HD), functools.partial(lambda p, i, h, fl, sc: (p, 0, h[i]), plane)
                )
            )
    if halves:
        out_shape = [jax.ShapeDtypeStruct((count, rows // 2, HD), BF16)] * 2
        out_specs = [pl.BlockSpec((1, rows // 2, HD), lambda i, h, fl, sc: (i, 0, 0))] * 2
    else:
        out_shape = jax.ShapeDtypeStruct((count, rows, HD), BF16)
        out_specs = pl.BlockSpec((1, rows, HD), lambda i, h, fl, sc: (i, 0, 0))
    return pl.pallas_call(
        functools.partial(attend_kernel, count_src, masked, halves),
        out_shape=out_shape,
        grid_spec=pltpu.PrefetchScalarGridSpec(
            num_scalar_prefetch=3, grid=(count,), in_specs=specs, out_specs=out_specs
        ),
        compiler_params=pltpu.CompilerParams(vmem_limit_bytes=VMEM_BYTES),
        cost_estimate=pl.CostEstimate(
            flops=8 * count * count_src * rows * rows * HD,
            bytes_accessed=2 * count * (count_src * 2 + 2) * rows * HD,
            transcendentals=count * count_src * rows * rows,
        ),
        name="attend",
    )(heads, flags.reshape(-1), scal, *args)


def blend(cond, uncond, strength):
    cond = cond.astype(F32)
    uncond = uncond.astype(F32)
    return (uncond + strength * (cond - uncond)).astype(BF16)


def assemble_kernel(sizes, pos_ref, scal_ref, strength_ref, *refs):
    chunks, local = sizes
    count = len(chunks)
    own, peer = refs[: count + 1], refs[count + 1 : 2 * count + 2]
    kept, moved = refs[2 * count + 2 : 3 * count + 2], refs[3 * count + 2 : 4 * count + 2]
    out_ref = refs[-1]
    branch, column = scal_ref[0], scal_ref[1]
    strength = strength_ref[0]
    exchanged = 2 * sum(chunks)

    def mix(mine_ref, other_ref, index):
        mine, other = mine_ref[index], other_ref[index]
        first = branch == 0
        return blend(jnp.where(first, mine, other), jnp.where(first, other, mine), strength)

    def one(t, carry):
        p = pos_ref[t]
        slot = lax.shift_right_logical(p, 1)
        here = jnp.bitwise_and(p, 1) == column
        is_local = p >= exchanged
        first = 0
        for k, size in enumerate(chunks):
            inside = jnp.logical_and(slot >= first, slot < first + size)
            inside = jnp.logical_and(inside, jnp.logical_not(is_local))
            index = jnp.clip(slot - first, 0, size - 1)

            @pl.when(jnp.logical_and(inside, here))
            def _(k=k, index=index):
                out_ref[t] = mix(own[k], peer[k], index)

            @pl.when(jnp.logical_and(inside, jnp.logical_not(here)))
            def _(k=k, index=index):
                half = kept[k].shape[1]
                low_here = branch == 0
                mine, other = kept[k][index], moved[k][index]
                out_ref[t, :half] = jnp.where(low_here, mine, other)
                out_ref[t, half:] = jnp.where(low_here, other, mine)

            first += size
        if local:
            index = jnp.clip(p - exchanged, 0, local - 1)

            @pl.when(is_local)
            def _():
                out_ref[t] = mix(own[count], peer[count], index)

        return carry

    lax.fori_loop(0, pos_ref.shape[0], one, 0)


def ranked_body(rungs, qkv, timestep, windows, segments):
    rows = qkv.shape[1]
    heads = windows.shape[0]
    seq_count = lax.axis_size("seq")
    frame_count = lax.axis_size("frame")
    cfg_count = lax.axis_size("cfg")
    column = lax.axis_index("seq").astype(jnp.int32)
    block = lax.axis_index("frame").astype(jnp.int32)
    branch = lax.axis_index("cfg").astype(jnp.int32)
    strength = 1.0 + 4.0 * timestep.astype(F32) / 999.0
    x3 = jnp.transpose(qkv[0], (1, 0, 2))

    ids = jnp.arange(heads, dtype=jnp.int32)
    ahead = (windows[None, :] > windows[:, None]) | (
        (windows[None, :] == windows[:, None]) & (ids[None, :] < ids[:, None])
    )
    rank = jnp.sum(ahead.astype(jnp.int32), axis=1)
    order = jnp.sum(jnp.where(rank[None, :] == ids[:, None], ids[None, :], 0), axis=1)
    sorted_windows = jnp.sum(
        jnp.where(rank[None, :] == ids[:, None], windows[None, :], 0), axis=1
    )
    by_column = order.reshape(heads // 2, 2)
    mine = lax.dynamic_index_in_dim(by_column, column, 1, keepdims=False)
    theirs = lax.dynamic_index_in_dim(by_column, 1 - column, 1, keepdims=False)
    my_windows = lax.dynamic_index_in_dim(
        sorted_windows.reshape(heads // 2, 2), column, 1, keepdims=False
    )

    own_frame = 2 * block + column
    sign = 1 - 2 * column
    fill = jnp.full((W_MAX,), -1, jnp.int32)
    seg_pad = jnp.concatenate([fill, segments, fill])
    steps = {"O": 0, "X": 1, "NO": 2, "NR": -1, "FO": -2, "FR": 3}
    shot = {
        name: lax.dynamic_index_in_dim(
            seg_pad, own_frame + step * sign + W_MAX, 0, keepdims=False
        )
        for name, step in steps.items()
    }
    own_names = ("FO", "NR", "O", "X", "NO")
    across_names = ("NR", "O", "X", "NO", "FR")
    distances = (2, 1, 0, 1, 2)

    def flags_of(names, own):
        columns = [
            (my_windows >= distance) & (shot[name] == shot[own])
            for name, distance in zip(names, distances)
        ]
        return jnp.stack(columns, axis=1).astype(jnp.int32)

    flags_own = flags_of(own_names, "O")
    flags_across = flags_of(across_names, "X")
    scal = jnp.stack([branch, column])

    per_half = heads // (seq_count * cfg_count)
    first_out = branch * per_half
    rank_grid = rank.reshape(seq_count, heads // seq_count)
    pos = lax.dynamic_slice_in_dim(rank_grid, first_out, per_half, 1).reshape(-1)

    grid_axes = ("seq", "frame")
    last = frame_count - 1
    apart = [(i, i - 1) for i in range(1, frame_count)] + [
        (frame_count + i, frame_count + i + 1) for i in range(last)
    ]
    onward = [(i, i + 1) for i in range(last)] + [
        (frame_count + i, frame_count + i - 1) for i in range(1, frame_count)
    ]
    swap = [(0, 1), (1, 0)]

    def attempt(rung, x3, strength, mine, theirs, order, flags_own, flags_across, scal, pos):
        exchanged, wide = rung
        slots, far = exchanged // 2, wide // 2
        local = heads - exchanged
        bounds = [(0, far)] if far == slots else [(0, far), (far, slots)]
        bounds = [(lo, hi) for lo, hi in bounds if hi > lo]
        kv_out = [pack(x3, theirs[lo:hi], (1, 2)) for lo, hi in bounds]
        kv_own = [pack(x3, mine[lo:hi], (1, 2)) for lo, hi in bounds]
        q_out = [pack(x3, theirs[lo:hi], (0,)) for lo, hi in bounds]
        kv_across = [lax.ppermute(a, "seq", swap) for a in kv_out]
        near_own = [lax.ppermute(a, grid_axes, apart) for a in kv_own]
        far_own = lax.ppermute(kv_own[0], grid_axes, onward)
        q_across = [lax.ppermute(a, "seq", swap) for a in q_out]
        near_across = [lax.ppermute(a, grid_axes, onward) for a in kv_across]
        far_across = lax.ppermute(kv_across[0], grid_axes, apart)
        own, kept, moved = [], [], []
        for k, (lo, hi) in enumerate(bounds):
            sources = {
                "O": kv_own[k],
                "X": kv_across[k],
                "NO": near_own[k],
                "NR": near_across[k],
                "FO": far_own,
                "FR": far_across,
            }
            cut = slice(0, 5) if k == 0 else slice(1, 4)
            own.append(
                attend_slots(
                    x3,
                    True,
                    [(sources[name], 0) for name in own_names[cut]],
                    flags_own[lo:hi, cut],
                    mine[lo:hi],
                    scal,
                    False,
                )
            )
            keep, send = attend_slots(
                q_across[k].reshape(hi - lo, rows, HD),
                False,
                [(sources[name], 0) for name in across_names[cut]],
                flags_across[lo:hi, cut],
                mine[lo:hi],
                scal,
                True,
            )
            got = lax.ppermute(send, "cfg", swap)
            first = scal[0] == 0
            mixed = blend(jnp.where(first, keep, got), jnp.where(first, got, keep), strength[0])
            kept.append(lax.ppermute(mixed, "seq", swap))
            moved.append(lax.ppermute(kept[-1], "cfg", swap))
        if local:
            own.append(attend_slots(x3, True, None, mine[:1], order[exchanged:], scal, False))
        peer = [lax.ppermute(a, "cfg", swap) for a in own]
        if not local:
            own, peer = own + own[:1], peer + peer[:1]
        arrays = [*own, *peer, *kept, *moved]
        return pl.pallas_call(
            functools.partial(assemble_kernel, ([hi - lo for lo, hi in bounds], local)),
            out_shape=jax.ShapeDtypeStruct((pos.shape[0], rows, HD), BF16),
            in_specs=[whole(pltpu.SMEM)] * 3 + [whole()] * len(arrays),
            out_specs=whole(),
            compiler_params=pltpu.CompilerParams(vmem_limit_bytes=VMEM_BYTES),
            name="assemble",
        )(pos, scal, strength, *arrays)

    many = jnp.sum((windows >= 1).astype(jnp.int32))
    most = jnp.sum((windows >= 2).astype(jnp.int32))
    index = jnp.int32(len(rungs) - 1)
    for k in reversed(range(len(rungs) - 1)):
        fits = (many <= rungs[k][0]) & (most <= rungs[k][1])
        index = jnp.where(fits, jnp.int32(k), index)
    out = lax.switch(
        index,
        [functools.partial(attempt, rung) for rung in rungs],
        x3, strength, mine, theirs, order, flags_own, flags_across, scal, pos,
    )
    out = out.reshape(seq_count, per_half, rows, HD)
    return jnp.transpose(out, (2, 1, 0, 3)).reshape(rows, per_half, seq_count * HD)


def rungs_of(heads):
    third = heads // 3
    return ((2 * third + 2, third), (2 * third + 2, 2 * third + 2), (heads, heads))


def solution(mesh):
    sizes = dict(mesh.shape)

    def whole_body(qkv, timestep, windows, segments):
        tokens_here = qkv.shape[1]
        frames_here = segments.shape[0] // sizes["frame"]
        one_frame = frames_here == sizes["seq"]
        if sizes["seq"] == 2 and sizes["cfg"] == 2 and one_frame and tokens_here % 32 == 0:
            return ranked_body(rungs_of(windows.shape[0]), qkv, timestep, windows, segments)
        return body(qkv, timestep, windows, segments)

    return jax.shard_map(
        whole_body,
        mesh=mesh,
        in_specs=(P("cfg", ("groups", "frame", "seq"), None, None), P("groups"), P(), P("groups")),
        out_specs=P(("groups", "frame", "seq"), "cfg", None),
        check_vma=False,
    )
```

```python
import functools
import math

import jax
import jax.numpy as jnp
from jax import lax
from jax.experimental import pallas as pl
from jax.experimental.pallas import tpu as pltpu
from jax.sharding import PartitionSpec as P

HD = 128
F_DEV = 2
W_MAX = 2


def padded_2(block, sides, width):
    for axis, dim in sides:
        count = lax.axis_size(axis)
        forward = [(i, i + 1) for i in range(count - 1)]
        backward = [(target, source) for source, target in forward]
        low = lax.ppermute(
            lax.slice_in_dim(block, block.shape[dim] - width, None, axis=dim), axis, forward
        )
        high = lax.ppermute(lax.slice_in_dim(block, 0, width, axis=dim), axis, backward)
        block = jnp.concatenate([low, block, high], axis=dim)
    return block


def attend(block, head_windows, seg_pad, first_frame):
    count_blocks = block.shape[0]
    branches = block.shape[1]
    rows_block = block.shape[2]
    columns = block.shape[4]
    heads_here = columns // HD
    per_frame = count_blocks // F_DEV
    reach = W_MAX * per_frame
    span = 2 * W_MAX + 1
    scale = 1.0 / math.sqrt(HD)
    pairs = block[:, :, :, 1:]
    padded = padded_2(pairs, (("frame", 0),), reach)
    queries = block[:, :, :, 0].reshape(count_blocks, branches, rows_block, heads_here, HD)
    offsets = jnp.arange(span, dtype=jnp.int32) - W_MAX
    within_reach = jnp.abs(offsets)[None, None, :] <= head_windows[:, :, None]
    results = []
    for frame_number in range(F_DEV):
        query = queries[frame_number * per_frame : (frame_number + 1) * per_frame]
        window_rows = padded[frame_number * per_frame : frame_number * per_frame + span * per_frame]
        window_rows = window_rows.reshape(span * per_frame, branches, rows_block, 2, heads_here, HD)
        key_rows = window_rows[:, :, :, 0]
        value_rows = window_rows[:, :, :, 1]
        here = first_frame + frame_number
        shots = lax.dynamic_slice_in_dim(seg_pad, here, span, 0)
        own_shot = lax.dynamic_index_in_dim(seg_pad, here + W_MAX, 0, keepdims=False)
        allowed = within_reach & (shots == own_shot)[None, None, :]
        allowed = jnp.repeat(allowed, per_frame, axis=2)
        scores = (
            jnp.einsum("sbthd,ubrhd->bhstur", query, key_rows, preferred_element_type=jnp.float32)
            * scale
        )
        scores = jnp.where(allowed[:, :, None, None, :, None], scores, -1e30)
        highest = jnp.max(scores, axis=(4, 5), keepdims=True)
        expd = jnp.exp(scores - highest)
        totals = jnp.sum(expd, axis=(4, 5))
        weights = expd.astype(jnp.bfloat16)
        mixed = jnp.einsum(
            "bhstur,ubrhd->sbthd", weights, value_rows, preferred_element_type=jnp.float32
        )
        mixed = mixed / jnp.transpose(totals, (2, 0, 3, 1))[..., None]
        results.append(mixed.astype(jnp.bfloat16))
    return jnp.concatenate(results, axis=0)


def body(qkv, timestep, windows, segments):
    first_frame = lax.axis_index("frame") * F_DEV
    fill = jnp.full((W_MAX,), -1, jnp.int32)
    seg_pad = jnp.concatenate([fill, segments, fill])
    strength = 1.0 + 4.0 * timestep[0].astype(jnp.float32) / 999.0
    seq_count = lax.axis_size("seq")
    cfg_count = lax.axis_size("cfg")
    spread = lax.all_to_all(qkv, ("seq", "cfg"), split_axis=3, concat_axis=0, tiled=True)
    columns = spread.shape[3]
    heads_here = columns // HD
    block = spread.reshape(seq_count, cfg_count, spread.shape[1], 3, columns)
    start_head = (lax.axis_index("seq") * cfg_count + lax.axis_index("cfg")) * heads_here
    head_windows = lax.dynamic_slice_in_dim(windows, start_head, heads_here, 0).reshape(
        1, heads_here
    )
    attended = attend(block, head_windows, seg_pad, first_frame)
    cond = attended[:, 0].astype(jnp.float32)
    uncond = attended[:, 1].astype(jnp.float32)
    guided = (uncond + strength * (cond - uncond)).astype(jnp.bfloat16)
    own_rows = lax.all_to_all(guided, "seq", split_axis=0, concat_axis=3, tiled=True)
    return own_rows[0]

LOG2E = 1.4426950408889634
MASKED = -1e30
BF16 = jnp.bfloat16
F32 = jnp.float32
VMEM_BYTES = 32 * 1024 * 1024
SWAP = ((0, 1), (1, 0))
STEPS = {"O": 0, "X": 1, "NO": 2, "NR": -1, "FO": -2, "FR": 3}
OWN_SOURCES = ("FO", "NR", "O", "X", "NO")
ACROSS_SOURCES = ("NR", "O", "X", "NO", "FR")
DISTANCES = (2, 1, 0, 1, 2)


def whole(space=pltpu.VMEM):
    return pl.BlockSpec(memory_space=space)


def params():
    return pltpu.CompilerParams(vmem_limit_bytes=VMEM_BYTES)


class Layout:
    def __init__(self, heads, outs):
        self.mine = 0
        self.theirs = heads // 2
        self.order = heads
        self.rank = 2 * heads
        self.reach = 3 * heads
        self.my_reach = 4 * heads
        self.pos = self.my_reach + heads // 2
        self.own_match = self.pos + outs
        self.across_match = self.own_match + len(DISTANCES)
        self.branch = self.across_match + len(DISTANCES)
        self.column = self.branch + 1
        self.rung = self.column + 1
        self.size = self.rung + 1


def plan_kernel(at, rungs, split, place_ref, windows_ref, segments_ref, plan_ref):
    heads = windows_ref.shape[0]
    frames = segments_ref.shape[0]
    column, block, branch = place_ref[0], place_ref[1], place_ref[2]
    reach = [windows_ref[h] for h in range(heads)]
    wide = [(w >= 2).astype(jnp.int32) for w in reach]
    some = [(w >= 1).astype(jnp.int32) for w in reach]
    most = functools.reduce(lambda a, b: a + b, wide)
    many = functools.reduce(lambda a, b: a + b, some)
    next_wide, next_some, next_none = jnp.int32(0), most, many
    for h in range(heads):
        spot = jnp.where(wide[h] == 1, next_wide, jnp.where(some[h] == 1, next_some, next_none))
        next_wide = next_wide + wide[h]
        next_some = next_some + some[h] - wide[h]
        next_none = next_none + 1 - some[h]
        plan_ref[at.order + spot] = jnp.int32(h)
        plan_ref[at.rank + h] = spot
        plan_ref[at.reach + spot] = reach[h]
    for j in range(heads // 2):
        plan_ref[at.mine + j] = plan_ref[at.order + 2 * j + column]
        plan_ref[at.theirs + j] = plan_ref[at.order + 2 * j + 1 - column]
        plan_ref[at.my_reach + j] = plan_ref[at.reach + 2 * j + column]
    columns, cores = split
    per_half = heads // (columns * cores)
    for t in range(columns * per_half):
        head = (t // per_half) * (heads // columns) + branch * per_half + t % per_half
        plan_ref[at.pos + t] = plan_ref[at.rank + head]
    own_frame = 2 * block + column
    sign = 1 - 2 * column

    def shot(name):
        frame = own_frame + STEPS[name] * sign
        inside = jnp.logical_and(frame >= 0, frame < frames)
        return jnp.where(inside, segments_ref[jnp.clip(frame, 0, frames - 1)], -1)

    for first, names, query in (
        (at.own_match, OWN_SOURCES, "O"),
        (at.across_match, ACROSS_SOURCES, "X"),
    ):
        for k, name in enumerate(names):
            plan_ref[first + k] = (shot(name) == shot(query)).astype(jnp.int32)
    plan_ref[at.branch] = branch
    plan_ref[at.column] = column
    index = jnp.int32(len(rungs) - 1)
    for k in reversed(range(len(rungs) - 1)):
        fits = jnp.logical_and(many <= rungs[k][0], most <= rungs[k][1])
        index = jnp.where(fits, jnp.int32(k), index)
    plan_ref[at.rung] = index


def pack_kernel(jobs, count_in, plan_ref, x_ref, *refs):
    outs, sems = refs[count_in:-1], refs[-1]
    copies = []
    for out_ref, (first, count, planes) in zip(outs, jobs):
        for j in range(count):
            start = pl.multiple_of(plan_ref[first + j] * HD, HD)
            for k, plane in enumerate(planes):
                copies.append(
                    pltpu.make_async_copy(
                        x_ref.at[plane, :, pl.ds(start, HD)],
                        out_ref.at[j, k],
                        sems.at[len(copies)],
                    )
                )
    for copy in copies:
        copy.start()
    for copy in copies:
        copy.wait()


def pack(plan, x3, jobs, after):
    rows = x3.shape[1]
    total = sum(count * len(planes) for _, count, planes in jobs)
    return pl.pallas_call(
        functools.partial(pack_kernel, jobs, len(after)),
        out_shape=[
            jax.ShapeDtypeStruct((count, len(planes), rows, HD), x3.dtype)
            for _, count, planes in jobs
        ],
        grid_spec=pltpu.PrefetchScalarGridSpec(
            num_scalar_prefetch=1,
            grid=(1,),
            in_specs=[whole(pl.ANY)] * (1 + len(after)),
            out_specs=[whole(pl.ANY)] * len(jobs),
            scratch_shapes=[pltpu.SemaphoreType.DMA((total,))],
        ),
        compiler_params=params(),
        cost_estimate=pl.CostEstimate(
            flops=0, bytes_accessed=4 * total * rows * HD, transcendentals=0
        ),
        name="pack_heads",
    )(plan, x3, *after)


def gate_kernel(*refs):
    del refs


def gate(values, after):
    count = len(values)
    return pl.pallas_call(
        gate_kernel,
        out_shape=[jax.ShapeDtypeStruct(v.shape, v.dtype) for v in values],
        in_specs=[whole(pl.ANY)] * (count + len(after)),
        out_specs=[whole(pl.ANY)] * count,
        input_output_aliases={i: i for i in range(count)},
        compiler_params=params(),
        name="gate",
    )(*values, *after)


def softmax_mix(q, keys, values, biases):
    factor = LOG2E / math.sqrt(HD)
    scores = []
    for key, bias in zip(keys, biases):
        score = lax.dot_general(q, key, (((1,), (1,)), ((), ())), preferred_element_type=F32)
        scores.append(score if bias is None else score + bias)
    top = jnp.max(functools.reduce(jnp.maximum, scores), axis=1, keepdims=True)
    expd = [jnp.exp2((score - top) * factor) for score in scores]
    total = jnp.sum(functools.reduce(jnp.add, expd), axis=1, keepdims=True)
    mixed = functools.reduce(
        jnp.add,
        [
            jnp.dot(e.astype(BF16), value, preferred_element_type=F32)
            for e, value in zip(expd, values)
        ],
    )
    return (mixed / total).astype(BF16)


def attend_kernel(spec, plan_ref, q_ref, *refs):
    count, sources, gathered, heads_at, reach_at, match_at, distances, branch_at, halves = spec
    kv_refs = refs[:sources]
    refs = refs[sources:]
    if gathered:
        outs, (held, sems) = refs[:-2], refs[-2:]
        outs = outs[-1:]
        copies = []
        planes = held.shape[1]
        for j in range(count):
            start = pl.multiple_of(plan_ref[heads_at + j] * HD, HD)
            for k in range(planes):
                copies.append(
                    pltpu.make_async_copy(
                        q_ref.at[k, :, pl.ds(start, HD)], held.at[j, k], sems.at[j * planes + k]
                    )
                )
        for copy in copies:
            copy.start()
        for copy in copies:
            copy.wait()
    else:
        outs = refs[-2:] if halves else refs[-1:]
    for j in range(count):
        if gathered:
            q = held[j, 0]
        else:
            q = q_ref[j, 0]
        if sources:
            keys = [ref[j, 0] for ref in kv_refs]
            values = [ref[j, 1] for ref in kv_refs]
            reach = plan_ref[reach_at + j]
            biases = []
            for k, distance in enumerate(distances):
                seen = jnp.logical_and(reach >= distance, plan_ref[match_at + k] != 0)
                biases.append(jnp.where(seen, 0.0, MASKED).astype(F32))
        else:
            keys, values, biases = [held[j, 1]], [held[j, 2]], [None]
        out = softmax_mix(q, keys, values, biases)
        if halves:
            half = out.shape[0] // 2
            low, high = out[:half], out[half:]
            first = plan_ref[branch_at] == 0
            outs[0][j] = jnp.where(first, low, high)
            outs[1][j] = jnp.where(first, high, low)
        else:
            outs[0][j] = out


def attend_slots(plan, at, q, sources, heads_at, first, count, match_at, distances, after):
    rows = q.shape[-2]
    gathered = q.ndim == 3
    spec = (
        count,
        len(sources),
        gathered,
        heads_at,
        at.my_reach + first,
        match_at,
        distances,
        at.branch,
        not gathered,
    )
    kv_specs, kvs = [], []
    for array, offset in sources:
        kvs.append(array)
        if array.shape[0] == count:
            kv_specs.append(whole())
        else:
            kv_specs.append(
                pl.BlockSpec(
                    (pl.Element(count), pl.Element(2), pl.Element(rows), pl.Element(HD)),
                    functools.partial(lambda o, i, plan: (o, 0, 0, 0), offset),
                )
            )
    scratch = []
    if gathered:
        planes = 1 if sources else 3
        scratch = [
            pltpu.VMEM((count, planes, rows, HD), BF16),
            pltpu.SemaphoreType.DMA((count * planes,)),
        ]
        out_shape = jax.ShapeDtypeStruct((count, rows, HD), BF16)
        out_specs = whole()
    else:
        out_shape = [jax.ShapeDtypeStruct((count, rows // 2, HD), BF16)] * 2
        out_specs = [whole()] * 2
    blocks = count * max(1, len(sources))
    return pl.pallas_call(
        functools.partial(attend_kernel, spec),
        out_shape=out_shape,
        grid_spec=pltpu.PrefetchScalarGridSpec(
            num_scalar_prefetch=1,
            grid=(1,),
            in_specs=[whole(pl.ANY) if gathered else whole()]
            + kv_specs
            + [whole(pl.ANY)] * len(after),
            out_specs=out_specs,
            scratch_shapes=scratch,
        ),
        compiler_params=params(),
        cost_estimate=pl.CostEstimate(
            flops=8 * blocks * rows * rows * HD,
            bytes_accessed=4 * (blocks + count) * rows * HD,
            transcendentals=blocks * rows * rows,
        ),
        name="attend",
    )(plan, q, *kvs, *after)


def blend(cond, uncond, strength):
    cond = cond.astype(F32)
    uncond = uncond.astype(F32)
    return (uncond + strength * (cond - uncond)).astype(BF16)


def assemble_kernel(at, chunks, local, plan_ref, strength_ref, *refs):
    count = len(chunks)
    own, peer = refs[: count + 1], refs[count + 1 : 2 * count + 2]
    kept, moved = refs[2 * count + 2 : 3 * count + 2], refs[3 * count + 2 : 4 * count + 2]
    out_ref = refs[-1]
    branch, column = plan_ref[at.branch], plan_ref[at.column]
    strength = strength_ref[0]
    exchanged = 2 * sum(chunks)

    def mix(mine_ref, other_ref, index):
        mine, other = mine_ref[index], other_ref[index]
        first = branch == 0
        return blend(jnp.where(first, mine, other), jnp.where(first, other, mine), strength)

    def one(t, carry):
        p = plan_ref[at.pos + t]
        slot = lax.shift_right_logical(p, 1)
        here = jnp.bitwise_and(p, 1) == column
        is_local = p >= exchanged
        first = 0
        for k, size in enumerate(chunks):
            inside = jnp.logical_and(slot >= first, slot < first + size)
            inside = jnp.logical_and(inside, jnp.logical_not(is_local))
            index = jnp.clip(slot - first, 0, size - 1)

            @pl.when(jnp.logical_and(inside, here))
            def _(k=k, index=index):
                out_ref[t] = mix(own[k], peer[k], index)

            @pl.when(jnp.logical_and(inside, jnp.logical_not(here)))
            def _(k=k, index=index):
                half = kept[k].shape[1]
                low_here = branch == 0
                mine, other = kept[k][index], moved[k][index]
                out_ref[t, :half] = jnp.where(low_here, mine, other)
                out_ref[t, half:] = jnp.where(low_here, other, mine)

            first += size
        if local:
            index = jnp.clip(p - exchanged, 0, local - 1)

            @pl.when(is_local)
            def _():
                out_ref[t] = mix(own[count], peer[count], index)

        return carry

    lax.fori_loop(0, out_ref.shape[0], one, 0)


def ranked_body(rungs, qkv, timestep, windows, segments):
    rows = qkv.shape[1]
    heads = windows.shape[0]
    seq_count = lax.axis_size("seq")
    frame_count = lax.axis_size("frame")
    cfg_count = lax.axis_size("cfg")
    per_half = heads // (seq_count * cfg_count)
    outs = seq_count * per_half
    at = Layout(heads, outs)
    strength = 1.0 + 4.0 * timestep.astype(F32) / 999.0
    x3 = jnp.transpose(qkv[0], (1, 0, 2))
    place = jnp.stack([lax.axis_index(a).astype(jnp.int32) for a in ("seq", "frame", "cfg")])
    plan = pl.pallas_call(
        functools.partial(plan_kernel, at, rungs, (seq_count, cfg_count)),
        out_shape=jax.ShapeDtypeStruct((at.size,), jnp.int32),
        in_specs=[whole(pltpu.SMEM)] * 3,
        out_specs=whole(pltpu.SMEM),
        name="plan",
    )(place, windows, segments)

    grid_axes = ("seq", "frame")
    last = frame_count - 1
    apart = [(i, i - 1) for i in range(1, frame_count)] + [
        (frame_count + i, frame_count + i + 1) for i in range(last)
    ]
    onward = [(i, i + 1) for i in range(last)] + [
        (frame_count + i, frame_count + i - 1) for i in range(1, frame_count)
    ]

    def attempt(rung, plan, x3, strength):
        exchanged, wide = rung
        slots, far = exchanged // 2, wide // 2
        local = heads - exchanged
        bounds = [(lo, hi) for lo, hi in ((0, far), (far, slots)) if hi > lo]
        two = len(bounds) == 2

        def cross(a):
            return lax.ppermute(a, "seq", SWAP)

        def mate(a):
            return lax.ppermute(a, "cfg", SWAP)

        (kv_out0,) = pack(plan, x3, [(at.theirs, far, (1, 2))], [])
        across = [cross(kv_out0)]
        kv_own, kv_far = pack(
            plan, x3, [(at.mine, slots, (1, 2)), (at.mine, far, (1, 2))], [kv_out0]
        )
        near_own = lax.ppermute(kv_own, grid_axes, apart)
        far_own = lax.ppermute(kv_far, grid_axes, onward)
        jobs = [(at.theirs, far, (0,))]
        if two:
            jobs += [(at.theirs + far, slots - far, (0,)), (at.theirs + far, slots - far, (1, 2))]
        q_out = list(pack(plan, x3, jobs, [kv_own]))
        if two:
            across.append(cross(q_out.pop()))
        done = [q_out[0]]
        if local:
            own_local = attend_slots(
                plan, at, x3, [], at.order + exchanged, 0, local, 0, (), done
            )
            peer_local = mate(own_local)
            done = [own_local]
        across[0], q_out[0] = gate([across[0], q_out[0]], [*done, far_own])
        near_across = [lax.ppermute(across[0], grid_axes, onward)]
        far_across = lax.ppermute(across[0], grid_axes, apart)
        q_across = [cross(q_out[0])]
        done = [across[0]]
        if two:
            across[1], q_out[1] = gate([across[1], q_out[1]], [*done, near_own])
            near_across.append(lax.ppermute(across[1], grid_axes, onward))
            q_across.append(cross(q_out[1]))
            done = [across[1]]

        def sources_of(k, names):
            lo = bounds[k][0]
            arrays = {
                "O": (kv_own, lo),
                "X": (across[k], 0),
                "NO": (near_own, lo),
                "NR": (near_across[k], 0),
                "FO": (far_own, 0),
                "FR": (far_across, 0),
            }
            return [arrays[name] for name in names]

        def cut(k):
            return slice(0, 5) if k == 0 else slice(1, 4)

        own, kept, moved = [], [], []

        def attend_own(k, after):
            lo, hi = bounds[k]
            own.append(
                attend_slots(
                    plan, at, x3, sources_of(k, OWN_SOURCES[cut(k)]), at.mine + lo, lo, hi - lo,
                    at.own_match + cut(k).start, DISTANCES[cut(k)], after,
                )
            )
            return [own[-1]]

        def attend_across(k, after):
            lo, hi = bounds[k]
            keep, send = attend_slots(
                plan, at, q_across[k], sources_of(k, ACROSS_SOURCES[cut(k)]), 0, lo, hi - lo,
                at.across_match + cut(k).start, DISTANCES[cut(k)], after,
            )
            got = mate(send)
            first = plan[at.branch] == 0
            mixed = blend(jnp.where(first, keep, got), jnp.where(first, got, keep), strength[0])
            kept.append(cross(mixed))
            moved.append(mate(kept[-1]))
            return [keep]

        done = attend_own(0, done)
        done = attend_across(0, done)
        if two:
            done = attend_across(1, done)
            done = attend_own(1, done)
        peer = [mate(a) for a in own]
        if local:
            own, peer = own + [own_local], peer + [peer_local]
        else:
            own, peer = own + own[:1], peer + peer[:1]
        arrays = [*own, *peer, *kept, *moved]
        return pl.pallas_call(
            functools.partial(assemble_kernel, at, [hi - lo for lo, hi in bounds], local),
            out_shape=jax.ShapeDtypeStruct((outs, rows, HD), BF16),
            in_specs=[whole(pltpu.SMEM)] * 2 + [whole()] * len(arrays),
            out_specs=whole(),
            compiler_params=params(),
            name="assemble",
        )(plan, strength, *arrays)

    out = lax.switch(
        plan[at.rung], [functools.partial(attempt, rung) for rung in rungs], plan, x3, strength
    )
    out = out.reshape(seq_count, per_half, rows, HD)
    return jnp.transpose(out, (2, 1, 0, 3)).reshape(rows, per_half, seq_count * HD)


def rungs_of(heads):
    third = heads // 3
    return ((2 * third + 2, third), (2 * third + 2, 2 * third + 2), (heads, heads))


def solution(mesh):
    sizes = dict(mesh.shape)

    def whole_body(qkv, timestep, windows, segments):
        frames_here = segments.shape[0] // sizes["frame"]
        one_frame = frames_here == sizes["seq"]
        if sizes["seq"] == 2 and sizes["cfg"] == 2 and one_frame and qkv.shape[1] % 32 == 0:
            return ranked_body(rungs_of(windows.shape[0]), qkv, timestep, windows, segments)
        return body(qkv, timestep, windows, segments)

    return jax.shard_map(
        whole_body,
        mesh=mesh,
        in_specs=(P("cfg", ("groups", "frame", "seq"), None, None), P("groups"), P(), P("groups")),
        out_specs=P(("groups", "frame", "seq"), "cfg", None),
        check_vma=False,
    )
```

```python
import functools
import math

import jax
import jax.numpy as jnp
from jax import lax
from jax.experimental import pallas as pl
from jax.experimental.pallas import tpu as pltpu
from jax.sharding import PartitionSpec as P

HD = 128
F_DEV = 2
W_MAX = 2


def padded_2(block, sides, width):
    for axis, dim in sides:
        count = lax.axis_size(axis)
        forward = [(i, i + 1) for i in range(count - 1)]
        backward = [(target, source) for source, target in forward]
        low = lax.ppermute(
            lax.slice_in_dim(block, block.shape[dim] - width, None, axis=dim), axis, forward
        )
        high = lax.ppermute(lax.slice_in_dim(block, 0, width, axis=dim), axis, backward)
        block = jnp.concatenate([low, block, high], axis=dim)
    return block


def attend(block, head_windows, seg_pad, first_frame):
    count_blocks = block.shape[0]
    branches = block.shape[1]
    rows_block = block.shape[2]
    columns = block.shape[4]
    heads_here = columns // HD
    per_frame = count_blocks // F_DEV
    reach = W_MAX * per_frame
    span = 2 * W_MAX + 1
    scale = 1.0 / math.sqrt(HD)
    pairs = block[:, :, :, 1:]
    padded = padded_2(pairs, (("frame", 0),), reach)
    queries = block[:, :, :, 0].reshape(count_blocks, branches, rows_block, heads_here, HD)
    offsets = jnp.arange(span, dtype=jnp.int32) - W_MAX
    within_reach = jnp.abs(offsets)[None, None, :] <= head_windows[:, :, None]
    results = []
    for frame_number in range(F_DEV):
        query = queries[frame_number * per_frame : (frame_number + 1) * per_frame]
        window_rows = padded[frame_number * per_frame : frame_number * per_frame + span * per_frame]
        window_rows = window_rows.reshape(span * per_frame, branches, rows_block, 2, heads_here, HD)
        key_rows = window_rows[:, :, :, 0]
        value_rows = window_rows[:, :, :, 1]
        here = first_frame + frame_number
        shots = lax.dynamic_slice_in_dim(seg_pad, here, span, 0)
        own_shot = lax.dynamic_index_in_dim(seg_pad, here + W_MAX, 0, keepdims=False)
        allowed = within_reach & (shots == own_shot)[None, None, :]
        allowed = jnp.repeat(allowed, per_frame, axis=2)
        scores = (
            jnp.einsum("sbthd,ubrhd->bhstur", query, key_rows, preferred_element_type=jnp.float32)
            * scale
        )
        scores = jnp.where(allowed[:, :, None, None, :, None], scores, -1e30)
        highest = jnp.max(scores, axis=(4, 5), keepdims=True)
        expd = jnp.exp(scores - highest)
        totals = jnp.sum(expd, axis=(4, 5))
        weights = expd.astype(jnp.bfloat16)
        mixed = jnp.einsum(
            "bhstur,ubrhd->sbthd", weights, value_rows, preferred_element_type=jnp.float32
        )
        mixed = mixed / jnp.transpose(totals, (2, 0, 3, 1))[..., None]
        results.append(mixed.astype(jnp.bfloat16))
    return jnp.concatenate(results, axis=0)


def body(qkv, timestep, windows, segments):
    first_frame = lax.axis_index("frame") * F_DEV
    fill = jnp.full((W_MAX,), -1, jnp.int32)
    seg_pad = jnp.concatenate([fill, segments, fill])
    strength = 1.0 + 4.0 * timestep[0].astype(jnp.float32) / 999.0
    seq_count = lax.axis_size("seq")
    cfg_count = lax.axis_size("cfg")
    spread = lax.all_to_all(qkv, ("seq", "cfg"), split_axis=3, concat_axis=0, tiled=True)
    columns = spread.shape[3]
    heads_here = columns // HD
    block = spread.reshape(seq_count, cfg_count, spread.shape[1], 3, columns)
    start_head = (lax.axis_index("seq") * cfg_count + lax.axis_index("cfg")) * heads_here
    head_windows = lax.dynamic_slice_in_dim(windows, start_head, heads_here, 0).reshape(
        1, heads_here
    )
    attended = attend(block, head_windows, seg_pad, first_frame)
    cond = attended[:, 0].astype(jnp.float32)
    uncond = attended[:, 1].astype(jnp.float32)
    guided = (uncond + strength * (cond - uncond)).astype(jnp.bfloat16)
    own_rows = lax.all_to_all(guided, "seq", split_axis=0, concat_axis=3, tiled=True)
    return own_rows[0]

LOG2E = 1.4426950408889634
MASKED = -1e30
BF16 = jnp.bfloat16
F32 = jnp.float32
VMEM_BYTES = 32 * 1024 * 1024
PLAN_VMEM_BYTES = 60 * 1024 * 1024
SWAP = ((0, 1), (1, 0))
COSTS = {"pack": 1e10, "attend": 1e9, "mix": 1e8, "gate": 1e9}
STEPS = {"O": 0, "X": 1, "NO": 2, "NR": -1, "FO": -2, "FR": 3}
OWN_SOURCES = ("FO", "NR", "O", "X", "NO")
ACROSS_SOURCES = ("NR", "O", "X", "NO", "FR")
DISTANCES = (2, 1, 0, 1, 2)


def whole(space=pltpu.VMEM):
    return pl.BlockSpec(memory_space=space)


def cost(kind):
    return pl.CostEstimate(flops=int(COSTS[kind]), bytes_accessed=1, transcendentals=0)


def params(limit=VMEM_BYTES):
    return pltpu.CompilerParams(vmem_limit_bytes=limit)


class Layout:
    def __init__(self, heads, outs):
        self.mine = 0
        self.theirs = heads // 2
        self.order = heads
        self.rank = 2 * heads
        self.reach = 3 * heads
        self.my_reach = 4 * heads
        self.pos = self.my_reach + heads // 2
        self.own_match = self.pos + outs
        self.across_match = self.own_match + len(DISTANCES)
        self.branch = self.across_match + len(DISTANCES)
        self.column = self.branch + 1
        self.step = self.column + 1
        self.size = self.step + 1


def plan_kernel(
    at, rungs, split, windows_in, segments_in, step_in, x_ref, plan_ref, rung_ref, kv_ref, own_ref,
    windows_ref, segments_ref, step_ref, in_sems, sems,
):
    get_windows = pltpu.make_async_copy(windows_in, windows_ref, in_sems.at[0])
    get_segments = pltpu.make_async_copy(segments_in, segments_ref, in_sems.at[1])
    get_windows.start()
    get_segments.start()
    get_step = pltpu.make_async_copy(step_in, step_ref, in_sems.at[2])
    get_step.start()
    heads = windows_ref.shape[0]
    frames = segments_ref.shape[0]
    column, block, branch = (lax.axis_index(a).astype(jnp.int32) for a in ("seq", "frame", "cfg"))
    get_windows.wait()
    reach = [windows_ref[h] for h in range(heads)]
    wide = [(w >= 2).astype(jnp.int32) for w in reach]
    some = [(w >= 1).astype(jnp.int32) for w in reach]
    most = functools.reduce(lambda a, b: a + b, wide)
    many = functools.reduce(lambda a, b: a + b, some)
    next_wide, next_some, next_none = jnp.int32(0), most, many
    for h in range(heads):
        spot = jnp.where(wide[h] == 1, next_wide, jnp.where(some[h] == 1, next_some, next_none))
        next_wide = next_wide + wide[h]
        next_some = next_some + some[h] - wide[h]
        next_none = next_none + 1 - some[h]
        plan_ref[at.order + spot] = jnp.int32(h)
        plan_ref[at.rank + h] = spot
        plan_ref[at.reach + spot] = reach[h]
    copies = []
    for out_ref, side in ((kv_ref, 1 - column), (own_ref, column)):
        for j in range(out_ref.shape[0]):
            start = pl.multiple_of(plan_ref[at.order + 2 * j + side] * HD, HD)
            for k in range(2):
                copies.append(
                    pltpu.make_async_copy(
                        x_ref.at[k + 1, :, pl.ds(start, HD)], out_ref.at[j, k], sems.at[len(copies)]
                    )
                )
                copies[-1].start()
    for j in range(heads // 2):
        plan_ref[at.mine + j] = plan_ref[at.order + 2 * j + column]
        plan_ref[at.theirs + j] = plan_ref[at.order + 2 * j + 1 - column]
        plan_ref[at.my_reach + j] = plan_ref[at.reach + 2 * j + column]
    columns, cores = split
    per_half = heads // (columns * cores)
    for t in range(columns * per_half):
        head = (t // per_half) * (heads // columns) + branch * per_half + t % per_half
        plan_ref[at.pos + t] = plan_ref[at.rank + head]
    own_frame = 2 * block + column
    sign = 1 - 2 * column

    get_segments.wait()
    get_step.wait()
    plan_ref[at.step] = step_ref[0]

    def shot(name):
        frame = own_frame + STEPS[name] * sign
        inside = jnp.logical_and(frame >= 0, frame < frames)
        return jnp.where(inside, segments_ref[jnp.clip(frame, 0, frames - 1)], -1)

    for first, names, query in (
        (at.own_match, OWN_SOURCES, "O"),
        (at.across_match, ACROSS_SOURCES, "X"),
    ):
        for k, name in enumerate(names):
            plan_ref[first + k] = (shot(name) == shot(query)).astype(jnp.int32)
    plan_ref[at.branch] = branch
    plan_ref[at.column] = column
    index = jnp.int32(len(rungs) - 1)
    for k in reversed(range(len(rungs) - 1)):
        fits = jnp.logical_and(many <= rungs[k][0], most <= rungs[k][1])
        index = jnp.where(fits, jnp.int32(k), index)
    rung_ref[0] = index
    for copy in copies:
        copy.wait()


def pack_kernel(jobs, count_in, plan_ref, x_ref, *refs):
    outs, sems = refs[count_in:-1], refs[-1]
    copies = []
    for out_ref, (first, count, planes) in zip(outs, jobs):
        for j in range(count):
            start = pl.multiple_of(plan_ref[first + j] * HD, HD)
            for k, plane in enumerate(planes):
                copies.append(
                    pltpu.make_async_copy(
                        x_ref.at[plane, :, pl.ds(start, HD)],
                        out_ref.at[j, k],
                        sems.at[len(copies)],
                    )
                )
    for copy in copies:
        copy.start()
    for copy in copies:
        copy.wait()


def pack(plan, x3, jobs, after):
    rows = x3.shape[1]
    total = sum(count * len(planes) for _, count, planes in jobs)
    return pl.pallas_call(
        functools.partial(pack_kernel, jobs, len(after)),
        out_shape=[
            jax.ShapeDtypeStruct((count, len(planes), rows, HD), x3.dtype)
            for _, count, planes in jobs
        ],
        grid_spec=pltpu.PrefetchScalarGridSpec(
            num_scalar_prefetch=1,
            grid=(1,),
            in_specs=[whole(pl.ANY)] * (1 + len(after)),
            out_specs=[whole(pl.ANY)] * len(jobs),
            scratch_shapes=[pltpu.SemaphoreType.DMA((total,))],
        ),
        compiler_params=params(),
        cost_estimate=cost("pack"),
        name="pack_heads",
    )(plan, x3, *after)


def gate_kernel(*refs):
    del refs


def gate(values, after):
    count = len(values)
    return pl.pallas_call(
        gate_kernel,
        out_shape=[jax.ShapeDtypeStruct(v.shape, v.dtype) for v in values],
        in_specs=[whole(pl.ANY)] * (count + len(after)),
        out_specs=[whole(pl.ANY)] * count,
        input_output_aliases={i: i for i in range(count)},
        compiler_params=params(),
        cost_estimate=cost("gate"),
        name="gate",
    )(*values, *after)


def softmax_mix(q, keys, values, biases):
    factor = LOG2E / math.sqrt(HD)
    scores = []
    for key, bias in zip(keys, biases):
        score = lax.dot_general(q, key, (((1,), (1,)), ((), ())), preferred_element_type=F32)
        scores.append(score if bias is None else score + bias)
    top = jnp.max(functools.reduce(jnp.maximum, scores), axis=1, keepdims=True)
    expd = [jnp.exp2((score - top) * factor) for score in scores]
    total = jnp.sum(functools.reduce(jnp.add, expd), axis=1, keepdims=True)
    mixed = functools.reduce(
        jnp.add,
        [
            jnp.dot(e.astype(BF16), value, preferred_element_type=F32)
            for e, value in zip(expd, values)
        ],
    )
    return (mixed / total).astype(BF16)


def attend_kernel(spec, plan_ref, q_ref, *refs):
    count, sources, gathered, heads_at, reach_at, match_at, distances, branch_at, halves = spec
    kv_refs = refs[:sources]
    refs = refs[sources:]
    if gathered:
        outs, (held, sems) = refs[:-2], refs[-2:]
        outs = outs[-1:]
        copies = []
        planes = held.shape[1]
        for j in range(count):
            start = pl.multiple_of(plan_ref[heads_at + j] * HD, HD)
            for k in range(planes):
                copies.append(
                    pltpu.make_async_copy(
                        q_ref.at[k, :, pl.ds(start, HD)], held.at[j, k], sems.at[j * planes + k]
                    )
                )
        for copy in copies:
            copy.start()
        for copy in copies:
            copy.wait()
    else:
        outs = refs[-2:] if halves else refs[-1:]
    for j in range(count):
        if gathered:
            q = held[j, 0]
        else:
            q = q_ref[j, 0]
        if sources:
            keys = [ref[j, 0] for ref in kv_refs]
            values = [ref[j, 1] for ref in kv_refs]
            reach = plan_ref[reach_at + j]
            biases = []
            for k, distance in enumerate(distances):
                seen = jnp.logical_and(reach >= distance, plan_ref[match_at + k] != 0)
                biases.append(jnp.where(seen, 0.0, MASKED).astype(F32))
        else:
            keys, values, biases = [held[j, 1]], [held[j, 2]], [None]
        out = softmax_mix(q, keys, values, biases)
        if halves:
            half = out.shape[0] // 2
            low, high = out[:half], out[half:]
            first = plan_ref[branch_at] == 0
            outs[0][j] = jnp.where(first, low, high)
            outs[1][j] = jnp.where(first, high, low)
        else:
            outs[0][j] = out


def slot_spec(array, first, count):
    if array.shape[0] == count:
        return whole()
    block = (count, *array.shape[1:])
    return pl.BlockSpec(
        tuple(pl.Element(size) for size in block), lambda i, plan: (first, 0, 0, 0)
    )


def attend_slots(plan, at, q, sources, heads_at, first, count, match_at, distances, after):
    rows = q.shape[-2]
    gathered = q.ndim == 3
    spec = (
        count,
        len(sources),
        gathered,
        heads_at,
        at.my_reach + first,
        match_at,
        distances,
        at.branch,
        not gathered,
    )
    kv_specs, kvs = [], []
    for array, offset in sources:
        kvs.append(array)
        kv_specs.append(slot_spec(array, offset, count))
    scratch = []
    if gathered:
        planes = 1 if sources else 3
        scratch = [
            pltpu.VMEM((count, planes, rows, HD), BF16),
            pltpu.SemaphoreType.DMA((count * planes,)),
        ]
        out_shape = jax.ShapeDtypeStruct((count, rows, HD), BF16)
        out_specs = whole()
    else:
        out_shape = [jax.ShapeDtypeStruct((count, rows // 2, HD), BF16)] * 2
        out_specs = [whole()] * 2
    return pl.pallas_call(
        functools.partial(attend_kernel, spec),
        out_shape=out_shape,
        grid_spec=pltpu.PrefetchScalarGridSpec(
            num_scalar_prefetch=1,
            grid=(1,),
            in_specs=[whole(pl.ANY) if gathered else slot_spec(q, first, count)]
            + kv_specs
            + [whole(pl.ANY)] * len(after),
            out_specs=out_specs,
            scratch_shapes=scratch,
        ),
        compiler_params=params(),
        cost_estimate=cost("attend"),
        name="attend",
    )(plan, q, *kvs, *after)


def blend(cond, uncond, strength):
    cond = cond.astype(F32)
    uncond = uncond.astype(F32)
    return (uncond + strength * (cond - uncond)).astype(BF16)


def strength_of(at, plan_ref):
    step = jnp.full((1, HD), plan_ref[at.step], jnp.int32).astype(F32)
    return 1.0 + 4.0 * step / 999.0


def mix_kernel(at, plan_ref, mine_ref, other_ref, *refs):
    out_ref = refs[-1]
    strength = strength_of(at, plan_ref)
    first = plan_ref[at.branch] == 0
    for j in range(out_ref.shape[0]):
        mine, other = mine_ref[j], other_ref[j]
        out_ref[j] = blend(
            jnp.where(first, mine, other), jnp.where(first, other, mine), strength
        )


def mix_cores(plan, at, mine, other, after):
    return pl.pallas_call(
        functools.partial(mix_kernel, at),
        out_shape=jax.ShapeDtypeStruct(mine.shape, mine.dtype),
        in_specs=[whole(pltpu.SMEM)] + [whole()] * 2 + [whole(pl.ANY)] * len(after),
        out_specs=whole(),
        compiler_params=params(),
        cost_estimate=cost("mix"),
        name="mix",
    )(plan, mine, other, *after)


def assemble_kernel(at, own_places, raw_places, places, local, plan_ref, *refs):
    count, own_count, raw_count = len(places), len(own_places), len(raw_places)
    own, refs = refs[:own_count], refs[own_count:]
    mine_refs, refs = refs[:raw_count], refs[raw_count:]
    other_refs, refs = refs[:raw_count], refs[raw_count:]
    strength = strength_of(at, plan_ref)
    kept, moved = refs[:count], refs[count : 2 * count]
    local_ref = refs[2 * count] if local else None
    out_ref, held, turned, sems = refs[-4:]
    branch, column = plan_ref[at.branch], plan_ref[at.column]
    exchanged = 2 * sum(size for _, size in places)

    def one(t, carry):
        p = plan_ref[at.pos + t]
        slot = lax.shift_right_logical(p, 1)
        here = jnp.bitwise_and(p, 1) == column
        is_local = p >= exchanged

        def place(first, size):
            inside = jnp.logical_and(slot >= first, slot < first + size)
            inside = jnp.logical_and(inside, jnp.logical_not(is_local))
            return inside, jnp.clip(slot - first, 0, size - 1)

        for k, (first, size) in enumerate(own_places):
            inside, index = place(first, size)

            @pl.when(jnp.logical_and(inside, here))
            def _(k=k, index=index):
                held[t] = own[k][index]

        for k, (first, size) in enumerate(raw_places):
            inside, index = place(first, size)

            @pl.when(jnp.logical_and(inside, here))
            def _(k=k, index=index):
                mine, other = mine_refs[k][index], other_refs[k][index]
                is_cond = branch == 0
                held[t] = blend(
                    jnp.where(is_cond, mine, other), jnp.where(is_cond, other, mine), strength
                )

        for k, (first, size) in enumerate(places):
            inside, index = place(first, size)

            @pl.when(jnp.logical_and(inside, jnp.logical_not(here)))
            def _(k=k, index=index):
                half = kept[k].shape[1]
                low_here = branch == 0
                mine, other = kept[k][index], moved[k][index]
                held[t, :half] = jnp.where(low_here, mine, other)
                held[t, half:] = jnp.where(low_here, other, mine)

        if local:
            index = jnp.clip(p - exchanged, 0, local - 1)

            @pl.when(is_local)
            def _():
                held[t] = local_ref[index]

        return carry

    lax.fori_loop(0, held.shape[0], one, 0)
    per_half = turned.shape[1]
    half = turned.shape[0] // 2
    copies = []
    for r in range(2):
        tokens = slice(r * half, (r + 1) * half)
        for s in range(held.shape[0] // per_half):
            part = held[s * per_half : (s + 1) * per_half, tokens]
            turned[tokens, :, s * HD : (s + 1) * HD] = jnp.swapaxes(part, 0, 1)
        copies.append(
            pltpu.make_async_copy(turned.at[tokens], out_ref.at[tokens], sems.at[r])
        )
        copies[-1].start()
    for copy in copies:
        copy.wait()


def ranked_body(rungs, qkv, timestep, windows, segments):
    rows = qkv.shape[1]
    heads = windows.shape[0]
    seq_count = lax.axis_size("seq")
    frame_count = lax.axis_size("frame")
    cfg_count = lax.axis_size("cfg")
    per_half = heads // (seq_count * cfg_count)
    outs = seq_count * per_half
    at = Layout(heads, outs)
    x3 = jnp.transpose(qkv[0], (1, 0, 2))
    lead, base = rungs[0][1] // 2, rungs[0][0] // 2
    plan, rung, kv_lead, kv_base = pl.pallas_call(
        functools.partial(plan_kernel, at, rungs, (seq_count, cfg_count)),
        out_shape=[
            jax.ShapeDtypeStruct((at.size,), jnp.int32),
            jax.ShapeDtypeStruct((1,), jnp.int32),
            jax.ShapeDtypeStruct((lead, 2, rows, HD), BF16),
            jax.ShapeDtypeStruct((base, 2, rows, HD), BF16),
        ],
        in_specs=[whole(pltpu.HBM)] * 3 + [whole(pl.ANY)],
        out_specs=[whole(pltpu.SMEM)] * 2 + [whole(pl.ANY)] * 2,
        scratch_shapes=[
            pltpu.SMEM(windows.shape, jnp.int32),
            pltpu.SMEM(segments.shape, jnp.int32),
            pltpu.SMEM(timestep.shape, jnp.int32),
            pltpu.SemaphoreType.DMA((3,)),
            pltpu.SemaphoreType.DMA((2 * (lead + base),)),
        ],
        compiler_params=params(PLAN_VMEM_BYTES),
        name="plan",
    )(windows, segments, timestep, x3)

    grid_axes = ("seq", "frame")
    last = frame_count - 1
    apart = [(i, i - 1) for i in range(1, frame_count)] + [
        (frame_count + i, frame_count + i + 1) for i in range(last)
    ]
    onward = [(i, i + 1) for i in range(last)] + [
        (frame_count + i, frame_count + i - 1) for i in range(1, frame_count)
    ]

    def attempt(rung, plan, x3, kv_lead, kv_base):
        exchanged, wide = rung
        slots, far = exchanged // 2, wide // 2
        local = heads - exchanged
        bounds = [(0, lead), (lead, base)]
        if slots > base:
            bounds.append((base, slots))
        chunks = range(len(bounds))
        reaches = [far >= hi for _, hi in bounds]

        def cross(a):
            return lax.ppermute(a, "seq", SWAP)

        def mate(a):
            return lax.ppermute(a, "cfg", SWAP)

        def mix(mine, other, after):
            return mix_cores(plan, at, mine, other, after)

        across = [cross(kv_lead)]
        near_base = lax.ppermute(kv_base, grid_axes, apart)
        jobs = [(at.mine, far, (1, 2)), (at.theirs, slots, (0,))]
        jobs += [(at.theirs + lo, hi - lo, (1, 2)) for lo, hi in bounds[1:]]
        jobs += [(at.mine + lo, hi - lo, (1, 2)) for lo, hi in bounds[2:]]
        kv_far, queries, *rest = pack(plan, x3, jobs, [kv_base])
        far_own = lax.ppermute(kv_far, grid_axes, onward)
        across += [cross(a) for a in rest[: len(bounds) - 1]]
        kv_more = rest[len(bounds) - 1 :]
        near_more = [lax.ppermute(a, grid_axes, apart) for a in kv_more]
        done = [rest[0]]
        if local:
            own_local = attend_slots(
                plan, at, x3, [], at.order + exchanged, 0, local, 0, (), done
            )
            peer_local = mate(own_local)
            done = [own_local]

        near_across, far_across, guided = [], [], []
        (across[0],) = gate([across[0]], done)
        near_across.append(lax.ppermute(across[0], grid_axes, onward))
        (queries,) = gate([queries], [across[0], far_own])
        q_across = cross(queries)
        done = [queries]
        if local:
            guided = [mix(own_local, peer_local, done)]
            done = guided
        for k in chunks[1:]:
            (across[k],) = gate([across[k]], done)
            done = [across[k]]
        (late,) = gate([across[0]], [across[1]])
        far_across.append(lax.ppermute(late, grid_axes, apart))
        for k in chunks[1:]:
            near_across.append(lax.ppermute(across[k], grid_axes, onward))
            far_across.append(
                lax.ppermute(across[k], grid_axes, apart) if reaches[k] else None
            )

        def attend_chunk(k, q, names, heads_at, match_at, after):
            lo, hi = bounds[k]
            arrays = {
                "O": (kv_more[0], 0) if lo == base else (kv_base, lo),
                "X": (across[k], 0),
                "NO": (near_more[0], 0) if lo == base else (near_base, lo),
                "NR": (near_across[k], 0),
                "FO": (far_own, lo),
                "FR": (far_across[k], 0),
            }
            cut = slice(0, 5) if reaches[k] else slice(1, 4)
            sources = [arrays[name] for name in names[cut]]
            return attend_slots(
                plan, at, q, sources, heads_at + lo, lo, hi - lo,
                match_at + cut.start, DISTANCES[cut], after,
            )

        def attend_own(k, after):
            return attend_chunk(k, x3, OWN_SOURCES, at.mine, at.own_match, after)

        def attend_across(k, after):
            return attend_chunk(k, q_across, ACROSS_SOURCES, 0, at.across_match, after)

        own, kept = {}, {}
        own[0] = attend_own(0, done)
        keep, send = attend_across(1, [own[0]])
        got = mate(send)
        end = mix(own[0], mate(own[0]), [keep])
        mixed = mix(keep, got, [end])
        for last_k, k in zip((1, *chunks[2:]), (*chunks[2:], 0)):
            kept[last_k] = cross(mixed)
            keep, send = attend_across(k, [mixed])
            mixed = mix(keep, mate(send), [])
        kept[0] = cross(mixed)
        raw = []
        for k in chunks[1:]:
            lo, hi = bounds[k]
            own[k] = attend_own(k, [mixed, kept[1]])
            middle = (hi - lo) // 2
            raw += [(lo, own[k][:middle]), (lo + middle, own[k][middle:])]
        others = [mate(a) for _, a in raw]
        own_places = ((0, lead),)
        raw_places = tuple((lo, a.shape[0]) for lo, a in raw)
        arrays = [end, *[a for _, a in raw], *others]
        arrays += [kept[k] for k in chunks] + [mate(kept[k]) for k in chunks] + guided
        places = tuple((lo, hi - lo) for lo, hi in bounds)
        return pl.pallas_call(
            functools.partial(assemble_kernel, at, own_places, raw_places, places, local),
            out_shape=jax.ShapeDtypeStruct((rows, per_half, seq_count * HD), BF16),
            in_specs=[whole(pltpu.SMEM)] + [whole()] * len(arrays),
            out_specs=whole(pltpu.HBM),
            scratch_shapes=[
                pltpu.VMEM((outs, rows, HD), BF16),
                pltpu.VMEM((rows, per_half, seq_count * HD), BF16),
                pltpu.SemaphoreType.DMA((2,)),
            ],
            compiler_params=params(),
            name="assemble",
        )(plan, *arrays)

    return lax.switch(
        rung[0],
        [functools.partial(attempt, rung) for rung in rungs],
        plan, x3, kv_lead, kv_base,
    )


def rungs_of(heads):
    third = heads // 3
    return ((2 * third + 2, third), (2 * third + 2, 2 * third + 2), (heads, heads))


def solution(mesh):
    sizes = dict(mesh.shape)

    def whole_body(qkv, timestep, windows, segments):
        frames_here = segments.shape[0] // sizes["frame"]
        one_frame = frames_here == sizes["seq"]
        if sizes["seq"] == 2 and sizes["cfg"] == 2 and one_frame and qkv.shape[1] % 32 == 0:
            return ranked_body(rungs_of(windows.shape[0]), qkv, timestep, windows, segments)
        return body(qkv, timestep, windows, segments)

    return jax.shard_map(
        whole_body,
        mesh=mesh,
        in_specs=(P("cfg", ("groups", "frame", "seq"), None, None), P("groups"), P(), P("groups")),
        out_specs=P(("groups", "frame", "seq"), "cfg", None),
        check_vma=False,
    )
```

```python
import functools
import math

import jax
import jax.numpy as jnp
from jax import lax
from jax.experimental import pallas as pl
from jax.experimental.pallas import tpu as pltpu
from jax.sharding import PartitionSpec as P

HD = 128
F_DEV = 2
W_MAX = 2


def padded_2(block, sides, width):
    for axis, dim in sides:
        count = lax.axis_size(axis)
        forward = [(i, i + 1) for i in range(count - 1)]
        backward = [(target, source) for source, target in forward]
        low = lax.ppermute(
            lax.slice_in_dim(block, block.shape[dim] - width, None, axis=dim), axis, forward
        )
        high = lax.ppermute(lax.slice_in_dim(block, 0, width, axis=dim), axis, backward)
        block = jnp.concatenate([low, block, high], axis=dim)
    return block


def attend(block, head_windows, seg_pad, first_frame):
    count_blocks = block.shape[0]
    branches = block.shape[1]
    rows_block = block.shape[2]
    columns = block.shape[4]
    heads_here = columns // HD
    per_frame = count_blocks // F_DEV
    reach = W_MAX * per_frame
    span = 2 * W_MAX + 1
    scale = 1.0 / math.sqrt(HD)
    pairs = block[:, :, :, 1:]
    padded = padded_2(pairs, (("frame", 0),), reach)
    queries = block[:, :, :, 0].reshape(count_blocks, branches, rows_block, heads_here, HD)
    offsets = jnp.arange(span, dtype=jnp.int32) - W_MAX
    within_reach = jnp.abs(offsets)[None, None, :] <= head_windows[:, :, None]
    results = []
    for frame_number in range(F_DEV):
        query = queries[frame_number * per_frame : (frame_number + 1) * per_frame]
        window_rows = padded[frame_number * per_frame : frame_number * per_frame + span * per_frame]
        window_rows = window_rows.reshape(span * per_frame, branches, rows_block, 2, heads_here, HD)
        key_rows = window_rows[:, :, :, 0]
        value_rows = window_rows[:, :, :, 1]
        here = first_frame + frame_number
        shots = lax.dynamic_slice_in_dim(seg_pad, here, span, 0)
        own_shot = lax.dynamic_index_in_dim(seg_pad, here + W_MAX, 0, keepdims=False)
        allowed = within_reach & (shots == own_shot)[None, None, :]
        allowed = jnp.repeat(allowed, per_frame, axis=2)
        scores = (
            jnp.einsum("sbthd,ubrhd->bhstur", query, key_rows, preferred_element_type=jnp.float32)
            * scale
        )
        scores = jnp.where(allowed[:, :, None, None, :, None], scores, -1e30)
        highest = jnp.max(scores, axis=(4, 5), keepdims=True)
        expd = jnp.exp(scores - highest)
        totals = jnp.sum(expd, axis=(4, 5))
        weights = expd.astype(jnp.bfloat16)
        mixed = jnp.einsum(
            "bhstur,ubrhd->sbthd", weights, value_rows, preferred_element_type=jnp.float32
        )
        mixed = mixed / jnp.transpose(totals, (2, 0, 3, 1))[..., None]
        results.append(mixed.astype(jnp.bfloat16))
    return jnp.concatenate(results, axis=0)


def body(qkv, timestep, windows, segments):
    first_frame = lax.axis_index("frame") * F_DEV
    fill = jnp.full((W_MAX,), -1, jnp.int32)
    seg_pad = jnp.concatenate([fill, segments, fill])
    strength = 1.0 + 4.0 * timestep[0].astype(jnp.float32) / 999.0
    seq_count = lax.axis_size("seq")
    cfg_count = lax.axis_size("cfg")
    spread = lax.all_to_all(qkv, ("seq", "cfg"), split_axis=3, concat_axis=0, tiled=True)
    columns = spread.shape[3]
    heads_here = columns // HD
    block = spread.reshape(seq_count, cfg_count, spread.shape[1], 3, columns)
    start_head = (lax.axis_index("seq") * cfg_count + lax.axis_index("cfg")) * heads_here
    head_windows = lax.dynamic_slice_in_dim(windows, start_head, heads_here, 0).reshape(
        1, heads_here
    )
    attended = attend(block, head_windows, seg_pad, first_frame)
    cond = attended[:, 0].astype(jnp.float32)
    uncond = attended[:, 1].astype(jnp.float32)
    guided = (uncond + strength * (cond - uncond)).astype(jnp.bfloat16)
    own_rows = lax.all_to_all(guided, "seq", split_axis=0, concat_axis=3, tiled=True)
    return own_rows[0]

LOG2E = 1.4426950408889634
MASKED = -1e30
BF16 = jnp.bfloat16
F32 = jnp.float32
VMEM_BYTES = 32 * 1024 * 1024
PLAN_VMEM_BYTES = 60 * 1024 * 1024
SWAP = ((0, 1), (1, 0))
COSTS = {"pack": 1e10, "local": 3e9, "own": 3e9, "across": 3e9, "mix": 1e8, "gate": 1e9}
STEPS = {"O": 0, "X": 1, "NO": 2, "NR": -1, "FO": -2, "FR": 3}
OWN_SOURCES = ("FO", "NR", "O", "X", "NO")
ACROSS_SOURCES = ("NR", "O", "X", "NO", "FR")
DISTANCES = (2, 1, 0, 1, 2)


def whole(space=pltpu.VMEM):
    return pl.BlockSpec(memory_space=space)


def cost(kind):
    return pl.CostEstimate(flops=int(COSTS[kind]), bytes_accessed=1, transcendentals=0)


def params(limit=VMEM_BYTES):
    return pltpu.CompilerParams(vmem_limit_bytes=limit)


class Layout:
    def __init__(self, heads, outs):
        self.mine = 0
        self.theirs = heads // 2
        self.order = heads
        self.rank = 2 * heads
        self.reach = 3 * heads
        self.my_reach = 4 * heads
        self.pos = self.my_reach + heads // 2
        self.own_match = self.pos + outs
        self.across_match = self.own_match + len(DISTANCES)
        self.branch = self.across_match + len(DISTANCES)
        self.column = self.branch + 1
        self.step = self.column + 1
        self.size = self.step + 1


def plan_kernel(
    at, rungs, split, windows_in, segments_in, step_in, x_ref, plan_ref, rung_ref, kv_ref, own_ref,
    windows_ref, segments_ref, step_ref, in_sems, sems,
):
    get_windows = pltpu.make_async_copy(windows_in, windows_ref, in_sems.at[0])
    get_segments = pltpu.make_async_copy(segments_in, segments_ref, in_sems.at[1])
    get_windows.start()
    get_segments.start()
    get_step = pltpu.make_async_copy(step_in, step_ref, in_sems.at[2])
    get_step.start()
    heads = windows_ref.shape[0]
    frames = segments_ref.shape[0]
    column, block, branch = (lax.axis_index(a).astype(jnp.int32) for a in ("seq", "frame", "cfg"))
    get_windows.wait()
    reach = [windows_ref[h] for h in range(heads)]
    wide = [(w >= 2).astype(jnp.int32) for w in reach]
    some = [(w >= 1).astype(jnp.int32) for w in reach]
    most = functools.reduce(lambda a, b: a + b, wide)
    many = functools.reduce(lambda a, b: a + b, some)
    next_wide, next_some, next_none = jnp.int32(0), most, many
    for h in range(heads):
        spot = jnp.where(wide[h] == 1, next_wide, jnp.where(some[h] == 1, next_some, next_none))
        next_wide = next_wide + wide[h]
        next_some = next_some + some[h] - wide[h]
        next_none = next_none + 1 - some[h]
        plan_ref[at.order + spot] = jnp.int32(h)
        plan_ref[at.rank + h] = spot
        plan_ref[at.reach + spot] = reach[h]
    copies = []
    for out_ref, side in ((kv_ref, 1 - column), (own_ref, column)):
        for j in range(out_ref.shape[0]):
            start = pl.multiple_of(plan_ref[at.order + 2 * j + side] * HD, HD)
            for k in range(2):
                copies.append(
                    pltpu.make_async_copy(
                        x_ref.at[k + 1, :, pl.ds(start, HD)], out_ref.at[j, k], sems.at[len(copies)]
                    )
                )
                copies[-1].start()
    for j in range(heads // 2):
        plan_ref[at.mine + j] = plan_ref[at.order + 2 * j + column]
        plan_ref[at.theirs + j] = plan_ref[at.order + 2 * j + 1 - column]
        plan_ref[at.my_reach + j] = plan_ref[at.reach + 2 * j + column]
    columns, cores = split
    per_half = heads // (columns * cores)
    for t in range(columns * per_half):
        head = (t // per_half) * (heads // columns) + branch * per_half + t % per_half
        plan_ref[at.pos + t] = plan_ref[at.rank + head]
    own_frame = 2 * block + column
    sign = 1 - 2 * column

    get_segments.wait()
    get_step.wait()
    plan_ref[at.step] = step_ref[0]

    def shot(name):
        frame = own_frame + STEPS[name] * sign
        inside = jnp.logical_and(frame >= 0, frame < frames)
        return jnp.where(inside, segments_ref[jnp.clip(frame, 0, frames - 1)], -1)

    for first, names, query in (
        (at.own_match, OWN_SOURCES, "O"),
        (at.across_match, ACROSS_SOURCES, "X"),
    ):
        for k, name in enumerate(names):
            plan_ref[first + k] = (shot(name) == shot(query)).astype(jnp.int32)
    plan_ref[at.branch] = branch
    plan_ref[at.column] = column
    index = jnp.int32(len(rungs) - 1)
    for k in reversed(range(len(rungs) - 1)):
        fits = jnp.logical_and(many <= rungs[k][0], most <= rungs[k][1])
        index = jnp.where(fits, jnp.int32(k), index)
    rung_ref[0] = index
    for copy in copies:
        copy.wait()


def pack_kernel(jobs, count_in, plan_ref, x_ref, *refs):
    outs, sems = refs[count_in:-1], refs[-1]
    copies = []
    for out_ref, (spots, planes) in zip(outs, jobs):
        for j, spot in enumerate(spots):
            start = pl.multiple_of(plan_ref[spot] * HD, HD)
            for k, plane in enumerate(planes):
                copies.append(
                    pltpu.make_async_copy(
                        x_ref.at[plane, :, pl.ds(start, HD)],
                        out_ref.at[j, k],
                        sems.at[len(copies)],
                    )
                )
    for copy in copies:
        copy.start()
    for copy in copies:
        copy.wait()


def pack(plan, x3, jobs, after):
    rows = x3.shape[1]
    total = sum(len(spots) * len(planes) for spots, planes in jobs)
    return pl.pallas_call(
        functools.partial(pack_kernel, jobs, len(after)),
        out_shape=[
            jax.ShapeDtypeStruct((len(spots), len(planes), rows, HD), x3.dtype)
            for spots, planes in jobs
        ],
        grid_spec=pltpu.PrefetchScalarGridSpec(
            num_scalar_prefetch=1,
            grid=(1,),
            in_specs=[whole(pl.ANY)] * (1 + len(after)),
            out_specs=[whole(pl.ANY)] * len(jobs),
            scratch_shapes=[pltpu.SemaphoreType.DMA((total,))],
        ),
        compiler_params=params(),
        cost_estimate=cost("pack"),
        name="pack_heads",
    )(plan, x3, *after)


def gate_kernel(*refs):
    del refs


def gate(values, after):
    count = len(values)
    return pl.pallas_call(
        gate_kernel,
        out_shape=[jax.ShapeDtypeStruct(v.shape, v.dtype) for v in values],
        in_specs=[whole(pl.ANY)] * (count + len(after)),
        out_specs=[whole(pl.ANY)] * count,
        input_output_aliases={i: i for i in range(count)},
        compiler_params=params(),
        cost_estimate=cost("gate"),
        name="gate",
    )(*values, *after)


def softmax_mix(q, keys, values, biases):
    factor = LOG2E / math.sqrt(HD)
    scores = []
    for key, bias in zip(keys, biases):
        score = lax.dot_general(q, key, (((1,), (1,)), ((), ())), preferred_element_type=F32)
        scores.append(score if bias is None else score + bias)
    top = jnp.max(functools.reduce(jnp.maximum, scores), axis=1, keepdims=True)
    expd = [jnp.exp2((score - top) * factor) for score in scores]
    total = jnp.sum(functools.reduce(jnp.add, expd), axis=1, keepdims=True)
    mixed = functools.reduce(
        jnp.add,
        [
            jnp.dot(e.astype(BF16), value, preferred_element_type=F32)
            for e, value in zip(expd, values)
        ],
    )
    return (mixed / total).astype(BF16)


def attend_kernel(spec, plan_ref, q_ref, *refs):
    count, sources, gathered, heads_at, reach_at, match_at, distances, branch_at, halves = spec
    kv_refs = refs[:sources]
    refs = refs[sources:]
    if gathered:
        outs, (held, sems) = refs[:-2], refs[-2:]
        outs = outs[-1:]
        copies = []
        planes = held.shape[1]
        for j in range(count):
            start = pl.multiple_of(plan_ref[heads_at + j] * HD, HD)
            for k in range(planes):
                copies.append(
                    pltpu.make_async_copy(
                        q_ref.at[k, :, pl.ds(start, HD)], held.at[j, k], sems.at[j * planes + k]
                    )
                )
        for copy in copies:
            copy.start()
        for copy in copies:
            copy.wait()
    else:
        outs = refs[-2:] if halves else refs[-1:]
    for j in range(count):
        if gathered:
            q = held[j, 0]
        else:
            q = q_ref[j, 0]
        if sources:
            keys = [ref[j, 0] for ref in kv_refs]
            values = [ref[j, 1] for ref in kv_refs]
            reach = plan_ref[reach_at + j]
            biases = []
            for k, distance in enumerate(distances):
                seen = jnp.logical_and(reach >= distance, plan_ref[match_at + k] != 0)
                biases.append(jnp.where(seen, 0.0, MASKED).astype(F32))
        else:
            keys, values, biases = [held[j, 1]], [held[j, 2]], [None]
        out = softmax_mix(q, keys, values, biases)
        if halves:
            half = out.shape[0] // 2
            low, high = out[:half], out[half:]
            first = plan_ref[branch_at] == 0
            outs[0][j] = jnp.where(first, low, high)
            outs[1][j] = jnp.where(first, high, low)
        else:
            outs[0][j] = out


def slot_spec(array, first, count):
    if array.shape[0] == count:
        return whole()
    block = (count, *array.shape[1:])
    return pl.BlockSpec(
        tuple(pl.Element(size) for size in block), lambda i, plan: (first, 0, 0, 0)
    )


def attend_slots(plan, at, q, q_offset, sources, heads_at, first, count, match_at, distances, after):
    rows = q.shape[-2]
    gathered = q.ndim == 3
    spec = (
        count,
        len(sources),
        gathered,
        heads_at,
        at.my_reach + first,
        match_at,
        distances,
        at.branch,
        not gathered,
    )
    kv_specs, kvs = [], []
    for array, offset in sources:
        kvs.append(array)
        kv_specs.append(slot_spec(array, offset, count))
    scratch = []
    if gathered:
        planes = 1 if sources else 3
        scratch = [
            pltpu.VMEM((count, planes, rows, HD), BF16),
            pltpu.SemaphoreType.DMA((count * planes,)),
        ]
        out_shape = jax.ShapeDtypeStruct((count, rows, HD), BF16)
        out_specs = whole()
    else:
        out_shape = [jax.ShapeDtypeStruct((count, rows // 2, HD), BF16)] * 2
        out_specs = [whole()] * 2
    return pl.pallas_call(
        functools.partial(attend_kernel, spec),
        out_shape=out_shape,
        grid_spec=pltpu.PrefetchScalarGridSpec(
            num_scalar_prefetch=1,
            grid=(1,),
            in_specs=[whole(pl.ANY) if gathered else slot_spec(q, q_offset, count)]
            + kv_specs
            + [whole(pl.ANY)] * len(after),
            out_specs=out_specs,
            scratch_shapes=scratch,
        ),
        compiler_params=params(),
        cost_estimate=cost("local" if not sources else "own" if gathered else "across"),
        name="attend",
    )(plan, q, *kvs, *after)


def blend(cond, uncond, strength):
    cond = cond.astype(F32)
    uncond = uncond.astype(F32)
    return (uncond + strength * (cond - uncond)).astype(BF16)


def strength_of(at, plan_ref):
    step = jnp.full((1, HD), plan_ref[at.step], jnp.int32).astype(F32)
    return 1.0 + 4.0 * step / 999.0


def mix_kernel(at, plan_ref, mine_ref, other_ref, *refs):
    out_ref = refs[-1]
    strength = strength_of(at, plan_ref)
    first = plan_ref[at.branch] == 0
    for j in range(out_ref.shape[0]):
        mine, other = mine_ref[j], other_ref[j]
        out_ref[j] = blend(
            jnp.where(first, mine, other), jnp.where(first, other, mine), strength
        )


def mix_cores(plan, at, mine, other, after):
    return pl.pallas_call(
        functools.partial(mix_kernel, at),
        out_shape=jax.ShapeDtypeStruct(mine.shape, mine.dtype),
        in_specs=[whole(pltpu.SMEM)] + [whole()] * 2 + [whole(pl.ANY)] * len(after),
        out_specs=whole(),
        compiler_params=params(),
        cost_estimate=cost("mix"),
        name="mix",
    )(plan, mine, other, *after)


def assemble_kernel(at, own_places, raw_places, places, local, plan_ref, *refs):
    count, own_count, raw_count = len(places), len(own_places), len(raw_places)
    own, refs = refs[:own_count], refs[own_count:]
    mine_refs, refs = refs[:raw_count], refs[raw_count:]
    other_refs, refs = refs[:raw_count], refs[raw_count:]
    strength = strength_of(at, plan_ref)
    kept, moved = refs[:count], refs[count : 2 * count]
    local_ref = refs[2 * count] if local else None
    out_ref, held, turned, sems = refs[-4:]
    branch, column = plan_ref[at.branch], plan_ref[at.column]
    exchanged = 2 * sum(size for _, size in places)

    def one(t, carry):
        p = plan_ref[at.pos + t]
        slot = lax.shift_right_logical(p, 1)
        here = jnp.bitwise_and(p, 1) == column
        is_local = p >= exchanged

        def place(first, size):
            inside = jnp.logical_and(slot >= first, slot < first + size)
            inside = jnp.logical_and(inside, jnp.logical_not(is_local))
            return inside, jnp.clip(slot - first, 0, size - 1)

        for k, (first, size) in enumerate(own_places):
            inside, index = place(first, size)

            @pl.when(jnp.logical_and(inside, here))
            def _(k=k, index=index):
                held[t] = own[k][index]

        for k, (first, size) in enumerate(raw_places):
            inside, index = place(first, size)

            @pl.when(jnp.logical_and(inside, here))
            def _(k=k, index=index):
                mine, other = mine_refs[k][index], other_refs[k][index]
                is_cond = branch == 0
                held[t] = blend(
                    jnp.where(is_cond, mine, other), jnp.where(is_cond, other, mine), strength
                )

        for k, (first, size) in enumerate(places):
            inside, index = place(first, size)

            @pl.when(jnp.logical_and(inside, jnp.logical_not(here)))
            def _(k=k, index=index):
                half = kept[k].shape[1]
                low_here = branch == 0
                mine, other = kept[k][index], moved[k][index]
                held[t, :half] = jnp.where(low_here, mine, other)
                held[t, half:] = jnp.where(low_here, other, mine)

        if local:
            index = jnp.clip(p - exchanged, 0, local - 1)

            @pl.when(is_local)
            def _():
                held[t] = local_ref[index]

        return carry

    lax.fori_loop(0, held.shape[0], one, 0)
    per_half = turned.shape[1]
    half = turned.shape[0] // 2
    copies = []
    for r in range(2):
        tokens = slice(r * half, (r + 1) * half)
        for s in range(held.shape[0] // per_half):
            part = held[s * per_half : (s + 1) * per_half, tokens]
            turned[tokens, :, s * HD : (s + 1) * HD] = jnp.swapaxes(part, 0, 1)
        copies.append(
            pltpu.make_async_copy(turned.at[tokens], out_ref.at[tokens], sems.at[r])
        )
        copies[-1].start()
    for copy in copies:
        copy.wait()


def ranked_body(rungs, qkv, timestep, windows, segments):
    rows = qkv.shape[1]
    heads = windows.shape[0]
    seq_count = lax.axis_size("seq")
    frame_count = lax.axis_size("frame")
    cfg_count = lax.axis_size("cfg")
    per_half = heads // (seq_count * cfg_count)
    outs = seq_count * per_half
    at = Layout(heads, outs)
    x3 = jnp.transpose(qkv[0], (1, 0, 2))
    lead, base = rungs[0][1] // 2, rungs[0][0] // 2
    plan, rung, kv_lead, kv_base = pl.pallas_call(
        functools.partial(plan_kernel, at, rungs, (seq_count, cfg_count)),
        out_shape=[
            jax.ShapeDtypeStruct((at.size,), jnp.int32),
            jax.ShapeDtypeStruct((1,), jnp.int32),
            jax.ShapeDtypeStruct((lead, 2, rows, HD), BF16),
            jax.ShapeDtypeStruct((base, 2, rows, HD), BF16),
        ],
        in_specs=[whole(pltpu.HBM)] * 3 + [whole(pl.ANY)],
        out_specs=[whole(pltpu.SMEM)] * 2 + [whole(pl.ANY)] * 2,
        scratch_shapes=[
            pltpu.SMEM(windows.shape, jnp.int32),
            pltpu.SMEM(segments.shape, jnp.int32),
            pltpu.SMEM(timestep.shape, jnp.int32),
            pltpu.SemaphoreType.DMA((3,)),
            pltpu.SemaphoreType.DMA((2 * (lead + base),)),
        ],
        compiler_params=params(PLAN_VMEM_BYTES),
        name="plan",
    )(windows, segments, timestep, x3)

    grid_axes = ("seq", "frame")
    last = frame_count - 1
    apart = [(i, i - 1) for i in range(1, frame_count)] + [
        (frame_count + i, frame_count + i + 1) for i in range(last)
    ]
    onward = [(i, i + 1) for i in range(last)] + [
        (frame_count + i, frame_count + i - 1) for i in range(1, frame_count)
    ]

    def attempt(rung, plan, x3, kv_lead, kv_base):
        exchanged, wide = rung
        slots, far = exchanged // 2, wide // 2
        local = heads - exchanged
        bounds = [(0, lead), (lead, base)]
        if slots > base:
            bounds.append((base, slots))
        chunks = range(len(bounds))
        reaches = [far >= hi for _, hi in bounds]

        def cross(a):
            return lax.ppermute(a, "seq", SWAP)

        def mate(a):
            return lax.ppermute(a, "cfg", SWAP)

        def mix(mine, other, after):
            return mix_cores(plan, at, mine, other, after)

        across = [cross(kv_lead)]
        near_base = lax.ppermute(kv_base, grid_axes, apart)
        (kv_far,) = pack(plan, x3, [(range(at.mine, at.mine + lead), (1, 2))], [kv_base])
        far_own = [lax.ppermute(kv_far, grid_axes, onward)]
        split = (lead + base) // 2
        parts = [(lead, split, 1), (0, lead, 0)]
        parts += [(lo, hi, k) for k, (lo, hi) in enumerate(bounds) if k > 1] + [(split, base, 1)]
        later = [slot for lo, hi, _ in parts[1:] for slot in range(lo, hi)]
        jobs = [
            ([at.theirs + slot for slot in slots_of], (0,))
            for slots_of in (range(lead, split), later)
        ]
        jobs += [(range(at.theirs + lo, at.theirs + hi), (1, 2)) for lo, hi in bounds[1:]]
        jobs += [(range(at.mine + lo, at.mine + hi), (1, 2)) for lo, hi in bounds[2:]]
        jobs += [(range(at.mine + lead, at.mine + far), (1, 2))] if far > lead else []
        q_early, q_late, *rest = pack(plan, x3, jobs, [kv_far])
        across += [cross(a) for a in rest[: len(bounds) - 1]]
        more = rest[len(bounds) - 1 :]
        if far > lead:
            far_own.append(lax.ppermute(more.pop(), grid_axes, onward))
        kv_more = more
        near_more = [lax.ppermute(a, grid_axes, apart) for a in kv_more]
        done = [rest[0]]
        if local:
            own_local = attend_slots(
                plan, at, x3, 0, [], at.order + exchanged, 0, local, 0, (), done
            )
            peer_local = mate(own_local)
            done = [own_local]

        near_across, far_across, guided = {}, {}, []
        (across[0],) = gate([across[0]], done)
        near_across[0] = lax.ppermute(across[0], grid_axes, onward)
        (q_early,) = gate([q_early], [across[0], *far_own])
        done = [q_early]
        q_early = cross(q_early)
        if local:
            guided = [mix(own_local, peer_local, done)]
            done = guided
        (late,) = gate([across[0]], done)
        far_across[0] = lax.ppermute(late, grid_axes, apart)
        (across[1],) = gate([across[1]], [late, *done])
        (q_late,) = gate([q_late], [across[1]])
        done = [near_across[0], q_late]
        q_late = cross(q_late)
        for k in chunks[1:]:
            (across[k],) = gate([across[k]], done)
            done = [across[k]]
            near_across[k] = lax.ppermute(across[k], grid_axes, onward)
            if reaches[k]:
                far_across[k] = lax.ppermute(across[k], grid_axes, apart)

        def attend_part(k, lo, hi, q, q_offset, names, heads_at, match_at, after):
            skip = lo - bounds[k][0]
            arrays = {
                "O": (kv_more[0], skip) if k > 1 else (kv_base, lo),
                "X": (across[k], skip),
                "NO": (near_more[0], skip) if k > 1 else (near_base, lo),
                "NR": (near_across[k], skip),
                "FO": (far_own[min(k, 1)], max(lo - lead, 0)) if reaches[k] else None,
                "FR": (far_across.get(k), skip),
            }
            cut = slice(0, 5) if reaches[k] else slice(1, 4)
            sources = [arrays[name] for name in names[cut]]
            return attend_slots(
                plan, at, q, q_offset, sources, heads_at + lo, lo, hi - lo,
                match_at + cut.start, DISTANCES[cut], after,
            )

        def attend_own(k, after):
            return attend_part(
                k, *bounds[k], x3, 0, OWN_SOURCES, at.mine, at.own_match, after
            )

        def attend_across(part, after):
            lo, hi, k = parts[part]
            q = q_late if part else q_early
            offset = later.index(lo) if part else 0
            return attend_part(
                k, lo, hi, q, offset, ACROSS_SOURCES, 0, at.across_match, after
            )

        own, kept = {}, []
        own[0] = attend_own(0, done)
        keep, send = attend_across(0, [own[0]])
        got = mate(send)
        end = mix(own[0], mate(own[0]), [keep])
        mixed = mix(keep, got, [end])
        kept.append(cross(mixed))
        waiting = []
        done = [mixed]
        for part in range(1, len(parts)):
            keep, send = attend_across(part, done)
            waiting.append((keep, mate(send)))
            done = [keep]
        done.append(kept[0])
        for keep, got in waiting:
            mixed = mix(keep, got, done)
            kept.append(cross(mixed))
            done = [mixed]
        raw = []
        for k in chunks[1:]:
            lo, hi = bounds[k]
            own[k] = attend_own(k, [mixed, kept[0]])
            middle = (hi - lo) // 2
            raw += [(lo, own[k][:middle]), (lo + middle, own[k][middle:])]
        others = [mate(a) for _, a in raw]
        own_places = ((0, lead),)
        raw_places = tuple((lo, a.shape[0]) for lo, a in raw)
        arrays = [end, *[a for _, a in raw], *others]
        arrays += kept + [mate(a) for a in kept] + guided
        places = tuple((lo, hi - lo) for lo, hi, _ in parts)
        return pl.pallas_call(
            functools.partial(assemble_kernel, at, own_places, raw_places, places, local),
            out_shape=pltpu.HBM((rows, per_half, seq_count * HD), BF16),
            in_specs=[whole(pltpu.SMEM)] + [whole()] * len(arrays),
            out_specs=whole(pltpu.HBM),
            scratch_shapes=[
                pltpu.VMEM((outs, rows, HD), BF16),
                pltpu.VMEM((rows, per_half, seq_count * HD), BF16),
                pltpu.SemaphoreType.DMA((2,)),
            ],
            compiler_params=params(),
            name="assemble",
        )(plan, *arrays)

    return lax.switch(
        rung[0],
        [functools.partial(attempt, rung) for rung in rungs],
        plan, x3, kv_lead, kv_base,
    )


def rungs_of(heads):
    third = heads // 3
    return ((2 * third + 2, third), (2 * third + 2, 2 * third + 2), (heads, heads))


def solution(mesh):
    sizes = dict(mesh.shape)

    def whole_body(qkv, timestep, windows, segments):
        frames_here = segments.shape[0] // sizes["frame"]
        one_frame = frames_here == sizes["seq"]
        if sizes["seq"] == 2 and sizes["cfg"] == 2 and one_frame and qkv.shape[1] % 32 == 0:
            return ranked_body(rungs_of(windows.shape[0]), qkv, timestep, windows, segments)
        return body(qkv, timestep, windows, segments)

    return jax.shard_map(
        whole_body,
        mesh=mesh,
        in_specs=(P("cfg", ("groups", "frame", "seq"), None, None), P("groups"), P(), P("groups")),
        out_specs=P(("groups", "frame", "seq"), "cfg", None),
        check_vma=False,
    )
```

```python
import functools
import math

import jax
import jax.numpy as jnp
from jax import lax
from jax.experimental import pallas as pl
from jax.experimental.pallas import tpu as pltpu
from jax.sharding import PartitionSpec as P

HD = 128
F_DEV = 2
W_MAX = 2


def padded_2(block, sides, width):
    for axis, dim in sides:
        count = lax.axis_size(axis)
        forward = [(i, i + 1) for i in range(count - 1)]
        backward = [(target, source) for source, target in forward]
        low = lax.ppermute(
            lax.slice_in_dim(block, block.shape[dim] - width, None, axis=dim), axis, forward
        )
        high = lax.ppermute(lax.slice_in_dim(block, 0, width, axis=dim), axis, backward)
        block = jnp.concatenate([low, block, high], axis=dim)
    return block


def attend(block, head_windows, seg_pad, first_frame):
    count_blocks = block.shape[0]
    branches = block.shape[1]
    rows_block = block.shape[2]
    columns = block.shape[4]
    heads_here = columns // HD
    per_frame = count_blocks // F_DEV
    reach = W_MAX * per_frame
    span = 2 * W_MAX + 1
    scale = 1.0 / math.sqrt(HD)
    pairs = block[:, :, :, 1:]
    padded = padded_2(pairs, (("frame", 0),), reach)
    queries = block[:, :, :, 0].reshape(count_blocks, branches, rows_block, heads_here, HD)
    offsets = jnp.arange(span, dtype=jnp.int32) - W_MAX
    within_reach = jnp.abs(offsets)[None, None, :] <= head_windows[:, :, None]
    results = []
    for frame_number in range(F_DEV):
        query = queries[frame_number * per_frame : (frame_number + 1) * per_frame]
        window_rows = padded[frame_number * per_frame : frame_number * per_frame + span * per_frame]
        window_rows = window_rows.reshape(span * per_frame, branches, rows_block, 2, heads_here, HD)
        key_rows = window_rows[:, :, :, 0]
        value_rows = window_rows[:, :, :, 1]
        here = first_frame + frame_number
        shots = lax.dynamic_slice_in_dim(seg_pad, here, span, 0)
        own_shot = lax.dynamic_index_in_dim(seg_pad, here + W_MAX, 0, keepdims=False)
        allowed = within_reach & (shots == own_shot)[None, None, :]
        allowed = jnp.repeat(allowed, per_frame, axis=2)
        scores = (
            jnp.einsum("sbthd,ubrhd->bhstur", query, key_rows, preferred_element_type=jnp.float32)
            * scale
        )
        scores = jnp.where(allowed[:, :, None, None, :, None], scores, -1e30)
        highest = jnp.max(scores, axis=(4, 5), keepdims=True)
        expd = jnp.exp(scores - highest)
        totals = jnp.sum(expd, axis=(4, 5))
        weights = expd.astype(jnp.bfloat16)
        mixed = jnp.einsum(
            "bhstur,ubrhd->sbthd", weights, value_rows, preferred_element_type=jnp.float32
        )
        mixed = mixed / jnp.transpose(totals, (2, 0, 3, 1))[..., None]
        results.append(mixed.astype(jnp.bfloat16))
    return jnp.concatenate(results, axis=0)


def body(qkv, timestep, windows, segments):
    first_frame = lax.axis_index("frame") * F_DEV
    fill = jnp.full((W_MAX,), -1, jnp.int32)
    seg_pad = jnp.concatenate([fill, segments, fill])
    strength = 1.0 + 4.0 * timestep[0].astype(jnp.float32) / 999.0
    seq_count = lax.axis_size("seq")
    cfg_count = lax.axis_size("cfg")
    spread = lax.all_to_all(qkv, ("seq", "cfg"), split_axis=3, concat_axis=0, tiled=True)
    columns = spread.shape[3]
    heads_here = columns // HD
    block = spread.reshape(seq_count, cfg_count, spread.shape[1], 3, columns)
    start_head = (lax.axis_index("seq") * cfg_count + lax.axis_index("cfg")) * heads_here
    head_windows = lax.dynamic_slice_in_dim(windows, start_head, heads_here, 0).reshape(
        1, heads_here
    )
    attended = attend(block, head_windows, seg_pad, first_frame)
    cond = attended[:, 0].astype(jnp.float32)
    uncond = attended[:, 1].astype(jnp.float32)
    guided = (uncond + strength * (cond - uncond)).astype(jnp.bfloat16)
    own_rows = lax.all_to_all(guided, "seq", split_axis=0, concat_axis=3, tiled=True)
    return own_rows[0]

LOG2E = 1.4426950408889634
MASKED = -1e30
BF16 = jnp.bfloat16
F32 = jnp.float32
VMEM_BYTES = 32 * 1024 * 1024
PLAN_VMEM_BYTES = 60 * 1024 * 1024
SWAP = ((0, 1), (1, 0))
COSTS = {"pack": 1e10, "local": 3e9, "own": 3e9, "across": 3e9, "mix": 1e8, "gate": 1e9}
STEPS = {"O": 0, "X": 1, "NO": 2, "NR": -1, "FO": -2, "FR": 3}
OWN_SOURCES = ("FO", "NR", "O", "X", "NO")
ACROSS_SOURCES = ("NR", "O", "X", "NO", "FR")
DISTANCES = (2, 1, 0, 1, 2)


def whole(space=pltpu.VMEM):
    return pl.BlockSpec(memory_space=space)


def cost(kind):
    return pl.CostEstimate(flops=int(COSTS[kind]), bytes_accessed=1, transcendentals=0)


def params(limit=VMEM_BYTES):
    return pltpu.CompilerParams(vmem_limit_bytes=limit)


class Rows:
    def __init__(self, heads):
        self.strength = 0
        self.cond = 1
        self.own = 8
        self.across = self.own + heads // 2 * len(DISTANCES)
        self.size = self.across + heads // 2 * len(DISTANCES)


class Layout:
    def __init__(self, heads, outs):
        self.mine = 0
        self.theirs = heads // 2
        self.order = heads
        self.rank = 2 * heads
        self.reach = 3 * heads
        self.my_reach = 4 * heads
        self.pos = self.my_reach + heads // 2
        self.own_match = self.pos + outs
        self.across_match = self.own_match + len(DISTANCES)
        self.branch = self.across_match + len(DISTANCES)
        self.column = self.branch + 1
        self.step = self.column + 1
        self.size = self.step + 1


def plan_kernel(
    at, rungs, split, windows_in, segments_in, step_in, x_ref, plan_ref, rung_ref, kv_ref, own_ref,
    windows_ref, segments_ref, step_ref, in_sems, sems,
):
    get_windows = pltpu.make_async_copy(windows_in, windows_ref, in_sems.at[0])
    get_segments = pltpu.make_async_copy(segments_in, segments_ref, in_sems.at[1])
    get_windows.start()
    get_segments.start()
    get_step = pltpu.make_async_copy(step_in, step_ref, in_sems.at[2])
    get_step.start()
    heads = windows_ref.shape[0]
    frames = segments_ref.shape[0]
    column, block, branch = (lax.axis_index(a).astype(jnp.int32) for a in ("seq", "frame", "cfg"))
    get_windows.wait()
    reach = [windows_ref[h] for h in range(heads)]
    wide = [(w >= 2).astype(jnp.int32) for w in reach]
    some = [(w >= 1).astype(jnp.int32) for w in reach]
    most = functools.reduce(lambda a, b: a + b, wide)
    many = functools.reduce(lambda a, b: a + b, some)
    next_wide, next_some, next_none = jnp.int32(0), most, many
    for h in range(heads):
        spot = jnp.where(wide[h] == 1, next_wide, jnp.where(some[h] == 1, next_some, next_none))
        next_wide = next_wide + wide[h]
        next_some = next_some + some[h] - wide[h]
        next_none = next_none + 1 - some[h]
        plan_ref[at.order + spot] = jnp.int32(h)
        plan_ref[at.rank + h] = spot
        plan_ref[at.reach + spot] = reach[h]
    copies = []
    for out_ref, side in ((kv_ref, 1 - column), (own_ref, column)):
        for j in range(out_ref.shape[0]):
            start = pl.multiple_of(plan_ref[at.order + 2 * j + side] * HD, HD)
            copies.append(
                pltpu.make_async_copy(
                    x_ref.at[1:3, :, pl.ds(start, HD)], out_ref.at[j], sems.at[len(copies)]
                )
            )
            copies[-1].start()
    for j in range(heads // 2):
        plan_ref[at.mine + j] = plan_ref[at.order + 2 * j + column]
        plan_ref[at.theirs + j] = plan_ref[at.order + 2 * j + 1 - column]
        plan_ref[at.my_reach + j] = plan_ref[at.reach + 2 * j + column]
    columns, cores = split
    per_half = heads // (columns * cores)
    for t in range(columns * per_half):
        head = (t // per_half) * (heads // columns) + branch * per_half + t % per_half
        plan_ref[at.pos + t] = plan_ref[at.rank + head]
    own_frame = 2 * block + column
    sign = 1 - 2 * column

    get_segments.wait()
    get_step.wait()
    plan_ref[at.step] = step_ref[0]

    def shot(name):
        frame = own_frame + STEPS[name] * sign
        inside = jnp.logical_and(frame >= 0, frame < frames)
        return jnp.where(inside, segments_ref[jnp.clip(frame, 0, frames - 1)], -1)

    for first, names, query in (
        (at.own_match, OWN_SOURCES, "O"),
        (at.across_match, ACROSS_SOURCES, "X"),
    ):
        for k, name in enumerate(names):
            plan_ref[first + k] = (shot(name) == shot(query)).astype(jnp.int32)
    plan_ref[at.branch] = branch
    plan_ref[at.column] = column
    index = jnp.int32(len(rungs) - 1)
    for k in reversed(range(len(rungs) - 1)):
        fits = jnp.logical_and(many <= rungs[k][0], most <= rungs[k][1])
        index = jnp.where(fits, jnp.int32(k), index)
    rung_ref[0] = index
    for copy in copies:
        copy.wait()


def pack_kernel(jobs, count_in, plan_ref, x_ref, *refs):
    outs, sems = refs[count_in:-1], refs[-1]
    copies = []
    for out_ref, (spots, first, last) in zip(outs, jobs):
        for j, spot in enumerate(spots):
            start = pl.multiple_of(plan_ref[spot] * HD, HD)
            copies.append(
                pltpu.make_async_copy(
                    x_ref.at[first:last, :, pl.ds(start, HD)],
                    out_ref.at[j],
                    sems.at[len(copies)],
                )
            )
    for copy in copies:
        copy.start()
    for copy in copies:
        copy.wait()


def pack(plan, x3, jobs, after):
    rows = x3.shape[1]
    return pl.pallas_call(
        functools.partial(pack_kernel, jobs, len(after)),
        out_shape=[
            jax.ShapeDtypeStruct((len(spots), last - first, rows, HD), x3.dtype)
            for spots, first, last in jobs
        ],
        in_specs=[whole(pltpu.SMEM)] + [whole(pl.ANY)] * (1 + len(after)),
        out_specs=[whole(pl.ANY)] * len(jobs),
        scratch_shapes=[pltpu.SemaphoreType.DMA((sum(len(spots) for spots, _, _ in jobs),))],
        compiler_params=params(),
        cost_estimate=cost("pack"),
        name="pack_heads",
    )(plan, x3, *after)


def gate_kernel(*refs):
    del refs


def gate(values, after):
    count = len(values)
    return pl.pallas_call(
        gate_kernel,
        out_shape=[jax.ShapeDtypeStruct(v.shape, v.dtype) for v in values],
        in_specs=[whole(pl.ANY)] * (count + len(after)),
        out_specs=[whole(pl.ANY)] * count,
        input_output_aliases={i: i for i in range(count)},
        compiler_params=params(),
        cost_estimate=cost("gate"),
        name="gate",
    )(*values, *after)


def softmax_mix(q, keys, values, biases):
    factor = LOG2E / math.sqrt(HD)
    scores = []
    for key, bias in zip(keys, biases):
        score = lax.dot_general(q, key, (((1,), (1,)), ((), ())), preferred_element_type=F32)
        scores.append(score if bias is None else score + bias)
    top = jnp.max(functools.reduce(jnp.maximum, scores), axis=1, keepdims=True)
    expd = [jnp.exp2((score - top) * factor) for score in scores]
    total = jnp.sum(functools.reduce(jnp.add, expd), axis=1, keepdims=True)
    mixed = functools.reduce(
        jnp.add,
        [
            jnp.dot(e.astype(BF16), value, preferred_element_type=F32)
            for e, value in zip(expd, values)
        ],
    )
    return mixed / total


def table_kernel(at, rows_at, plan_ref, *refs):
    table_ref = refs[-1]
    width = table_ref.shape[1]

    def put(row, value):
        table_ref[row : row + 1, :] = jnp.full((1, width), value, F32)

    step = jnp.full((1, width), plan_ref[at.step], jnp.int32).astype(F32)
    table_ref[rows_at.strength : rows_at.strength + 1, :] = 1.0 + 4.0 * step / 999.0
    put(rows_at.cond, jnp.where(plan_ref[at.branch] == 0, 1.0, 0.0).astype(F32))
    for first, match_at in ((rows_at.own, at.own_match), (rows_at.across, at.across_match)):
        for slot in range((rows_at.across - rows_at.own) // len(DISTANCES)):
            reach = plan_ref[at.my_reach + slot]
            for k, distance in enumerate(DISTANCES):
                seen = jnp.logical_and(reach >= distance, plan_ref[match_at + k] != 0)
                put(
                    first + slot * len(DISTANCES) + k, jnp.where(seen, 0.0, MASKED).astype(F32)
                )


def make_table(plan, at, rows_at, width, after):
    return pl.pallas_call(
        functools.partial(table_kernel, at, rows_at),
        out_shape=jax.ShapeDtypeStruct((rows_at.size, width), F32),
        in_specs=[whole(pltpu.SMEM)] + [whole(pl.ANY)] * len(after),
        out_specs=whole(),
        compiler_params=params(),
        cost_estimate=cost("mix"),
        name="table",
    )(plan, *after)


def local_kernel(count, heads_at, plan_ref, x_ref, *refs):
    out_ref, held, sems = refs[-3:]
    copies = []
    for j in range(count):
        start = pl.multiple_of(plan_ref[heads_at + j] * HD, HD)
        copies.append(
            pltpu.make_async_copy(x_ref.at[:, :, pl.ds(start, HD)], held.at[j], sems.at[j])
        )
        copies[-1].start()
    for copy in copies:
        copy.wait()
    for j in range(count):
        out_ref[j] = softmax_mix(held[j, 0], [held[j, 1]], [held[j, 2]], [None]).astype(BF16)


def attend_local(plan, x3, heads_at, count, after):
    planes, rows, _ = x3.shape
    return pl.pallas_call(
        functools.partial(local_kernel, count, heads_at),
        out_shape=jax.ShapeDtypeStruct((count, rows, HD), BF16),
        in_specs=[whole(pltpu.SMEM)] + [whole(pl.ANY)] * (1 + len(after)),
        out_specs=whole(),
        scratch_shapes=[
            pltpu.VMEM((count, planes, rows, HD), BF16),
            pltpu.SemaphoreType.DMA((count,)),
        ],
        compiler_params=params(),
        cost_estimate=cost("local"),
        name="attend_local",
    )(plan, x3, *after)


def attend_kernel(count, q_offset, offsets, bias_at, cond_at, table_ref, q_ref, *refs):
    sources = len(offsets)
    kv_refs = refs[:sources]
    halves = cond_at is not None
    outs = refs[-2:] if halves else refs[-1:]
    for j in range(count):
        keys = [ref[o + j, 0] for ref, o in zip(kv_refs, offsets)]
        values = [ref[o + j, 1] for ref, o in zip(kv_refs, offsets)]
        first = bias_at + j * len(DISTANCES)
        biases = [table_ref[first + k : first + k + 1, :] for k in range(sources)]
        out = softmax_mix(q_ref[q_offset + j, 0], keys, values, biases)
        if halves:
            half = out.shape[0] // 2
            low, high = out[:half], out[half:]
            is_first = table_ref[cond_at : cond_at + 1, :HD] > 0.0
            outs[0][j] = jnp.where(is_first, low, high).astype(BF16)
            outs[1][j] = jnp.where(is_first, high, low).astype(BF16)
        else:
            outs[0][j] = out.astype(BF16)


def attend_slots(table, q, q_offset, sources, count, bias_at, cond_at, after):
    rows = q.shape[-2]
    if cond_at is None:
        out_shape = jax.ShapeDtypeStruct((count, rows, HD), BF16)
        out_specs = whole()
    else:
        out_shape = [jax.ShapeDtypeStruct((count, rows // 2, HD), BF16)] * 2
        out_specs = [whole()] * 2
    arrays = [array for array, _ in sources]
    offsets = [offset for _, offset in sources]
    return pl.pallas_call(
        functools.partial(attend_kernel, count, q_offset, offsets, bias_at, cond_at),
        out_shape=out_shape,
        in_specs=[whole()] * (2 + len(arrays)) + [whole(pl.ANY)] * len(after),
        out_specs=out_specs,
        compiler_params=params(),
        cost_estimate=cost("own" if cond_at is None else "across"),
        name="attend",
    )(table, q, *arrays, *after)


def blend(cond, uncond, strength):
    cond = cond.astype(F32)
    uncond = uncond.astype(F32)
    return (uncond + strength * (cond - uncond)).astype(BF16)


def mix_branches(rows_at, table_ref, mine, other):
    strength = table_ref[rows_at.strength : rows_at.strength + 1, :HD]
    is_cond = table_ref[rows_at.cond : rows_at.cond + 1, :HD] > 0.0
    mine = mine.astype(F32)
    other = other.astype(F32)
    return blend(jnp.where(is_cond, mine, other), jnp.where(is_cond, other, mine), strength)


def mix_kernel(rows_at, pieces, table_ref, mine_ref, *refs):
    out_ref = refs[-1]
    j = 0
    for other_ref in refs[:pieces]:
        for i in range(other_ref.shape[0]):
            out_ref[j] = mix_branches(rows_at, table_ref, mine_ref[j], other_ref[i])
            j += 1


def mix_cores(table, rows_at, mine, others, after):
    return pl.pallas_call(
        functools.partial(mix_kernel, rows_at, len(others)),
        out_shape=jax.ShapeDtypeStruct(mine.shape, mine.dtype),
        in_specs=[whole()] * (2 + len(others)) + [whole(pl.ANY)] * len(after),
        out_specs=whole(),
        compiler_params=params(),
        cost_estimate=cost("mix"),
        name="mix",
    )(table, mine, *others, *after)


def assemble_kernel(at, rows_at, sizes, slots, places, plan_in, table_ref, *refs):
    out_ref, plan_ref, listed, turned, plan_sem, out_sems = refs[-6:]
    get_plan = pltpu.make_async_copy(plan_in, plan_ref, plan_sem.at[0])
    get_plan.start()
    own_count, raw_count, cross_count = sizes
    refs = list(refs[:-6])

    def take(count):
        taken = refs[:count]
        del refs[:count]
        return taken

    own, raw, raw_other = take(own_count), take(raw_count), take(raw_count)
    kept, moved, local = take(cross_count), take(cross_count), refs
    for ref, first in zip(own, places[0]):
        for j in range(ref.shape[0]):
            listed[first + j] = ref[j]
    for ref in local:
        for j in range(ref.shape[0]):
            listed[2 * slots + j] = ref[j]
    for ref, other, first in zip(raw, raw_other, places[1]):
        for j in range(ref.shape[0]):
            listed[first + j] = mix_branches(rows_at, table_ref, ref[j], other[j])
    low_here = table_ref[rows_at.cond : rows_at.cond + 1, :HD] > 0.0
    for ref, other, first in zip(kept, moved, places[2]):
        half = ref.shape[1]
        for j in range(ref.shape[0]):
            mine, theirs = ref[j].astype(F32), other[j].astype(F32)
            low = jnp.where(low_here, mine, theirs).astype(BF16)
            high = jnp.where(low_here, theirs, mine).astype(BF16)
            listed[slots + first + j, :half] = low
            listed[slots + first + j, half:] = high
    get_plan.wait()
    column = plan_ref[at.column]
    per_half = turned.shape[1]
    count = turned.shape[2] // HD * per_half
    spots = []
    for t in range(count):
        p = plan_ref[at.pos + t]
        slot = lax.shift_right_logical(p, 1)
        paired = jnp.where(jnp.bitwise_and(p, 1) == column, slot, slots + slot)
        spots.append(jnp.where(p >= 2 * slots, p, paired))
    parts = 2
    size = turned.shape[0] // parts
    copies = []
    for r in range(parts):
        tokens = slice(r * size, (r + 1) * size)
        for s in range(count // per_half):
            picked = [listed[spots[s * per_half + a], tokens] for a in range(per_half)]
            turned[tokens, :, s * HD : (s + 1) * HD] = jnp.swapaxes(jnp.stack(picked), 0, 1)
        copies.append(
            pltpu.make_async_copy(turned.at[tokens], out_ref.at[tokens], out_sems.at[r])
        )
        copies[-1].start()
    for copy in copies:
        copy.wait()


def ranked_body(rungs, qkv, timestep, windows, segments):
    rows = qkv.shape[1]
    heads = windows.shape[0]
    seq_count = lax.axis_size("seq")
    frame_count = lax.axis_size("frame")
    cfg_count = lax.axis_size("cfg")
    per_half = heads // (seq_count * cfg_count)
    outs = seq_count * per_half
    at = Layout(heads, outs)
    rows_at = Rows(heads)
    x3 = jnp.transpose(qkv[0], (1, 0, 2))
    lead, base = rungs[0][1] // 2, rungs[0][0] // 2
    plan, rung, kv_lead, kv_base = pl.pallas_call(
        functools.partial(plan_kernel, at, rungs, (seq_count, cfg_count)),
        out_shape=[
            jax.ShapeDtypeStruct((at.size,), jnp.int32),
            jax.ShapeDtypeStruct((1,), jnp.int32),
            jax.ShapeDtypeStruct((lead, 2, rows, HD), BF16),
            jax.ShapeDtypeStruct((base, 2, rows, HD), BF16),
        ],
        in_specs=[whole(pltpu.HBM)] * 3 + [whole(pl.ANY)],
        out_specs=[whole(pltpu.SMEM)] * 2 + [whole(pl.ANY)] * 2,
        scratch_shapes=[
            pltpu.SMEM(windows.shape, jnp.int32),
            pltpu.SMEM(segments.shape, jnp.int32),
            pltpu.SMEM(timestep.shape, jnp.int32),
            pltpu.SemaphoreType.DMA((3,)),
            pltpu.SemaphoreType.DMA((lead + base,)),
        ],
        compiler_params=params(PLAN_VMEM_BYTES),
        name="plan",
    )(windows, segments, timestep, x3)

    grid_axes = ("seq", "frame")
    last = frame_count - 1
    apart = [(i, i - 1) for i in range(1, frame_count)] + [
        (frame_count + i, frame_count + i + 1) for i in range(last)
    ]
    onward = [(i, i + 1) for i in range(last)] + [
        (frame_count + i, frame_count + i - 1) for i in range(1, frame_count)
    ]

    def attempt(rung, plan, x3, kv_lead, kv_base):
        exchanged, wide = rung
        slots, far = exchanged // 2, wide // 2
        local = heads - exchanged
        bounds = [(0, lead), (lead, base)]
        if slots > base:
            bounds.append((base, slots))
        chunks = range(len(bounds))
        reaches = [far >= hi for _, hi in bounds]

        def cross(a):
            return lax.ppermute(a, "seq", SWAP)

        def mate(a):
            return lax.ppermute(a, "cfg", SWAP)

        def mix(mine, others, after):
            return mix_cores(table, rows_at, mine, others, after)

        across = [cross(kv_lead)]
        near_base = lax.ppermute(kv_base, grid_axes, apart)
        (kv_far,) = pack(plan, x3, [(range(at.mine, at.mine + lead), 1, 3)], [kv_base])
        far_own = [lax.ppermute(kv_far, grid_axes, onward)]
        split = (lead + base) // 2
        parts = [(lead, split, 1), (split, base, 1)]
        parts += [(lo, hi, k) for k, (lo, hi) in enumerate(bounds) if k > 1] + [(0, lead, 0)]
        later = [slot for lo, hi, _ in parts[1:] for slot in range(lo, hi)]
        jobs = [
            ([at.theirs + slot for slot in slots_of], 0, 1)
            for slots_of in (range(lead, split), later)
        ]
        jobs += [(range(at.theirs + lo, at.theirs + hi), 1, 3) for lo, hi in bounds[1:]]
        jobs += [(range(at.mine + lo, at.mine + hi), 1, 3) for lo, hi in bounds[2:]]
        jobs += [(range(at.mine + lead, at.mine + far), 1, 3)] if far > lead else []
        jobs.insert(0, (range(at.mine, at.mine + slots), 0, 1))
        q_own, q_early, q_late, *rest = pack(plan, x3, jobs, [kv_far])
        across += [cross(a) for a in rest[: len(bounds) - 1]]
        more = rest[len(bounds) - 1 :]
        if far > lead:
            far_own.append(lax.ppermute(more.pop(), grid_axes, onward))
        kv_more = more
        near_more = [lax.ppermute(a, grid_axes, apart) for a in kv_more]
        table = make_table(plan, at, rows_at, rows, [rest[0]])
        done = [table]
        if local:
            own_local = attend_local(plan, x3, at.order + exchanged, local, done)
            peer_local = mate(own_local)
            done = [own_local]

        near_across, far_across, guided = {}, {}, []
        (across[0],) = gate([across[0]], done)
        near_across[0] = lax.ppermute(across[0], grid_axes, onward)
        (q_early,) = gate([q_early], [across[0], *far_own])
        done = [q_early]
        q_early = cross(q_early)
        if local:
            guided = [mix(own_local, [peer_local], done)]
            done = guided
        (late,) = gate([across[0]], done)
        far_across[0] = lax.ppermute(late, grid_axes, apart)
        (across[1],) = gate([across[1]], [late, *done])
        (q_late,) = gate([q_late], [across[1]])
        done = [near_across[0], q_late]
        q_late = cross(q_late)
        for k in chunks[1:]:
            (across[k],) = gate([across[k]], done)
            done = [across[k]]
            near_across[k] = lax.ppermute(across[k], grid_axes, onward)
            if reaches[k]:
                far_across[k] = lax.ppermute(across[k], grid_axes, apart)

        def attend_part(k, lo, hi, q, q_offset, names, bias_at, cond_at, after):
            skip = lo - bounds[k][0]
            arrays = {
                "O": (kv_more[0], skip) if k > 1 else (kv_base, lo),
                "X": (across[k], skip),
                "NO": (near_more[0], skip) if k > 1 else (near_base, lo),
                "NR": (near_across[k], skip),
                "FO": (far_own[min(k, 1)], max(lo - lead, 0)) if reaches[k] else None,
                "FR": (far_across.get(k), skip),
            }
            cut = slice(0, 5) if reaches[k] else slice(1, 4)
            sources = [arrays[name] for name in names[cut]]
            bias_at += lo * len(DISTANCES) + cut.start
            return attend_slots(table, q, q_offset, sources, hi - lo, bias_at, cond_at, after)

        def attend_own(k, after):
            lo, hi = bounds[k]
            return attend_part(k, lo, hi, q_own, lo, OWN_SOURCES, rows_at.own, None, after)

        def attend_across(part, after):
            lo, hi, k = parts[part]
            q = q_late if part else q_early
            offset = later.index(lo) if part else 0
            return attend_part(
                k, lo, hi, q, offset, ACROSS_SOURCES, rows_at.across, rows_at.cond, after
            )

        own, kept = {}, []
        own[0] = attend_own(0, done)
        keep, send = attend_across(0, [own[0]])
        got = mate(send)
        end = mix(own[0], [mate(own[0])], [keep])
        mixed = mix(keep, [got], [end])
        kept.append(cross(mixed))
        waiting = []
        done = [mixed]
        for part in range(1, len(parts)):
            keep, send = attend_across(part, done)
            middle = send.shape[0] // 2
            pieces = [send] if part < len(parts) - 1 else [send[:middle], send[middle:]]
            waiting.append((keep, [mate(piece) for piece in pieces]))
            done = [keep]
        done.append(kept[0])
        for keep, got in waiting:
            mixed = mix(keep, got, done)
            kept.append(cross(mixed))
            done = [mixed]
        raw = []
        for k in chunks[1:]:
            lo, hi = bounds[k]
            own[k] = attend_own(k, [mixed, kept[0]])
            middle = (hi - lo) // 2
            raw += [(lo, own[k][:middle]), (lo + middle, own[k][middle:])]
        others = [mate(a) for _, a in raw]
        arrays = [end, *[a for _, a in raw], *others, *kept, *[mate(a) for a in kept], *guided]
        places = ([0], [lo for lo, _ in raw], [lo for lo, _, _ in parts])
        sizes = tuple(len(firsts) for firsts in places)
        return pl.pallas_call(
            functools.partial(assemble_kernel, at, rows_at, sizes, slots, places),
            out_shape=pltpu.HBM((rows, per_half, seq_count * HD), BF16),
            in_specs=[whole(pl.ANY)] + [whole()] * (1 + len(arrays)),
            out_specs=whole(pltpu.HBM),
            scratch_shapes=[
                pltpu.SMEM(plan.shape, plan.dtype),
                pltpu.VMEM((heads, rows, HD), BF16),
                pltpu.VMEM((rows, per_half, seq_count * HD), BF16),
                pltpu.SemaphoreType.DMA((1,)),
                pltpu.SemaphoreType.DMA((2,)),
            ],
            compiler_params=params(),
            name="assemble",
        )(plan, table, *arrays)

    return lax.switch(
        rung[0],
        [functools.partial(attempt, rung) for rung in rungs],
        plan, x3, kv_lead, kv_base,
    )


def rungs_of(heads):
    third = heads // 3
    return ((2 * third + 2, third), (2 * third + 2, 2 * third + 2), (heads, heads))


def solution(mesh):
    sizes = dict(mesh.shape)

    def whole_body(qkv, timestep, windows, segments):
        frames_here = segments.shape[0] // sizes["frame"]
        one_frame = frames_here == sizes["seq"]
        if sizes["seq"] == 2 and sizes["cfg"] == 2 and one_frame and qkv.shape[1] % 32 == 0:
            return ranked_body(rungs_of(windows.shape[0]), qkv, timestep, windows, segments)
        return body(qkv, timestep, windows, segments)

    return jax.shard_map(
        whole_body,
        mesh=mesh,
        in_specs=(P("cfg", ("groups", "frame", "seq"), None, None), P("groups"), P(), P("groups")),
        out_specs=P(("groups", "frame", "seq"), "cfg", None),
        check_vma=False,
    )
```

```python
import functools
import math

import jax
import jax.numpy as jnp
from jax import lax
from jax.experimental import pallas as pl
from jax.experimental.pallas import tpu as pltpu
from jax.sharding import PartitionSpec as P

HD = 128
F_DEV = 2
W_MAX = 2


def padded_2(block, sides, width):
    for axis, dim in sides:
        count = lax.axis_size(axis)
        forward = [(i, i + 1) for i in range(count - 1)]
        backward = [(target, source) for source, target in forward]
        low = lax.ppermute(
            lax.slice_in_dim(block, block.shape[dim] - width, None, axis=dim), axis, forward
        )
        high = lax.ppermute(lax.slice_in_dim(block, 0, width, axis=dim), axis, backward)
        block = jnp.concatenate([low, block, high], axis=dim)
    return block


def attend(block, head_windows, seg_pad, first_frame):
    count_blocks = block.shape[0]
    branches = block.shape[1]
    rows_block = block.shape[2]
    columns = block.shape[4]
    heads_here = columns // HD
    per_frame = count_blocks // F_DEV
    reach = W_MAX * per_frame
    span = 2 * W_MAX + 1
    scale = 1.0 / math.sqrt(HD)
    pairs = block[:, :, :, 1:]
    padded = padded_2(pairs, (("frame", 0),), reach)
    queries = block[:, :, :, 0].reshape(count_blocks, branches, rows_block, heads_here, HD)
    offsets = jnp.arange(span, dtype=jnp.int32) - W_MAX
    within_reach = jnp.abs(offsets)[None, None, :] <= head_windows[:, :, None]
    results = []
    for frame_number in range(F_DEV):
        query = queries[frame_number * per_frame : (frame_number + 1) * per_frame]
        window_rows = padded[frame_number * per_frame : frame_number * per_frame + span * per_frame]
        window_rows = window_rows.reshape(span * per_frame, branches, rows_block, 2, heads_here, HD)
        key_rows = window_rows[:, :, :, 0]
        value_rows = window_rows[:, :, :, 1]
        here = first_frame + frame_number
        shots = lax.dynamic_slice_in_dim(seg_pad, here, span, 0)
        own_shot = lax.dynamic_index_in_dim(seg_pad, here + W_MAX, 0, keepdims=False)
        allowed = within_reach & (shots == own_shot)[None, None, :]
        allowed = jnp.repeat(allowed, per_frame, axis=2)
        scores = (
            jnp.einsum("sbthd,ubrhd->bhstur", query, key_rows, preferred_element_type=jnp.float32)
            * scale
        )
        scores = jnp.where(allowed[:, :, None, None, :, None], scores, -1e30)
        highest = jnp.max(scores, axis=(4, 5), keepdims=True)
        expd = jnp.exp(scores - highest)
        totals = jnp.sum(expd, axis=(4, 5))
        weights = expd.astype(jnp.bfloat16)
        mixed = jnp.einsum(
            "bhstur,ubrhd->sbthd", weights, value_rows, preferred_element_type=jnp.float32
        )
        mixed = mixed / jnp.transpose(totals, (2, 0, 3, 1))[..., None]
        results.append(mixed.astype(jnp.bfloat16))
    return jnp.concatenate(results, axis=0)


def body(qkv, timestep, windows, segments):
    first_frame = lax.axis_index("frame") * F_DEV
    fill = jnp.full((W_MAX,), -1, jnp.int32)
    seg_pad = jnp.concatenate([fill, segments, fill])
    strength = 1.0 + 4.0 * timestep[0].astype(jnp.float32) / 999.0
    seq_count = lax.axis_size("seq")
    cfg_count = lax.axis_size("cfg")
    spread = lax.all_to_all(qkv, ("seq", "cfg"), split_axis=3, concat_axis=0, tiled=True)
    columns = spread.shape[3]
    heads_here = columns // HD
    block = spread.reshape(seq_count, cfg_count, spread.shape[1], 3, columns)
    start_head = (lax.axis_index("seq") * cfg_count + lax.axis_index("cfg")) * heads_here
    head_windows = lax.dynamic_slice_in_dim(windows, start_head, heads_here, 0).reshape(
        1, heads_here
    )
    attended = attend(block, head_windows, seg_pad, first_frame)
    cond = attended[:, 0].astype(jnp.float32)
    uncond = attended[:, 1].astype(jnp.float32)
    guided = (uncond + strength * (cond - uncond)).astype(jnp.bfloat16)
    own_rows = lax.all_to_all(guided, "seq", split_axis=0, concat_axis=3, tiled=True)
    return own_rows[0]

LOG2E = 1.4426950408889634
MASKED = -1e30
UNROLLED_BLOCKS = 25
BF16 = jnp.bfloat16
F32 = jnp.float32
VMEM_BYTES = 32 * 1024 * 1024
PLAN_VMEM_BYTES = 60 * 1024 * 1024
SWAP = ((0, 1), (1, 0))
COSTS = {"pack": 1e10, "local": 3e9, "own": 3e9, "across": 3e9, "mix": 1e8, "gate": 1e9}
STEPS = {"O": 0, "X": 1, "NO": 2, "NR": -1, "FO": -2, "FR": 3}
OWN_SOURCES = ("FO", "NR", "O", "X", "NO")
ACROSS_SOURCES = ("NR", "O", "X", "NO", "FR")
DISTANCES = (2, 1, 0, 1, 2)


def whole(space=pltpu.VMEM):
    return pl.BlockSpec(memory_space=space)


def cost(kind):
    return pl.CostEstimate(flops=int(COSTS[kind]), bytes_accessed=1, transcendentals=0)


def params(limit=VMEM_BYTES):
    return pltpu.CompilerParams(vmem_limit_bytes=limit)


class Rows:
    def __init__(self, heads):
        self.strength = 0
        self.cond = 1
        self.own = 8
        self.across = self.own + heads // 2 * len(DISTANCES)
        self.size = self.across + heads // 2 * len(DISTANCES)


class Layout:
    def __init__(self, heads, outs):
        self.mine = 0
        self.theirs = heads // 2
        self.order = heads
        self.rank = 2 * heads
        self.reach = 3 * heads
        self.my_reach = 4 * heads
        self.pos = self.my_reach + heads // 2
        self.own_match = self.pos + outs
        self.across_match = self.own_match + len(DISTANCES)
        self.branch = self.across_match + len(DISTANCES)
        self.column = self.branch + 1
        self.step = self.column + 1
        self.size = self.step + 1


def plan_kernel(
    at, rungs, split, windows_in, segments_in, step_in, x_ref, plan_out, rung_out, kv_ref, own_ref,
    windows_ref, segments_ref, step_ref, plan_ref, rung_ref, in_sems, out_sems, sems,
):
    get_windows = pltpu.make_async_copy(windows_in, windows_ref, in_sems.at[0])
    get_segments = pltpu.make_async_copy(segments_in, segments_ref, in_sems.at[1])
    get_windows.start()
    get_segments.start()
    get_step = pltpu.make_async_copy(step_in, step_ref, in_sems.at[2])
    get_step.start()
    heads = windows_ref.shape[0]
    frames = segments_ref.shape[0]
    column, block, branch = (lax.axis_index(a).astype(jnp.int32) for a in ("seq", "frame", "cfg"))
    get_windows.wait()
    reach = [windows_ref[h] for h in range(heads)]
    wide = [(w >= 2).astype(jnp.int32) for w in reach]
    some = [(w >= 1).astype(jnp.int32) for w in reach]
    most = functools.reduce(lambda a, b: a + b, wide)
    many = functools.reduce(lambda a, b: a + b, some)
    next_wide, next_some, next_none = jnp.int32(0), most, many
    for h in range(heads):
        spot = jnp.where(wide[h] == 1, next_wide, jnp.where(some[h] == 1, next_some, next_none))
        next_wide = next_wide + wide[h]
        next_some = next_some + some[h] - wide[h]
        next_none = next_none + 1 - some[h]
        plan_ref[at.order + spot] = jnp.int32(h)
        plan_ref[at.rank + h] = spot
        plan_ref[at.reach + spot] = reach[h]
    copies = []
    for out_ref, side in ((kv_ref, 1 - column), (own_ref, column)):
        for j in range(out_ref.shape[0]):
            start = pl.multiple_of(plan_ref[at.order + 2 * j + side] * HD, HD)
            copies.append(
                pltpu.make_async_copy(
                    x_ref.at[1:3, :, pl.ds(start, HD)], out_ref.at[j], sems.at[len(copies)]
                )
            )
            copies[-1].start()
    for j in range(heads // 2):
        plan_ref[at.mine + j] = plan_ref[at.order + 2 * j + column]
        plan_ref[at.theirs + j] = plan_ref[at.order + 2 * j + 1 - column]
        plan_ref[at.my_reach + j] = plan_ref[at.reach + 2 * j + column]
    columns, cores = split
    per_half = heads // (columns * cores)
    for t in range(columns * per_half):
        head = (t // per_half) * (heads // columns) + branch * per_half + t % per_half
        plan_ref[at.pos + t] = plan_ref[at.rank + head]
    own_frame = 2 * block + column
    sign = 1 - 2 * column

    get_segments.wait()
    get_step.wait()
    plan_ref[at.step] = step_ref[0]

    def shot(name):
        frame = own_frame + STEPS[name] * sign
        inside = jnp.logical_and(frame >= 0, frame < frames)
        return jnp.where(inside, segments_ref[jnp.clip(frame, 0, frames - 1)], -1)

    for first, names, query in (
        (at.own_match, OWN_SOURCES, "O"),
        (at.across_match, ACROSS_SOURCES, "X"),
    ):
        for k, name in enumerate(names):
            plan_ref[first + k] = (shot(name) == shot(query)).astype(jnp.int32)
    plan_ref[at.branch] = branch
    plan_ref[at.column] = column
    index = jnp.int32(len(rungs) - 1)
    for k in reversed(range(len(rungs) - 1)):
        fits = jnp.logical_and(many <= rungs[k][0], most <= rungs[k][1])
        index = jnp.where(fits, jnp.int32(k), index)
    rung_ref[0] = index
    for k, (ref, out) in enumerate(((plan_ref, plan_out), (rung_ref, rung_out))):
        copies.append(pltpu.make_async_copy(ref, out, out_sems.at[k]))
        copies[-1].start()
    for copy in copies:
        copy.wait()


def pack_kernel(jobs, count_in, plan_ref, x_ref, *refs):
    outs, sems = refs[count_in:-1], refs[-1]
    copies = []
    for out_ref, (spots, first, last) in zip(outs, jobs):
        for j, spot in enumerate(spots):
            start = pl.multiple_of(plan_ref[spot] * HD, HD)
            copies.append(
                pltpu.make_async_copy(
                    x_ref.at[first:last, :, pl.ds(start, HD)],
                    out_ref.at[j],
                    sems.at[len(copies)],
                )
            )
    for copy in copies:
        copy.start()
    for copy in copies:
        copy.wait()


def pack(plan, x3, jobs, after):
    rows = x3.shape[1]
    return pl.pallas_call(
        functools.partial(pack_kernel, jobs, len(after)),
        out_shape=[
            jax.ShapeDtypeStruct((len(spots), last - first, rows, HD), x3.dtype)
            for spots, first, last in jobs
        ],
        in_specs=[whole(pltpu.SMEM)] + [whole(pl.ANY)] * (1 + len(after)),
        out_specs=[whole(pl.ANY)] * len(jobs),
        scratch_shapes=[pltpu.SemaphoreType.DMA((sum(len(spots) for spots, _, _ in jobs),))],
        compiler_params=params(),
        cost_estimate=cost("pack"),
        name="pack_heads",
    )(plan, x3, *after)


def gate_kernel(*refs):
    del refs


def gate(values, after):
    count = len(values)
    return pl.pallas_call(
        gate_kernel,
        out_shape=[jax.ShapeDtypeStruct(v.shape, v.dtype) for v in values],
        in_specs=[whole(pl.ANY)] * (count + len(after)),
        out_specs=[whole(pl.ANY)] * count,
        input_output_aliases={i: i for i in range(count)},
        compiler_params=params(),
        cost_estimate=cost("gate"),
        name="gate",
    )(*values, *after)


def softmax_mix(q, keys, values, biases):
    factor = LOG2E / math.sqrt(HD)
    scores = []
    for key, bias in zip(keys, biases):
        score = lax.dot_general(q, key, (((1,), (1,)), ((), ())), preferred_element_type=F32)
        scores.append(score if bias is None else score + bias)
    top = jnp.max(functools.reduce(jnp.maximum, scores), axis=1, keepdims=True)
    expd = [jnp.exp2((score - top) * factor) for score in scores]
    total = jnp.sum(functools.reduce(jnp.add, expd), axis=1, keepdims=True)
    mixed = functools.reduce(
        jnp.add,
        [
            jnp.dot(e.astype(BF16), value, preferred_element_type=F32)
            for e, value in zip(expd, values)
        ],
    )
    return mixed / total


def table_kernel(at, rows_at, plan_ref, *refs):
    table_ref = refs[-1]
    width = table_ref.shape[1]

    def put(row, value):
        table_ref[row : row + 1, :] = jnp.full((1, width), value, F32)

    step = jnp.full((1, width), plan_ref[at.step], jnp.int32).astype(F32)
    table_ref[rows_at.strength : rows_at.strength + 1, :] = 1.0 + 4.0 * step / 999.0
    put(rows_at.cond, jnp.where(plan_ref[at.branch] == 0, 1.0, 0.0).astype(F32))
    for first, match_at in ((rows_at.own, at.own_match), (rows_at.across, at.across_match)):
        for slot in range((rows_at.across - rows_at.own) // len(DISTANCES)):
            reach = plan_ref[at.my_reach + slot]
            for k, distance in enumerate(DISTANCES):
                seen = jnp.logical_and(reach >= distance, plan_ref[match_at + k] != 0)
                put(
                    first + slot * len(DISTANCES) + k, jnp.where(seen, 0.0, MASKED).astype(F32)
                )


def make_table(plan, at, rows_at, width, after):
    return pl.pallas_call(
        functools.partial(table_kernel, at, rows_at),
        out_shape=jax.ShapeDtypeStruct((rows_at.size, width), F32),
        in_specs=[whole(pltpu.SMEM)] + [whole(pl.ANY)] * len(after),
        out_specs=whole(),
        compiler_params=params(),
        cost_estimate=cost("mix"),
        name="table",
    )(plan, *after)


def local_kernel(count, heads_at, plan_ref, x_ref, *refs):
    out_ref, held, sems = refs[-3:]
    copies = []
    for j in range(count):
        start = pl.multiple_of(plan_ref[heads_at + j] * HD, HD)
        copies.append(
            pltpu.make_async_copy(x_ref.at[:, :, pl.ds(start, HD)], held.at[j], sems.at[j])
        )
        copies[-1].start()
    for copy in copies:
        copy.wait()
    for j in range(count):
        out_ref[j] = softmax_mix(held[j, 0], [held[j, 1]], [held[j, 2]], [None]).astype(BF16)


def attend_local(plan, x3, heads_at, count, after):
    planes, rows, _ = x3.shape
    return pl.pallas_call(
        functools.partial(local_kernel, count, heads_at),
        out_shape=jax.ShapeDtypeStruct((count, rows, HD), BF16),
        in_specs=[whole(pltpu.SMEM)] + [whole(pl.ANY)] * (1 + len(after)),
        out_specs=whole(),
        scratch_shapes=[
            pltpu.VMEM((count, planes, rows, HD), BF16),
            pltpu.SemaphoreType.DMA((count,)),
        ],
        compiler_params=params(),
        cost_estimate=cost("local"),
        name="attend_local",
    )(plan, x3, *after)


def attend_kernel(count, q_offset, offsets, bias_at, cond_at, table_ref, q_ref, *refs):
    sources = len(offsets)
    kv_refs = refs[:sources]
    halves = cond_at is not None
    outs = refs[-2:] if halves else refs[-1:]

    def one(j):
        keys = [ref[o + j, 0] for ref, o in zip(kv_refs, offsets)]
        values = [ref[o + j, 1] for ref, o in zip(kv_refs, offsets)]
        first = bias_at + j * len(DISTANCES)
        biases = [table_ref[pl.ds(first + k, 1), :] for k in range(sources)]
        out = softmax_mix(q_ref[q_offset + j, 0], keys, values, biases)
        if halves:
            half = out.shape[0] // 2
            low, high = out[:half], out[half:]
            is_first = table_ref[cond_at : cond_at + 1, :HD] > 0.0
            outs[0][j] = jnp.where(is_first, low, high).astype(BF16)
            outs[1][j] = jnp.where(is_first, high, low).astype(BF16)
        else:
            outs[0][j] = out.astype(BF16)

    pairs = 0 if count * sources <= UNROLLED_BLOCKS else count // 2

    def two(i, carry):
        one(2 * i)
        one(2 * i + 1)
        return carry

    if pairs:
        lax.fori_loop(0, pairs, two, 0)
    for j in range(2 * pairs, count):
        one(j)


def attend_slots(table, q, q_offset, sources, count, bias_at, cond_at, after):
    rows = q.shape[-2]
    if cond_at is None:
        out_shape = jax.ShapeDtypeStruct((count, rows, HD), BF16)
        out_specs = whole()
    else:
        out_shape = [jax.ShapeDtypeStruct((count, rows // 2, HD), BF16)] * 2
        out_specs = [whole()] * 2
    arrays = [array for array, _ in sources]
    offsets = [offset for _, offset in sources]
    return pl.pallas_call(
        functools.partial(attend_kernel, count, q_offset, offsets, bias_at, cond_at),
        out_shape=out_shape,
        in_specs=[whole()] * (2 + len(arrays)) + [whole(pl.ANY)] * len(after),
        out_specs=out_specs,
        compiler_params=params(),
        cost_estimate=cost("own" if cond_at is None else "across"),
        name="attend",
    )(table, q, *arrays, *after)


def blend(cond, uncond, strength):
    cond = cond.astype(F32)
    uncond = uncond.astype(F32)
    return (uncond + strength * (cond - uncond)).astype(BF16)


def mix_branches(rows_at, table_ref, mine, other):
    strength = table_ref[rows_at.strength : rows_at.strength + 1, :HD]
    is_cond = table_ref[rows_at.cond : rows_at.cond + 1, :HD] > 0.0
    mine = mine.astype(F32)
    other = other.astype(F32)
    return blend(jnp.where(is_cond, mine, other), jnp.where(is_cond, other, mine), strength)


def mix_kernel(rows_at, pieces, table_ref, mine_ref, *refs):
    out_ref = refs[-1]
    j = 0
    for other_ref in refs[:pieces]:
        for i in range(other_ref.shape[0]):
            out_ref[j] = mix_branches(rows_at, table_ref, mine_ref[j], other_ref[i])
            j += 1


def mix_cores(table, rows_at, mine, others, after):
    return pl.pallas_call(
        functools.partial(mix_kernel, rows_at, len(others)),
        out_shape=jax.ShapeDtypeStruct(mine.shape, mine.dtype),
        in_specs=[whole()] * (2 + len(others)) + [whole(pl.ANY)] * len(after),
        out_specs=whole(),
        compiler_params=params(),
        cost_estimate=cost("mix"),
        name="mix",
    )(table, mine, *others, *after)


def assemble_kernel(at, rows_at, sizes, slots, places, plan_in, table_ref, *refs):
    out_ref, plan_ref, listed, turned, plan_sem, out_sems = refs[-6:]
    get_plan = pltpu.make_async_copy(plan_in, plan_ref, plan_sem.at[0])
    get_plan.start()
    own_count, raw_count, cross_count = sizes
    refs = list(refs[:-6])

    def take(count):
        taken = refs[:count]
        del refs[:count]
        return taken

    own, raw, raw_other = take(own_count), take(raw_count), take(raw_count)
    kept, moved, local = take(cross_count), take(cross_count), refs
    for ref, first in zip(own, places[0]):
        for j in range(ref.shape[0]):
            listed[first + j] = ref[j]
    for ref in local:
        for j in range(ref.shape[0]):
            listed[2 * slots + j] = ref[j]
    for ref, other, first in zip(raw, raw_other, places[1]):
        for j in range(ref.shape[0]):
            listed[first + j] = mix_branches(rows_at, table_ref, ref[j], other[j])
    low_here = table_ref[rows_at.cond : rows_at.cond + 1, :HD] > 0.0
    for ref, other, first in zip(kept, moved, places[2]):
        half = ref.shape[1]
        for j in range(ref.shape[0]):
            mine, theirs = ref[j].astype(F32), other[j].astype(F32)
            low = jnp.where(low_here, mine, theirs).astype(BF16)
            high = jnp.where(low_here, theirs, mine).astype(BF16)
            listed[slots + first + j, :half] = low
            listed[slots + first + j, half:] = high
    get_plan.wait()
    column = plan_ref[at.column]
    per_half = turned.shape[1]
    count = turned.shape[2] // HD * per_half
    spots = []
    for t in range(count):
        p = plan_ref[at.pos + t]
        slot = lax.shift_right_logical(p, 1)
        paired = jnp.where(jnp.bitwise_and(p, 1) == column, slot, slots + slot)
        spots.append(jnp.where(p >= 2 * slots, p, paired))
    parts = 2
    size = turned.shape[0] // parts
    copies = []
    for r in range(parts):
        tokens = slice(r * size, (r + 1) * size)
        for s in range(count // per_half):
            picked = [listed[spots[s * per_half + a], tokens] for a in range(per_half)]
            turned[tokens, :, s * HD : (s + 1) * HD] = jnp.swapaxes(jnp.stack(picked), 0, 1)
        copies.append(
            pltpu.make_async_copy(turned.at[tokens], out_ref.at[tokens], out_sems.at[r])
        )
        copies[-1].start()
    for copy in copies:
        copy.wait()


def ranked_body(rungs, qkv, timestep, windows, segments):
    rows = qkv.shape[1]
    heads = windows.shape[0]
    seq_count = lax.axis_size("seq")
    frame_count = lax.axis_size("frame")
    cfg_count = lax.axis_size("cfg")
    per_half = heads // (seq_count * cfg_count)
    outs = seq_count * per_half
    at = Layout(heads, outs)
    rows_at = Rows(heads)
    x3 = jnp.transpose(qkv[0], (1, 0, 2))
    lead, base = rungs[0][1] // 2, rungs[0][0] // 2
    plan, rung, kv_lead, kv_base = pl.pallas_call(
        functools.partial(plan_kernel, at, rungs, (seq_count, cfg_count)),
        out_shape=[
            jax.ShapeDtypeStruct((at.size,), jnp.int32),
            jax.ShapeDtypeStruct((1,), jnp.int32),
            jax.ShapeDtypeStruct((lead, 2, rows, HD), BF16),
            jax.ShapeDtypeStruct((base, 2, rows, HD), BF16),
        ],
        in_specs=[whole(pltpu.HBM)] * 3 + [whole(pl.ANY)],
        out_specs=[whole(pl.ANY)] * 4,
        scratch_shapes=[
            pltpu.SMEM(windows.shape, jnp.int32),
            pltpu.SMEM(segments.shape, jnp.int32),
            pltpu.SMEM(timestep.shape, jnp.int32),
            pltpu.SMEM((at.size,), jnp.int32),
            pltpu.SMEM((1,), jnp.int32),
            pltpu.SemaphoreType.DMA((3,)),
            pltpu.SemaphoreType.DMA((2,)),
            pltpu.SemaphoreType.DMA((lead + base,)),
        ],
        compiler_params=params(PLAN_VMEM_BYTES),
        name="plan",
    )(windows, segments, timestep, x3)

    grid_axes = ("seq", "frame")
    last = frame_count - 1
    apart = [(i, i - 1) for i in range(1, frame_count)] + [
        (frame_count + i, frame_count + i + 1) for i in range(last)
    ]
    onward = [(i, i + 1) for i in range(last)] + [
        (frame_count + i, frame_count + i - 1) for i in range(1, frame_count)
    ]

    def attempt(rung, plan, x3, kv_lead, kv_base):
        exchanged, wide = rung
        slots, far = exchanged // 2, wide // 2
        local = heads - exchanged
        bounds = [(0, lead), (lead, base)]
        if slots > base:
            bounds.append((base, slots))
        chunks = range(len(bounds))
        reaches = [far >= hi for _, hi in bounds]

        def cross(a):
            return lax.ppermute(a, "seq", SWAP)

        def mate(a):
            return lax.ppermute(a, "cfg", SWAP)

        def mix(mine, others, after):
            return mix_cores(table, rows_at, mine, others, after)

        across = [cross(kv_lead)]
        near_base = lax.ppermute(kv_base, grid_axes, apart)
        (kv_far,) = pack(plan, x3, [(range(at.mine, at.mine + lead), 1, 3)], [kv_base])
        far_own = [lax.ppermute(kv_far, grid_axes, onward)]
        split = base
        cut = 0
        parts = [(lead, split, 1), (split, base, 1)]
        parts += [(lo, hi, k) for k, (lo, hi) in enumerate(bounds) if k > 1]
        parts += [(0, cut, 0), (cut, lead, 0)]
        parts = [(lo, hi, k) for lo, hi, k in parts if hi > lo]
        later = [slot for lo, hi, _ in parts[1:] for slot in range(lo, hi)]
        jobs = [
            ([at.theirs + slot for slot in slots_of], 0, 1)
            for slots_of in (range(lead, split), later)
        ]
        jobs += [(range(at.theirs + lo, at.theirs + hi), 1, 3) for lo, hi in bounds[1:]]
        jobs += [(range(at.mine + lo, at.mine + hi), 1, 3) for lo, hi in bounds[2:]]
        jobs += [(range(at.mine + lead, at.mine + far), 1, 3)] if far > lead else []
        jobs.insert(0, (range(at.mine, at.mine + slots), 0, 1))
        q_own, q_early, q_late, *rest = pack(plan, x3, jobs, [kv_far])
        across += [cross(a) for a in rest[: len(bounds) - 1]]
        more = rest[len(bounds) - 1 :]
        if far > lead:
            far_own.append(lax.ppermute(more.pop(), grid_axes, onward))
        kv_more = more
        near_more = [lax.ppermute(a, grid_axes, apart) for a in kv_more]
        table = make_table(plan, at, rows_at, rows, [rest[0]])
        done = [table]
        if local:
            own_local = attend_local(plan, x3, at.order + exchanged, local, done)
            peer_local = mate(own_local)
            done = [own_local]

        near_across, far_across, guided = {}, {}, []
        (across[0],) = gate([across[0]], done)
        near_across[0] = lax.ppermute(across[0], grid_axes, onward)
        (q_early,) = gate([q_early], [across[0], *far_own])
        done = [q_early]
        q_early = cross(q_early)
        if local:
            guided = [mix(own_local, [peer_local], done)]
            done = guided
        (late,) = gate([across[0]], done)
        far_across[0] = lax.ppermute(late, grid_axes, apart)
        (across[1],) = gate([across[1]], [late, *done])
        (q_late,) = gate([q_late], [across[1]])
        done = [near_across[0], q_late]
        q_late = cross(q_late)
        for k in chunks[1:]:
            (across[k],) = gate([across[k]], done)
            done = [across[k]]
            near_across[k] = lax.ppermute(across[k], grid_axes, onward)
            if reaches[k]:
                far_across[k] = lax.ppermute(across[k], grid_axes, apart)

        def attend_part(k, lo, hi, q, q_offset, names, bias_at, cond_at, after):
            skip = lo - bounds[k][0]
            arrays = {
                "O": (kv_more[0], skip) if k > 1 else (kv_base, lo),
                "X": (across[k], skip),
                "NO": (near_more[0], skip) if k > 1 else (near_base, lo),
                "NR": (near_across[k], skip),
                "FO": (far_own[min(k, 1)], max(lo - lead, 0)) if reaches[k] else None,
                "FR": (far_across.get(k), skip),
            }
            cut = slice(0, 5) if reaches[k] else slice(1, 4)
            sources = [arrays[name] for name in names[cut]]
            bias_at += lo * len(DISTANCES) + cut.start
            return attend_slots(table, q, q_offset, sources, hi - lo, bias_at, cond_at, after)

        def attend_own(k, after):
            lo, hi = bounds[k]
            return attend_part(k, lo, hi, q_own, lo, OWN_SOURCES, rows_at.own, None, after)

        def attend_across(part, after):
            lo, hi, k = parts[part]
            q = q_late if part else q_early
            offset = later.index(lo) if part else 0
            return attend_part(
                k, lo, hi, q, offset, ACROSS_SOURCES, rows_at.across, rows_at.cond, after
            )

        own, kept = {}, []
        own[0] = attend_own(0, done)
        keep, send = attend_across(0, [own[0]])
        got = mate(send)
        end = mix(own[0], [mate(own[0])], [keep])
        mixed = mix(keep, [got], [end])
        kept.append(cross(mixed))
        waiting = []
        done = [mixed]
        for part in range(1, len(parts)):
            keep, send = attend_across(part, done)
            middle = send.shape[0] // 2
            pieces = [send] if part < len(parts) - 1 else [send[:middle], send[middle:]]
            waiting.append((keep, [mate(piece) for piece in pieces]))
            done = [keep]
        done.append(kept[0])
        for keep, got in waiting:
            mixed = mix(keep, got, done)
            kept.append(cross(mixed))
            done = [mixed]
        raw = []
        for k in chunks[1:]:
            lo, hi = bounds[k]
            own[k] = attend_own(k, [mixed, kept[0]])
            middle = (hi - lo) // 2
            raw += [(lo, own[k][:middle]), (lo + middle, own[k][middle:])]
        others = [mate(a) for _, a in raw]
        arrays = [end, *[a for _, a in raw], *others, *kept, *[mate(a) for a in kept], *guided]
        places = ([0], [lo for lo, _ in raw], [lo for lo, _, _ in parts])
        sizes = tuple(len(firsts) for firsts in places)
        return pl.pallas_call(
            functools.partial(assemble_kernel, at, rows_at, sizes, slots, places),
            out_shape=pltpu.HBM((rows, per_half, seq_count * HD), BF16),
            in_specs=[whole(pl.ANY)] + [whole()] * (1 + len(arrays)),
            out_specs=whole(pltpu.HBM),
            scratch_shapes=[
                pltpu.SMEM(plan.shape, plan.dtype),
                pltpu.VMEM((heads, rows, HD), BF16),
                pltpu.VMEM((rows, per_half, seq_count * HD), BF16),
                pltpu.SemaphoreType.DMA((1,)),
                pltpu.SemaphoreType.DMA((2,)),
            ],
            compiler_params=params(),
            name="assemble",
        )(plan, table, *arrays)

    return lax.switch(
        rung[0],
        [functools.partial(attempt, rung) for rung in rungs],
        plan, x3, kv_lead, kv_base,
    )


def rungs_of(heads):
    third = heads // 3
    return ((2 * third + 2, third), (2 * third + 2, 2 * third + 2), (heads, heads))


def solution(mesh):
    sizes = dict(mesh.shape)

    def whole_body(qkv, timestep, windows, segments):
        frames_here = segments.shape[0] // sizes["frame"]
        one_frame = frames_here == sizes["seq"]
        if sizes["seq"] == 2 and sizes["cfg"] == 2 and one_frame and qkv.shape[1] % 32 == 0:
            return ranked_body(rungs_of(windows.shape[0]), qkv, timestep, windows, segments)
        return body(qkv, timestep, windows, segments)

    return jax.shard_map(
        whole_body,
        mesh=mesh,
        in_specs=(P("cfg", ("groups", "frame", "seq"), None, None), P("groups"), P(), P("groups")),
        out_specs=P(("groups", "frame", "seq"), "cfg", None),
        check_vma=False,
    )
```

```python
import functools
import math

import jax
import jax.numpy as jnp
from jax import lax
from jax.experimental import pallas as pl
from jax.experimental.pallas import tpu as pltpu
from jax.sharding import PartitionSpec as P

HD = 128
F_DEV = 2
W_MAX = 2


def padded_2(block, sides, width):
    for axis, dim in sides:
        count = lax.axis_size(axis)
        forward = [(i, i + 1) for i in range(count - 1)]
        backward = [(target, source) for source, target in forward]
        low = lax.ppermute(
            lax.slice_in_dim(block, block.shape[dim] - width, None, axis=dim), axis, forward
        )
        high = lax.ppermute(lax.slice_in_dim(block, 0, width, axis=dim), axis, backward)
        block = jnp.concatenate([low, block, high], axis=dim)
    return block


def attend(block, head_windows, seg_pad, first_frame):
    count_blocks = block.shape[0]
    branches = block.shape[1]
    rows_block = block.shape[2]
    columns = block.shape[4]
    heads_here = columns // HD
    per_frame = count_blocks // F_DEV
    reach = W_MAX * per_frame
    span = 2 * W_MAX + 1
    scale = 1.0 / math.sqrt(HD)
    pairs = block[:, :, :, 1:]
    padded = padded_2(pairs, (("frame", 0),), reach)
    queries = block[:, :, :, 0].reshape(count_blocks, branches, rows_block, heads_here, HD)
    offsets = jnp.arange(span, dtype=jnp.int32) - W_MAX
    within_reach = jnp.abs(offsets)[None, None, :] <= head_windows[:, :, None]
    results = []
    for frame_number in range(F_DEV):
        query = queries[frame_number * per_frame : (frame_number + 1) * per_frame]
        window_rows = padded[frame_number * per_frame : frame_number * per_frame + span * per_frame]
        window_rows = window_rows.reshape(span * per_frame, branches, rows_block, 2, heads_here, HD)
        key_rows = window_rows[:, :, :, 0]
        value_rows = window_rows[:, :, :, 1]
        here = first_frame + frame_number
        shots = lax.dynamic_slice_in_dim(seg_pad, here, span, 0)
        own_shot = lax.dynamic_index_in_dim(seg_pad, here + W_MAX, 0, keepdims=False)
        allowed = within_reach & (shots == own_shot)[None, None, :]
        allowed = jnp.repeat(allowed, per_frame, axis=2)
        scores = (
            jnp.einsum("sbthd,ubrhd->bhstur", query, key_rows, preferred_element_type=jnp.float32)
            * scale
        )
        scores = jnp.where(allowed[:, :, None, None, :, None], scores, -1e30)
        highest = jnp.max(scores, axis=(4, 5), keepdims=True)
        expd = jnp.exp(scores - highest)
        totals = jnp.sum(expd, axis=(4, 5))
        weights = expd.astype(jnp.bfloat16)
        mixed = jnp.einsum(
            "bhstur,ubrhd->sbthd", weights, value_rows, preferred_element_type=jnp.float32
        )
        mixed = mixed / jnp.transpose(totals, (2, 0, 3, 1))[..., None]
        results.append(mixed.astype(jnp.bfloat16))
    return jnp.concatenate(results, axis=0)


def body(qkv, timestep, windows, segments):
    first_frame = lax.axis_index("frame") * F_DEV
    fill = jnp.full((W_MAX,), -1, jnp.int32)
    seg_pad = jnp.concatenate([fill, segments, fill])
    strength = 1.0 + 4.0 * timestep[0].astype(jnp.float32) / 999.0
    seq_count = lax.axis_size("seq")
    cfg_count = lax.axis_size("cfg")
    spread = lax.all_to_all(qkv, ("seq", "cfg"), split_axis=3, concat_axis=0, tiled=True)
    columns = spread.shape[3]
    heads_here = columns // HD
    block = spread.reshape(seq_count, cfg_count, spread.shape[1], 3, columns)
    start_head = (lax.axis_index("seq") * cfg_count + lax.axis_index("cfg")) * heads_here
    head_windows = lax.dynamic_slice_in_dim(windows, start_head, heads_here, 0).reshape(
        1, heads_here
    )
    attended = attend(block, head_windows, seg_pad, first_frame)
    cond = attended[:, 0].astype(jnp.float32)
    uncond = attended[:, 1].astype(jnp.float32)
    guided = (uncond + strength * (cond - uncond)).astype(jnp.bfloat16)
    own_rows = lax.all_to_all(guided, "seq", split_axis=0, concat_axis=3, tiled=True)
    return own_rows[0]

LOG2E = 1.4426950408889634
MASKED = -1e30
UNROLLED_BLOCKS = 25
BF16 = jnp.bfloat16
F32 = jnp.float32
VMEM_BYTES = 32 * 1024 * 1024
PLAN_VMEM_BYTES = 60 * 1024 * 1024
SWAP = ((0, 1), (1, 0))
COSTS = {"pack": 1e10, "local": 3e9, "own": 3e9, "across": 3e9, "mix": 1e8, "gate": 1e9}
STEPS = {"O": 0, "X": 1, "NO": 2, "NR": -1, "FO": -2, "FR": 3}
OWN_SOURCES = ("FO", "NR", "O", "X", "NO")
ACROSS_SOURCES = ("NR", "O", "X", "NO", "FR")
DISTANCES = (2, 1, 0, 1, 2)


def whole(space=pltpu.VMEM):
    return pl.BlockSpec(memory_space=space)


def cost(kind):
    return pl.CostEstimate(flops=int(COSTS[kind]), bytes_accessed=1, transcendentals=0)


def params(limit=VMEM_BYTES):
    return pltpu.CompilerParams(vmem_limit_bytes=limit)


class Rows:
    def __init__(self, heads):
        self.strength = 0
        self.cond = 1
        self.own = 8
        self.across = self.own + heads // 2 * len(DISTANCES)
        self.size = self.across + heads // 2 * len(DISTANCES)


class Layout:
    def __init__(self, heads, outs):
        self.mine = 0
        self.theirs = heads // 2
        self.order = heads
        self.rank = 2 * heads
        self.reach = 3 * heads
        self.my_reach = 4 * heads
        self.pos = self.my_reach + heads // 2
        self.own_match = self.pos + outs
        self.across_match = self.own_match + len(DISTANCES)
        self.branch = self.across_match + len(DISTANCES)
        self.column = self.branch + 1
        self.step = self.column + 1
        self.size = self.step + 1


def plan_kernel(
    at, rungs, split, windows_in, segments_in, step_in, x_ref, plan_out, rung_out, kv_ref, own_ref,
    windows_ref, segments_ref, step_ref, plan_ref, rung_ref, in_sems, out_sems, sems,
):
    get_windows = pltpu.make_async_copy(windows_in, windows_ref, in_sems.at[0])
    get_segments = pltpu.make_async_copy(segments_in, segments_ref, in_sems.at[1])
    get_windows.start()
    get_segments.start()
    get_step = pltpu.make_async_copy(step_in, step_ref, in_sems.at[2])
    get_step.start()
    heads = windows_ref.shape[0]
    frames = segments_ref.shape[0]
    column, block, branch = (lax.axis_index(a).astype(jnp.int32) for a in ("seq", "frame", "cfg"))
    get_windows.wait()
    reach = [windows_ref[h] for h in range(heads)]
    wide = [(w >= 2).astype(jnp.int32) for w in reach]
    some = [(w >= 1).astype(jnp.int32) for w in reach]
    most = functools.reduce(lambda a, b: a + b, wide)
    many = functools.reduce(lambda a, b: a + b, some)
    next_wide, next_some, next_none = jnp.int32(0), most, many
    for h in range(heads):
        spot = jnp.where(wide[h] == 1, next_wide, jnp.where(some[h] == 1, next_some, next_none))
        next_wide = next_wide + wide[h]
        next_some = next_some + some[h] - wide[h]
        next_none = next_none + 1 - some[h]
        plan_ref[at.order + spot] = jnp.int32(h)
        plan_ref[at.rank + h] = spot
        plan_ref[at.reach + spot] = reach[h]
    copies = []
    for out_ref, side in ((kv_ref, 1 - column), (own_ref, column)):
        for j in range(out_ref.shape[0]):
            start = pl.multiple_of(plan_ref[at.order + 2 * j + side] * HD, HD)
            copies.append(
                pltpu.make_async_copy(
                    x_ref.at[1:3, :, pl.ds(start, HD)], out_ref.at[j], sems.at[len(copies)]
                )
            )
            copies[-1].start()
    for j in range(heads // 2):
        plan_ref[at.mine + j] = plan_ref[at.order + 2 * j + column]
        plan_ref[at.theirs + j] = plan_ref[at.order + 2 * j + 1 - column]
        plan_ref[at.my_reach + j] = plan_ref[at.reach + 2 * j + column]
    columns, cores = split
    per_half = heads // (columns * cores)
    for t in range(columns * per_half):
        head = (t // per_half) * (heads // columns) + branch * per_half + t % per_half
        plan_ref[at.pos + t] = plan_ref[at.rank + head]
    own_frame = 2 * block + column
    sign = 1 - 2 * column

    get_segments.wait()
    get_step.wait()
    plan_ref[at.step] = step_ref[0]

    def shot(name):
        frame = own_frame + STEPS[name] * sign
        inside = jnp.logical_and(frame >= 0, frame < frames)
        return jnp.where(inside, segments_ref[jnp.clip(frame, 0, frames - 1)], -1)

    for first, names, query in (
        (at.own_match, OWN_SOURCES, "O"),
        (at.across_match, ACROSS_SOURCES, "X"),
    ):
        for k, name in enumerate(names):
            plan_ref[first + k] = (shot(name) == shot(query)).astype(jnp.int32)
    plan_ref[at.branch] = branch
    plan_ref[at.column] = column
    index = jnp.int32(len(rungs) - 1)
    for k in reversed(range(len(rungs) - 1)):
        fits = jnp.logical_and(many <= rungs[k][0], most <= rungs[k][1])
        index = jnp.where(fits, jnp.int32(k), index)
    rung_ref[0] = index
    for k, (ref, out) in enumerate(((plan_ref, plan_out), (rung_ref, rung_out))):
        copies.append(pltpu.make_async_copy(ref, out, out_sems.at[k]))
        copies[-1].start()
    for copy in copies:
        copy.wait()


def pack_kernel(jobs, count_in, plan_ref, x_ref, *refs):
    outs, sems = refs[count_in:-1], refs[-1]
    copies = []
    for out_ref, (spots, first, last) in zip(outs, jobs):
        for j, spot in enumerate(spots):
            start = pl.multiple_of(plan_ref[spot] * HD, HD)
            copies.append(
                pltpu.make_async_copy(
                    x_ref.at[first:last, :, pl.ds(start, HD)],
                    out_ref.at[j],
                    sems.at[len(copies)],
                )
            )
    for copy in copies:
        copy.start()
    for copy in copies:
        copy.wait()


def pack(plan, x3, jobs, after):
    rows = x3.shape[1]
    return pl.pallas_call(
        functools.partial(pack_kernel, jobs, len(after)),
        out_shape=[
            jax.ShapeDtypeStruct((len(spots), last - first, rows, HD), x3.dtype)
            for spots, first, last in jobs
        ],
        in_specs=[whole(pltpu.SMEM)] + [whole(pl.ANY)] * (1 + len(after)),
        out_specs=[whole()] * len(jobs),
        scratch_shapes=[pltpu.SemaphoreType.DMA((sum(len(spots) for spots, _, _ in jobs),))],
        compiler_params=params(),
        cost_estimate=cost("pack"),
        name="pack_heads",
    )(plan, x3, *after)


def gate_kernel(*refs):
    del refs


def gate(values, after):
    count = len(values)
    return pl.pallas_call(
        gate_kernel,
        out_shape=[jax.ShapeDtypeStruct(v.shape, v.dtype) for v in values],
        in_specs=[whole(pl.ANY)] * (count + len(after)),
        out_specs=[whole(pl.ANY)] * count,
        input_output_aliases={i: i for i in range(count)},
        compiler_params=params(),
        cost_estimate=cost("gate"),
        name="gate",
    )(*values, *after)


def softmax_mix(q, keys, values, biases):
    factor = LOG2E / math.sqrt(HD)
    scores = []
    for key, bias in zip(keys, biases):
        score = lax.dot_general(q, key, (((1,), (1,)), ((), ())), preferred_element_type=F32)
        scores.append(score if bias is None else score + bias)
    top = jnp.max(functools.reduce(jnp.maximum, scores), axis=1, keepdims=True)
    expd = [jnp.exp2((score - top) * factor) for score in scores]
    total = jnp.sum(functools.reduce(jnp.add, expd), axis=1, keepdims=True)
    mixed = functools.reduce(
        jnp.add,
        [
            jnp.dot(e.astype(BF16), value, preferred_element_type=F32)
            for e, value in zip(expd, values)
        ],
    )
    return mixed / total


def table_kernel(at, rows_at, plan_ref, *refs):
    table_ref = refs[-1]
    width = table_ref.shape[1]

    def put(row, value):
        table_ref[row : row + 1, :] = jnp.full((1, width), value, F32)

    step = jnp.full((1, width), plan_ref[at.step], jnp.int32).astype(F32)
    table_ref[rows_at.strength : rows_at.strength + 1, :] = 1.0 + 4.0 * step / 999.0
    put(rows_at.cond, jnp.where(plan_ref[at.branch] == 0, 1.0, 0.0).astype(F32))
    for first, match_at in ((rows_at.own, at.own_match), (rows_at.across, at.across_match)):
        for slot in range((rows_at.across - rows_at.own) // len(DISTANCES)):
            reach = plan_ref[at.my_reach + slot]
            for k, distance in enumerate(DISTANCES):
                seen = jnp.logical_and(reach >= distance, plan_ref[match_at + k] != 0)
                put(
                    first + slot * len(DISTANCES) + k, jnp.where(seen, 0.0, MASKED).astype(F32)
                )


def make_table(plan, at, rows_at, width, after):
    return pl.pallas_call(
        functools.partial(table_kernel, at, rows_at),
        out_shape=jax.ShapeDtypeStruct((rows_at.size, width), F32),
        in_specs=[whole(pltpu.SMEM)] + [whole(pl.ANY)] * len(after),
        out_specs=whole(),
        compiler_params=params(),
        cost_estimate=cost("mix"),
        name="table",
    )(plan, *after)


def local_kernel(count, heads_at, plan_ref, x_ref, *refs):
    out_ref, held, sems = refs[-3:]
    copies = []
    for j in range(count):
        start = pl.multiple_of(plan_ref[heads_at + j] * HD, HD)
        copies.append(
            pltpu.make_async_copy(x_ref.at[:, :, pl.ds(start, HD)], held.at[j], sems.at[j])
        )
        copies[-1].start()
    for copy in copies:
        copy.wait()
    for j in range(count):
        out_ref[j] = softmax_mix(held[j, 0], [held[j, 1]], [held[j, 2]], [None]).astype(BF16)


def attend_local(plan, x3, heads_at, count, after):
    planes, rows, _ = x3.shape
    return pl.pallas_call(
        functools.partial(local_kernel, count, heads_at),
        out_shape=jax.ShapeDtypeStruct((count, rows, HD), BF16),
        in_specs=[whole(pltpu.SMEM)] + [whole(pl.ANY)] * (1 + len(after)),
        out_specs=whole(),
        scratch_shapes=[
            pltpu.VMEM((count, planes, rows, HD), BF16),
            pltpu.SemaphoreType.DMA((count,)),
        ],
        compiler_params=params(),
        cost_estimate=cost("local"),
        name="attend_local",
    )(plan, x3, *after)


def attend_kernel(count, q_offset, offsets, always, bias_at, cond_at, table_ref, q_ref, *refs):
    sources = len(offsets)
    kv_refs = refs[:sources]
    halves = cond_at is not None
    outs = refs[-2:] if halves else refs[-1:]

    def one(j):
        keys = [ref[o + j, 0] for ref, o in zip(kv_refs, offsets)]
        values = [ref[o + j, 1] for ref, o in zip(kv_refs, offsets)]
        first = bias_at + j * len(DISTANCES)
        biases = [
            None if k == always else table_ref[pl.ds(first + k, 1), :] for k in range(sources)
        ]
        out = softmax_mix(q_ref[q_offset + j, 0], keys, values, biases)
        if halves:
            half = out.shape[0] // 2
            low, high = out[:half], out[half:]
            is_first = table_ref[cond_at : cond_at + 1, :HD] > 0.0
            outs[0][j] = jnp.where(is_first, low, high).astype(BF16)
            outs[1][j] = jnp.where(is_first, high, low).astype(BF16)
        else:
            outs[0][j] = out.astype(BF16)

    pairs = 0 if count * sources <= UNROLLED_BLOCKS else count // 2

    def two(i, carry):
        one(2 * i)
        one(2 * i + 1)
        return carry

    if pairs:
        lax.fori_loop(0, pairs, two, 0)
    for j in range(2 * pairs, count):
        one(j)


def attend_slots(table, q, q_offset, sources, always, count, bias_at, cond_at, after):
    rows = q.shape[-2]
    if cond_at is None:
        out_shape = jax.ShapeDtypeStruct((count, rows, HD), BF16)
        out_specs = whole()
    else:
        out_shape = [jax.ShapeDtypeStruct((count, rows // 2, HD), BF16)] * 2
        out_specs = [whole()] * 2
    arrays = [array for array, _ in sources]
    offsets = [offset for _, offset in sources]
    return pl.pallas_call(
        functools.partial(attend_kernel, count, q_offset, offsets, always, bias_at, cond_at),
        out_shape=out_shape,
        in_specs=[whole()] * (2 + len(arrays)) + [whole(pl.ANY)] * len(after),
        out_specs=out_specs,
        compiler_params=params(),
        cost_estimate=cost("own" if cond_at is None else "across"),
        name="attend",
    )(table, q, *arrays, *after)


def blend(cond, uncond, strength):
    cond = cond.astype(F32)
    uncond = uncond.astype(F32)
    return (uncond + strength * (cond - uncond)).astype(BF16)


def mix_branches(rows_at, table_ref, mine, other):
    strength = table_ref[rows_at.strength : rows_at.strength + 1, :HD]
    is_cond = table_ref[rows_at.cond : rows_at.cond + 1, :HD] > 0.0
    mine = mine.astype(F32)
    other = other.astype(F32)
    return blend(jnp.where(is_cond, mine, other), jnp.where(is_cond, other, mine), strength)


def mix_kernel(rows_at, pieces, table_ref, mine_ref, *refs):
    out_ref = refs[-1]
    j = 0
    for other_ref in refs[:pieces]:
        for i in range(other_ref.shape[0]):
            out_ref[j] = mix_branches(rows_at, table_ref, mine_ref[j], other_ref[i])
            j += 1


def mix_cores(table, rows_at, mine, others, after):
    return pl.pallas_call(
        functools.partial(mix_kernel, rows_at, len(others)),
        out_shape=jax.ShapeDtypeStruct(mine.shape, mine.dtype),
        in_specs=[whole()] * (2 + len(others)) + [whole(pl.ANY)] * len(after),
        out_specs=whole(),
        compiler_params=params(),
        cost_estimate=cost("mix"),
        name="mix",
    )(table, mine, *others, *after)


def assemble_kernel(at, rows_at, sizes, slots, places, plan_in, table_ref, *refs):
    out_ref, plan_ref, listed, turned, plan_sem, out_sems = refs[-6:]
    get_plan = pltpu.make_async_copy(plan_in, plan_ref, plan_sem.at[0])
    get_plan.start()
    own_count, raw_count, cross_count = sizes
    refs = list(refs[:-6])

    def take(count):
        taken = refs[:count]
        del refs[:count]
        return taken

    own, raw, raw_other = take(own_count), take(raw_count), take(raw_count)
    kept, moved, local = take(cross_count), take(cross_count), refs
    for ref, first in zip(own, places[0]):
        for j in range(ref.shape[0]):
            listed[first + j] = ref[j]
    for ref in local:
        for j in range(ref.shape[0]):
            listed[2 * slots + j] = ref[j]
    for ref, other, first in zip(raw, raw_other, places[1]):
        for j in range(ref.shape[0]):
            listed[first + j] = mix_branches(rows_at, table_ref, ref[j], other[j])
    get_plan.wait()
    column, branch = plan_ref[at.column], plan_ref[at.branch]
    for ref, other, first in zip(kept, moved, places[2]):
        half = ref.shape[1]
        here = pl.multiple_of(branch * half, half)
        there = pl.multiple_of((1 - branch) * half, half)
        for j in range(ref.shape[0]):
            listed[slots + first + j, pl.ds(here, half)] = ref[j]
            listed[slots + first + j, pl.ds(there, half)] = other[j]
    per_half = turned.shape[1]
    count = turned.shape[2] // HD * per_half
    spots = []
    for t in range(count):
        p = plan_ref[at.pos + t]
        slot = lax.shift_right_logical(p, 1)
        paired = jnp.where(jnp.bitwise_and(p, 1) == column, slot, slots + slot)
        spots.append(jnp.where(p >= 2 * slots, p, paired))
    parts = out_sems.shape[0]
    size = turned.shape[0] // parts
    copies = []
    for r in range(parts):
        tokens = slice(r * size, (r + 1) * size)
        for s in range(count // per_half):
            picked = [listed[spots[s * per_half + a], tokens] for a in range(per_half)]
            turned[tokens, :, s * HD : (s + 1) * HD] = jnp.swapaxes(jnp.stack(picked), 0, 1)
        copies.append(
            pltpu.make_async_copy(turned.at[tokens], out_ref.at[tokens], out_sems.at[r])
        )
        copies[-1].start()
    for copy in copies:
        copy.wait()


def ranked_body(rungs, qkv, timestep, windows, segments):
    rows = qkv.shape[1]
    heads = windows.shape[0]
    seq_count = lax.axis_size("seq")
    frame_count = lax.axis_size("frame")
    cfg_count = lax.axis_size("cfg")
    per_half = heads // (seq_count * cfg_count)
    outs = seq_count * per_half
    at = Layout(heads, outs)
    rows_at = Rows(heads)
    x3 = jnp.transpose(qkv[0], (1, 0, 2))
    lead, base = rungs[0][1] // 2, rungs[0][0] // 2
    plan, rung, kv_lead, kv_base = pl.pallas_call(
        functools.partial(plan_kernel, at, rungs, (seq_count, cfg_count)),
        out_shape=[
            jax.ShapeDtypeStruct((at.size,), jnp.int32),
            jax.ShapeDtypeStruct((1,), jnp.int32),
            jax.ShapeDtypeStruct((lead, 2, rows, HD), BF16),
            jax.ShapeDtypeStruct((base, 2, rows, HD), BF16),
        ],
        in_specs=[whole(pltpu.HBM)] * 3 + [whole(pl.ANY)],
        out_specs=[whole(pl.ANY)] * 2 + [whole()] * 2,
        scratch_shapes=[
            pltpu.SMEM(windows.shape, jnp.int32),
            pltpu.SMEM(segments.shape, jnp.int32),
            pltpu.SMEM(timestep.shape, jnp.int32),
            pltpu.SMEM((at.size,), jnp.int32),
            pltpu.SMEM((1,), jnp.int32),
            pltpu.SemaphoreType.DMA((3,)),
            pltpu.SemaphoreType.DMA((2,)),
            pltpu.SemaphoreType.DMA((lead + base,)),
        ],
        compiler_params=params(PLAN_VMEM_BYTES),
        name="plan",
    )(windows, segments, timestep, x3)

    grid_axes = ("seq", "frame")
    last = frame_count - 1
    apart = [(i, i - 1) for i in range(1, frame_count)] + [
        (frame_count + i, frame_count + i + 1) for i in range(last)
    ]
    onward = [(i, i + 1) for i in range(last)] + [
        (frame_count + i, frame_count + i - 1) for i in range(1, frame_count)
    ]

    def attempt(rung, plan, x3, kv_lead, kv_base):
        exchanged, wide = rung
        slots, far = exchanged // 2, wide // 2
        local = heads - exchanged
        bounds = [(0, lead), (lead, base)]
        if slots > base:
            bounds.append((base, slots))
        chunks = range(len(bounds))
        reaches = [far >= hi for _, hi in bounds]

        def cross(a):
            return lax.ppermute(a, "seq", SWAP)

        def mate(a):
            return lax.ppermute(a, "cfg", SWAP)

        def mix(mine, others, after):
            return mix_cores(table, rows_at, mine, others, after)

        across = [cross(kv_lead)]
        near_base = lax.ppermute(kv_base, grid_axes, apart)
        (kv_far,) = pack(plan, x3, [(range(at.mine, at.mine + lead), 1, 3)], [kv_base])
        far_own = [lax.ppermute(kv_far, grid_axes, onward)]
        split = base
        cut = 0
        parts = [(lead, split, 1), (split, base, 1)]
        parts += [(lo, hi, k) for k, (lo, hi) in enumerate(bounds) if k > 1]
        parts += [(0, cut, 0), (cut, lead, 0)]
        parts = [(lo, hi, k) for lo, hi, k in parts if hi > lo]
        later = [slot for lo, hi, _ in parts[1:] for slot in range(lo, hi)]
        jobs = [
            ([at.theirs + slot for slot in slots_of], 0, 1)
            for slots_of in (range(lead, split), later)
        ]
        jobs += [(range(at.theirs + lo, at.theirs + hi), 1, 3) for lo, hi in bounds[1:]]
        jobs += [(range(at.mine + lo, at.mine + hi), 1, 3) for lo, hi in bounds[2:]]
        jobs += [(range(at.mine + lead, at.mine + far), 1, 3)] if far > lead else []
        jobs.insert(0, (range(at.mine, at.mine + slots), 0, 1))
        q_own, q_early, q_late, *rest = pack(plan, x3, jobs, [kv_far])
        across += [cross(a) for a in rest[: len(bounds) - 1]]
        more = rest[len(bounds) - 1 :]
        if far > lead:
            far_own.append(lax.ppermute(more.pop(), grid_axes, onward))
        kv_more = more
        near_more = [lax.ppermute(a, grid_axes, apart) for a in kv_more]
        table = make_table(plan, at, rows_at, rows, [rest[0]])
        done = [table]
        if local:
            own_local = attend_local(plan, x3, at.order + exchanged, local, done)
            peer_local = mate(own_local)
            done = [own_local]

        near_across, far_across, guided = {}, {}, []
        (across[0],) = gate([across[0]], done)
        near_across[0] = lax.ppermute(across[0], grid_axes, onward)
        (q_early,) = gate([q_early], [across[0], *far_own])
        done = [q_early]
        q_early = cross(q_early)
        if local:
            guided = [mix(own_local, [peer_local], done)]
            done = guided
        (late,) = gate([across[0]], done)
        far_across[0] = lax.ppermute(late, grid_axes, apart)
        (across[1],) = gate([across[1]], [late, *done])
        done = [across[1]]
        for k in chunks[1:]:
            if k > 1:
                (across[k],) = gate([across[k]], done)
            done = [across[k]]
            near_across[k] = lax.ppermute(across[k], grid_axes, onward)
            if reaches[k]:
                far_across[k] = lax.ppermute(across[k], grid_axes, apart)
        (q_late,) = gate([q_late], [*done, near_across[0]])
        done = [q_late]
        q_late = cross(q_late)

        def attend_part(k, lo, hi, q, q_offset, names, bias_at, cond_at, after):
            skip = lo - bounds[k][0]
            arrays = {
                "O": (kv_more[0], skip) if k > 1 else (kv_base, lo),
                "X": (across[k], skip),
                "NO": (near_more[0], skip) if k > 1 else (near_base, lo),
                "NR": (near_across[k], skip),
                "FO": (far_own[min(k, 1)], max(lo - lead, 0)) if reaches[k] else None,
                "FR": (far_across.get(k), skip),
            }
            cut = slice(0, 5) if reaches[k] else slice(1, 4)
            sources = [arrays[name] for name in names[cut]]
            bias_at += lo * len(DISTANCES) + cut.start
            always = DISTANCES[cut].index(0)
            return attend_slots(
                table, q, q_offset, sources, always, hi - lo, bias_at, cond_at, after
            )

        def attend_own(k, after):
            lo, hi = bounds[k]
            return attend_part(k, lo, hi, q_own, lo, OWN_SOURCES, rows_at.own, None, after)

        def attend_across(part, after):
            lo, hi, k = parts[part]
            q = q_late if part else q_early
            offset = later.index(lo) if part else 0
            return attend_part(
                k, lo, hi, q, offset, ACROSS_SOURCES, rows_at.across, rows_at.cond, after
            )

        own, kept = {}, []
        own[0] = attend_own(0, done)
        keep, send = attend_across(0, [own[0]])
        got = mate(send)
        end = mix(own[0], [mate(own[0])], [keep])
        mixed = mix(keep, [got], [end])
        kept.append(cross(mixed))
        waiting = []
        done = [mixed]
        for part in range(1, len(parts)):
            keep, send = attend_across(part, done)
            middle = send.shape[0] // 2
            pieces = [send] if part < len(parts) - 1 else [send[:middle], send[middle:]]
            waiting.append((keep, [mate(piece) for piece in pieces]))
            done = [keep]
        done.append(kept[0])
        for keep, got in waiting:
            mixed = mix(keep, got, done)
            kept.append(cross(mixed))
            done = [mixed]
        raw = []
        for k in chunks[1:]:
            lo, hi = bounds[k]
            own[k] = attend_own(k, [mixed, kept[0]])
            middle = (hi - lo) // 2
            raw += [(lo, own[k][:middle]), (lo + middle, own[k][middle:])]
        others = [mate(a) for _, a in raw]
        arrays = [end, *[a for _, a in raw], *others, *kept, *[mate(a) for a in kept], *guided]
        places = ([0], [lo for lo, _ in raw], [lo for lo, _, _ in parts])
        sizes = tuple(len(firsts) for firsts in places)
        return pl.pallas_call(
            functools.partial(assemble_kernel, at, rows_at, sizes, slots, places),
            out_shape=pltpu.HBM((rows, per_half, seq_count * HD), BF16),
            in_specs=[whole(pl.ANY)] + [whole()] * (1 + len(arrays)),
            out_specs=whole(pltpu.HBM),
            scratch_shapes=[
                pltpu.SMEM(plan.shape, plan.dtype),
                pltpu.VMEM((heads, rows, HD), BF16),
                pltpu.VMEM((rows, per_half, seq_count * HD), BF16),
                pltpu.SemaphoreType.DMA((1,)),
                pltpu.SemaphoreType.DMA((4,)),
            ],
            compiler_params=params(),
            name="assemble",
        )(plan, table, *arrays)

    return lax.switch(
        rung[0],
        [functools.partial(attempt, rung) for rung in rungs],
        plan, x3, kv_lead, kv_base,
    )


def rungs_of(heads):
    third = heads // 3
    return ((2 * third + 2, third), (2 * third + 2, 2 * third + 2), (heads, heads))


def solution(mesh):
    sizes = dict(mesh.shape)

    def whole_body(qkv, timestep, windows, segments):
        frames_here = segments.shape[0] // sizes["frame"]
        one_frame = frames_here == sizes["seq"]
        if sizes["seq"] == 2 and sizes["cfg"] == 2 and one_frame and qkv.shape[1] % 32 == 0:
            return ranked_body(rungs_of(windows.shape[0]), qkv, timestep, windows, segments)
        return body(qkv, timestep, windows, segments)

    return jax.shard_map(
        whole_body,
        mesh=mesh,
        in_specs=(P("cfg", ("groups", "frame", "seq"), None, None), P("groups"), P(), P("groups")),
        out_specs=P(("groups", "frame", "seq"), "cfg", None),
        check_vma=False,
    )
```

```python
import functools
import math

import jax
import jax.numpy as jnp
from jax import lax
from jax.experimental import pallas as pl
from jax.experimental.pallas import tpu as pltpu
from jax.sharding import PartitionSpec as P

HD = 128
F_DEV = 2
W_MAX = 2


def padded_2(block, sides, width):
    for axis, dim in sides:
        count = lax.axis_size(axis)
        forward = [(i, i + 1) for i in range(count - 1)]
        backward = [(target, source) for source, target in forward]
        low = lax.ppermute(
            lax.slice_in_dim(block, block.shape[dim] - width, None, axis=dim), axis, forward
        )
        high = lax.ppermute(lax.slice_in_dim(block, 0, width, axis=dim), axis, backward)
        block = jnp.concatenate([low, block, high], axis=dim)
    return block


def attend(block, head_windows, seg_pad, first_frame):
    count_blocks = block.shape[0]
    branches = block.shape[1]
    rows_block = block.shape[2]
    columns = block.shape[4]
    heads_here = columns // HD
    per_frame = count_blocks // F_DEV
    reach = W_MAX * per_frame
    span = 2 * W_MAX + 1
    scale = 1.0 / math.sqrt(HD)
    pairs = block[:, :, :, 1:]
    padded = padded_2(pairs, (("frame", 0),), reach)
    queries = block[:, :, :, 0].reshape(count_blocks, branches, rows_block, heads_here, HD)
    offsets = jnp.arange(span, dtype=jnp.int32) - W_MAX
    within_reach = jnp.abs(offsets)[None, None, :] <= head_windows[:, :, None]
    results = []
    for frame_number in range(F_DEV):
        query = queries[frame_number * per_frame : (frame_number + 1) * per_frame]
        window_rows = padded[frame_number * per_frame : frame_number * per_frame + span * per_frame]
        window_rows = window_rows.reshape(span * per_frame, branches, rows_block, 2, heads_here, HD)
        key_rows = window_rows[:, :, :, 0]
        value_rows = window_rows[:, :, :, 1]
        here = first_frame + frame_number
        shots = lax.dynamic_slice_in_dim(seg_pad, here, span, 0)
        own_shot = lax.dynamic_index_in_dim(seg_pad, here + W_MAX, 0, keepdims=False)
        allowed = within_reach & (shots == own_shot)[None, None, :]
        allowed = jnp.repeat(allowed, per_frame, axis=2)
        scores = (
            jnp.einsum("sbthd,ubrhd->bhstur", query, key_rows, preferred_element_type=jnp.float32)
            * scale
        )
        scores = jnp.where(allowed[:, :, None, None, :, None], scores, -1e30)
        highest = jnp.max(scores, axis=(4, 5), keepdims=True)
        expd = jnp.exp(scores - highest)
        totals = jnp.sum(expd, axis=(4, 5))
        weights = expd.astype(jnp.bfloat16)
        mixed = jnp.einsum(
            "bhstur,ubrhd->sbthd", weights, value_rows, preferred_element_type=jnp.float32
        )
        mixed = mixed / jnp.transpose(totals, (2, 0, 3, 1))[..., None]
        results.append(mixed.astype(jnp.bfloat16))
    return jnp.concatenate(results, axis=0)


def body(qkv, timestep, windows, segments):
    first_frame = lax.axis_index("frame") * F_DEV
    fill = jnp.full((W_MAX,), -1, jnp.int32)
    seg_pad = jnp.concatenate([fill, segments, fill])
    strength = 1.0 + 4.0 * timestep[0].astype(jnp.float32) / 999.0
    seq_count = lax.axis_size("seq")
    cfg_count = lax.axis_size("cfg")
    spread = lax.all_to_all(qkv, ("seq", "cfg"), split_axis=3, concat_axis=0, tiled=True)
    columns = spread.shape[3]
    heads_here = columns // HD
    block = spread.reshape(seq_count, cfg_count, spread.shape[1], 3, columns)
    start_head = (lax.axis_index("seq") * cfg_count + lax.axis_index("cfg")) * heads_here
    head_windows = lax.dynamic_slice_in_dim(windows, start_head, heads_here, 0).reshape(
        1, heads_here
    )
    attended = attend(block, head_windows, seg_pad, first_frame)
    cond = attended[:, 0].astype(jnp.float32)
    uncond = attended[:, 1].astype(jnp.float32)
    guided = (uncond + strength * (cond - uncond)).astype(jnp.bfloat16)
    own_rows = lax.all_to_all(guided, "seq", split_axis=0, concat_axis=3, tiled=True)
    return own_rows[0]

LOG2E = 1.4426950408889634
MASKED = -1e30
BF16 = jnp.bfloat16
F32 = jnp.float32
VMEM_BYTES = 32 * 1024 * 1024
PLAN_VMEM_BYTES = 60 * 1024 * 1024
SWAP = ((0, 1), (1, 0))
COSTS = {"pack": 1e10, "local": 3e9, "own": 3e9, "across": 3e9, "mix": 1e8, "gate": 1e9}
STEPS = {"O": 0, "X": 1, "NO": 2, "NR": -1, "FO": -2, "FR": 3}
OWN_SOURCES = ("FO", "NR", "O", "X", "NO")
ACROSS_SOURCES = ("NR", "O", "X", "NO", "FR")
DISTANCES = (2, 1, 0, 1, 2)


def whole(space=pltpu.VMEM):
    return pl.BlockSpec(memory_space=space)


def cost(kind):
    return pl.CostEstimate(flops=int(COSTS[kind]), bytes_accessed=1, transcendentals=0)


def params(limit=VMEM_BYTES):
    return pltpu.CompilerParams(vmem_limit_bytes=limit)


class Rows:
    def __init__(self, heads):
        self.strength = 0
        self.cond = 1
        self.own = 8
        self.across = self.own + heads // 2 * len(DISTANCES)
        self.size = self.across + heads // 2 * len(DISTANCES)


class Layout:
    def __init__(self, heads, outs):
        self.mine = 0
        self.theirs = heads // 2
        self.order = heads
        self.rank = 2 * heads
        self.reach = 3 * heads
        self.my_reach = 4 * heads
        self.pos = self.my_reach + heads // 2
        self.own_match = self.pos + outs
        self.across_match = self.own_match + len(DISTANCES)
        self.branch = self.across_match + len(DISTANCES)
        self.column = self.branch + 1
        self.step = self.column + 1
        self.size = self.step + 1


def plan_kernel(
    at, rungs, split, windows_in, segments_in, step_in, x_ref, plan_out, rung_out, kv_ref, own_ref,
    windows_ref, segments_ref, step_ref, plan_ref, rung_ref, in_sems, out_sems, sems,
):
    get_windows = pltpu.make_async_copy(windows_in, windows_ref, in_sems.at[0])
    get_segments = pltpu.make_async_copy(segments_in, segments_ref, in_sems.at[1])
    get_windows.start()
    get_segments.start()
    get_step = pltpu.make_async_copy(step_in, step_ref, in_sems.at[2])
    get_step.start()
    heads = windows_ref.shape[0]
    frames = segments_ref.shape[0]
    column, block, branch = (lax.axis_index(a).astype(jnp.int32) for a in ("seq", "frame", "cfg"))
    get_windows.wait()
    reach = [windows_ref[h] for h in range(heads)]
    wide = [(w >= 2).astype(jnp.int32) for w in reach]
    some = [(w >= 1).astype(jnp.int32) for w in reach]
    most = functools.reduce(lambda a, b: a + b, wide)
    many = functools.reduce(lambda a, b: a + b, some)
    next_wide, next_some, next_none = jnp.int32(0), most, many
    for h in range(heads):
        spot = jnp.where(wide[h] == 1, next_wide, jnp.where(some[h] == 1, next_some, next_none))
        next_wide = next_wide + wide[h]
        next_some = next_some + some[h] - wide[h]
        next_none = next_none + 1 - some[h]
        plan_ref[at.order + spot] = jnp.int32(h)
        plan_ref[at.rank + h] = spot
        plan_ref[at.reach + spot] = reach[h]
    copies = []
    for out_ref, side in ((kv_ref, 1 - column), (own_ref, column)):
        for j in range(out_ref.shape[0]):
            start = pl.multiple_of(plan_ref[at.order + 2 * j + side] * HD, HD)
            copies.append(
                pltpu.make_async_copy(
                    x_ref.at[1:3, :, pl.ds(start, HD)], out_ref.at[j], sems.at[len(copies)]
                )
            )
            copies[-1].start()
    for j in range(heads // 2):
        plan_ref[at.mine + j] = plan_ref[at.order + 2 * j + column]
        plan_ref[at.theirs + j] = plan_ref[at.order + 2 * j + 1 - column]
        plan_ref[at.my_reach + j] = plan_ref[at.reach + 2 * j + column]
    columns, cores = split
    per_half = heads // (columns * cores)
    for t in range(columns * per_half):
        head = (t // per_half) * (heads // columns) + branch * per_half + t % per_half
        plan_ref[at.pos + t] = plan_ref[at.rank + head]
    own_frame = 2 * block + column
    sign = 1 - 2 * column

    get_segments.wait()
    get_step.wait()
    plan_ref[at.step] = step_ref[0]

    def shot(name):
        frame = own_frame + STEPS[name] * sign
        inside = jnp.logical_and(frame >= 0, frame < frames)
        return jnp.where(inside, segments_ref[jnp.clip(frame, 0, frames - 1)], -1)

    for first, names, query in (
        (at.own_match, OWN_SOURCES, "O"),
        (at.across_match, ACROSS_SOURCES, "X"),
    ):
        for k, name in enumerate(names):
            plan_ref[first + k] = (shot(name) == shot(query)).astype(jnp.int32)
    plan_ref[at.branch] = branch
    plan_ref[at.column] = column
    index = jnp.int32(len(rungs) - 1)
    for k in reversed(range(len(rungs) - 1)):
        fits = jnp.logical_and(many <= rungs[k][0], most <= rungs[k][1])
        index = jnp.where(fits, jnp.int32(k), index)
    rung_ref[0] = index
    for k, (ref, out) in enumerate(((plan_ref, plan_out), (rung_ref, rung_out))):
        copies.append(pltpu.make_async_copy(ref, out, out_sems.at[k]))
        copies[-1].start()
    for copy in copies:
        copy.wait()


def pack_kernel(jobs, count_in, plan_ref, x_ref, *refs):
    outs, sems = refs[count_in:-1], refs[-1]
    copies = []
    for out_ref, (spots, first, last) in zip(outs, jobs):
        for j, spot in enumerate(spots):
            start = pl.multiple_of(plan_ref[spot] * HD, HD)
            copies.append(
                pltpu.make_async_copy(
                    x_ref.at[first:last, :, pl.ds(start, HD)],
                    out_ref.at[j],
                    sems.at[len(copies)],
                )
            )
    for copy in copies:
        copy.start()
    for copy in copies:
        copy.wait()


def pack(plan, x3, jobs, after):
    rows = x3.shape[1]
    return pl.pallas_call(
        functools.partial(pack_kernel, jobs, len(after)),
        out_shape=[
            jax.ShapeDtypeStruct((len(spots), last - first, rows, HD), x3.dtype)
            for spots, first, last in jobs
        ],
        in_specs=[whole(pltpu.SMEM)] + [whole(pl.ANY)] * (1 + len(after)),
        out_specs=[whole()] * len(jobs),
        scratch_shapes=[pltpu.SemaphoreType.DMA((sum(len(spots) for spots, _, _ in jobs),))],
        compiler_params=params(),
        cost_estimate=cost("pack"),
        name="pack_heads",
    )(plan, x3, *after)


def gate_kernel(*refs):
    del refs


def gate(values, after):
    count = len(values)
    return pl.pallas_call(
        gate_kernel,
        out_shape=[jax.ShapeDtypeStruct(v.shape, v.dtype) for v in values],
        in_specs=[whole(pl.ANY)] * (count + len(after)),
        out_specs=[whole(pl.ANY)] * count,
        input_output_aliases={i: i for i in range(count)},
        compiler_params=params(),
        cost_estimate=cost("gate"),
        name="gate",
    )(*values, *after)


def softmax_mix(q, keys, values, biases):
    factor = LOG2E / math.sqrt(HD)
    scores = []
    for key, bias in zip(keys, biases):
        score = lax.dot_general(q, key, (((1,), (1,)), ((), ())), preferred_element_type=F32)
        scores.append(score if bias is None else score + bias)
    top = jnp.max(functools.reduce(jnp.maximum, scores), axis=1, keepdims=True)
    expd = [jnp.exp2((score - top) * factor) for score in scores]
    total = jnp.sum(functools.reduce(jnp.add, expd), axis=1, keepdims=True)
    mixed = functools.reduce(
        jnp.add,
        [
            jnp.dot(e.astype(BF16), value, preferred_element_type=F32)
            for e, value in zip(expd, values)
        ],
    )
    return mixed / total


def table_kernel(at, rows_at, plan_ref, *refs):
    table_ref = refs[-1]
    width = table_ref.shape[1]

    def put(row, value):
        table_ref[row : row + 1, :] = jnp.full((1, width), value, F32)

    step = jnp.full((1, width), plan_ref[at.step], jnp.int32).astype(F32)
    table_ref[rows_at.strength : rows_at.strength + 1, :] = 1.0 + 4.0 * step / 999.0
    put(rows_at.cond, jnp.where(plan_ref[at.branch] == 0, 1.0, 0.0).astype(F32))
    for first, match_at in ((rows_at.own, at.own_match), (rows_at.across, at.across_match)):
        for slot in range((rows_at.across - rows_at.own) // len(DISTANCES)):
            reach = plan_ref[at.my_reach + slot]
            for k, distance in enumerate(DISTANCES):
                seen = jnp.logical_and(reach >= distance, plan_ref[match_at + k] != 0)
                put(
                    first + slot * len(DISTANCES) + k, jnp.where(seen, 0.0, MASKED).astype(F32)
                )


def make_table(plan, at, rows_at, width, after):
    return pl.pallas_call(
        functools.partial(table_kernel, at, rows_at),
        out_shape=jax.ShapeDtypeStruct((rows_at.size, width), F32),
        in_specs=[whole(pltpu.SMEM)] + [whole(pl.ANY)] * len(after),
        out_specs=whole(),
        compiler_params=params(),
        cost_estimate=cost("mix"),
        name="table",
    )(plan, *after)


def local_kernel(count, heads_at, plan_ref, x_ref, *refs):
    out_ref, held, sems = refs[-3:]
    copies = []
    for j in range(count):
        start = pl.multiple_of(plan_ref[heads_at + j] * HD, HD)
        copies.append(
            pltpu.make_async_copy(x_ref.at[:, :, pl.ds(start, HD)], held.at[j], sems.at[j])
        )
        copies[-1].start()
    for copy in copies:
        copy.wait()
    for j in range(count):
        out_ref[j] = softmax_mix(held[j, 0], [held[j, 1]], [held[j, 2]], [None]).astype(BF16)


def attend_local(plan, x3, heads_at, count, after):
    planes, rows, _ = x3.shape
    return pl.pallas_call(
        functools.partial(local_kernel, count, heads_at),
        out_shape=jax.ShapeDtypeStruct((count, rows, HD), BF16),
        in_specs=[whole(pltpu.SMEM)] + [whole(pl.ANY)] * (1 + len(after)),
        out_specs=whole(),
        scratch_shapes=[
            pltpu.VMEM((count, planes, rows, HD), BF16),
            pltpu.SemaphoreType.DMA((count,)),
        ],
        compiler_params=params(),
        cost_estimate=cost("local"),
        name="attend_local",
    )(plan, x3, *after)


def attend_kernel(
    count, q_offset, offsets, always, bias_at, cond_at, written_out, table_ref, q_ref, *refs
):
    sources = len(offsets)
    kv_refs = refs[:sources]
    halves = cond_at is not None
    outs = refs[-2:] if halves else refs[-1:]

    def one(j):
        keys = [ref[o + j, 0] for ref, o in zip(kv_refs, offsets)]
        values = [ref[o + j, 1] for ref, o in zip(kv_refs, offsets)]
        first = bias_at + j * len(DISTANCES)
        biases = [
            None if k == always else table_ref[pl.ds(first + k, 1), :] for k in range(sources)
        ]
        out = softmax_mix(q_ref[q_offset + j, 0], keys, values, biases)
        if halves:
            half = out.shape[0] // 2
            low, high = out[:half], out[half:]
            is_first = table_ref[cond_at : cond_at + 1, :HD] > 0.0
            outs[0][j] = jnp.where(is_first, low, high).astype(BF16)
            outs[1][j] = jnp.where(is_first, high, low).astype(BF16)
        else:
            outs[0][j] = out.astype(BF16)

    pairs = 0 if written_out else count // 2

    def two(i, carry):
        one(2 * i)
        one(2 * i + 1)
        return carry

    if pairs:
        lax.fori_loop(0, pairs, two, 0)
    for j in range(2 * pairs, count):
        one(j)


def attend_slots(
    table, q, q_offset, sources, always, count, bias_at, cond_at, written_out, after
):
    rows = q.shape[-2]
    if cond_at is None:
        out_shape = jax.ShapeDtypeStruct((count, rows, HD), BF16)
        out_specs = whole()
    else:
        out_shape = [jax.ShapeDtypeStruct((count, rows // 2, HD), BF16)] * 2
        out_specs = [whole()] * 2
    arrays = [array for array, _ in sources]
    offsets = [offset for _, offset in sources]
    return pl.pallas_call(
        functools.partial(
            attend_kernel, count, q_offset, offsets, always, bias_at, cond_at, written_out
        ),
        out_shape=out_shape,
        in_specs=[whole()] * (2 + len(arrays)) + [whole(pl.ANY)] * len(after),
        out_specs=out_specs,
        compiler_params=params(),
        cost_estimate=cost("own" if cond_at is None else "across"),
        name="attend",
    )(table, q, *arrays, *after)


def blend(cond, uncond, strength):
    cond = cond.astype(F32)
    uncond = uncond.astype(F32)
    return (uncond + strength * (cond - uncond)).astype(BF16)


def mix_branches(rows_at, table_ref, mine, other):
    strength = table_ref[rows_at.strength : rows_at.strength + 1, :HD]
    is_cond = table_ref[rows_at.cond : rows_at.cond + 1, :HD] > 0.0
    mine = mine.astype(F32)
    other = other.astype(F32)
    return blend(jnp.where(is_cond, mine, other), jnp.where(is_cond, other, mine), strength)


def mix_kernel(rows_at, pieces, table_ref, mine_ref, *refs):
    out_ref = refs[-1]
    j = 0
    for other_ref in refs[:pieces]:
        for i in range(other_ref.shape[0]):
            out_ref[j] = mix_branches(rows_at, table_ref, mine_ref[j], other_ref[i])
            j += 1


def mix_cores(table, rows_at, mine, others, after):
    return pl.pallas_call(
        functools.partial(mix_kernel, rows_at, len(others)),
        out_shape=jax.ShapeDtypeStruct(mine.shape, mine.dtype),
        in_specs=[whole()] * (2 + len(others)) + [whole(pl.ANY)] * len(after),
        out_specs=whole(),
        compiler_params=params(),
        cost_estimate=cost("mix"),
        name="mix",
    )(table, mine, *others, *after)


def assemble_kernel(at, rows_at, sizes, slots, places, plan_in, table_ref, *refs):
    out_ref, plan_ref, listed, turned, plan_sem, out_sems = refs[-6:]
    get_plan = pltpu.make_async_copy(plan_in, plan_ref, plan_sem.at[0])
    get_plan.start()
    own_count, raw_count, cross_count = sizes
    refs = list(refs[:-6])

    def take(count):
        taken = refs[:count]
        del refs[:count]
        return taken

    own, raw, raw_other = take(own_count), take(raw_count), take(raw_count)
    kept, moved, local = take(cross_count), take(cross_count), refs
    for ref, first in zip(own, places[0]):
        for j in range(ref.shape[0]):
            listed[first + j] = ref[j]
    for ref in local:
        for j in range(ref.shape[0]):
            listed[2 * slots + j] = ref[j]
    for ref, other, first in zip(raw, raw_other, places[1]):
        for j in range(ref.shape[0]):
            listed[first + j] = mix_branches(rows_at, table_ref, ref[j], other[j])
    get_plan.wait()
    column, branch = plan_ref[at.column], plan_ref[at.branch]
    for ref, other, first in zip(kept, moved, places[2]):
        half = ref.shape[1]
        here = pl.multiple_of(branch * half, half)
        there = pl.multiple_of((1 - branch) * half, half)
        for j in range(ref.shape[0]):
            listed[slots + first + j, pl.ds(here, half)] = ref[j]
            listed[slots + first + j, pl.ds(there, half)] = other[j]
    per_half = turned.shape[1]
    count = turned.shape[2] // HD * per_half
    spots = []
    for t in range(count):
        p = plan_ref[at.pos + t]
        slot = lax.shift_right_logical(p, 1)
        paired = jnp.where(jnp.bitwise_and(p, 1) == column, slot, slots + slot)
        spots.append(jnp.where(p >= 2 * slots, p, paired))
    parts = out_sems.shape[0]
    size = turned.shape[0] // parts
    copies = []
    for r in range(parts):
        tokens = slice(r * size, (r + 1) * size)
        for s in range(count // per_half):
            picked = [listed[spots[s * per_half + a], tokens] for a in range(per_half)]
            turned[tokens, :, s * HD : (s + 1) * HD] = jnp.swapaxes(jnp.stack(picked), 0, 1)
        copies.append(
            pltpu.make_async_copy(turned.at[tokens], out_ref.at[tokens], out_sems.at[r])
        )
        copies[-1].start()
    for copy in copies:
        copy.wait()


def ranked_body(rungs, qkv, timestep, windows, segments):
    rows = qkv.shape[1]
    heads = windows.shape[0]
    seq_count = lax.axis_size("seq")
    frame_count = lax.axis_size("frame")
    cfg_count = lax.axis_size("cfg")
    per_half = heads // (seq_count * cfg_count)
    outs = seq_count * per_half
    at = Layout(heads, outs)
    rows_at = Rows(heads)
    x3 = jnp.transpose(qkv[0], (1, 0, 2))
    lead, base = rungs[0][1] // 2, rungs[0][0] // 2
    plan, rung, kv_lead, kv_base = pl.pallas_call(
        functools.partial(plan_kernel, at, rungs, (seq_count, cfg_count)),
        out_shape=[
            jax.ShapeDtypeStruct((at.size,), jnp.int32),
            jax.ShapeDtypeStruct((1,), jnp.int32),
            jax.ShapeDtypeStruct((lead, 2, rows, HD), BF16),
            jax.ShapeDtypeStruct((base, 2, rows, HD), BF16),
        ],
        in_specs=[whole(pltpu.HBM)] * 3 + [whole(pl.ANY)],
        out_specs=[whole(pl.ANY)] * 2 + [whole()] * 2,
        scratch_shapes=[
            pltpu.SMEM(windows.shape, jnp.int32),
            pltpu.SMEM(segments.shape, jnp.int32),
            pltpu.SMEM(timestep.shape, jnp.int32),
            pltpu.SMEM((at.size,), jnp.int32),
            pltpu.SMEM((1,), jnp.int32),
            pltpu.SemaphoreType.DMA((3,)),
            pltpu.SemaphoreType.DMA((2,)),
            pltpu.SemaphoreType.DMA((lead + base,)),
        ],
        compiler_params=params(PLAN_VMEM_BYTES),
        name="plan",
    )(windows, segments, timestep, x3)

    grid_axes = ("seq", "frame")
    last = frame_count - 1
    apart = [(i, i - 1) for i in range(1, frame_count)] + [
        (frame_count + i, frame_count + i + 1) for i in range(last)
    ]
    onward = [(i, i + 1) for i in range(last)] + [
        (frame_count + i, frame_count + i - 1) for i in range(1, frame_count)
    ]

    def attempt(rung, plan, x3, kv_lead, kv_base):
        exchanged, wide = rung
        slots, far = exchanged // 2, wide // 2
        local = heads - exchanged
        bounds = [(0, lead), (lead, base)]
        if slots > base:
            bounds.append((base, slots))
        chunks = range(len(bounds))
        reaches = [far >= hi for _, hi in bounds]

        def cross(a):
            return lax.ppermute(a, "seq", SWAP)

        def mate(a):
            return lax.ppermute(a, "cfg", SWAP)

        def mix(mine, others, after):
            return mix_cores(table, rows_at, mine, others, after)

        across = [cross(kv_lead)]
        near_base = lax.ppermute(kv_base, grid_axes, apart)
        (kv_far,) = pack(plan, x3, [(range(at.mine, at.mine + lead), 1, 3)], [kv_base])
        far_own = [lax.ppermute(kv_far, grid_axes, onward)]
        split = base
        cut = 0
        parts = [(lead, split, 1), (split, base, 1)]
        parts += [(lo, hi, k) for k, (lo, hi) in enumerate(bounds) if k > 1]
        parts += [(0, cut, 0), (cut, lead, 0)]
        parts = [(lo, hi, k) for lo, hi, k in parts if hi > lo]
        later = [slot for lo, hi, _ in parts[1:] for slot in range(lo, hi)]
        jobs = [
            ([at.theirs + slot for slot in slots_of], 0, 1)
            for slots_of in (range(lead, split), later)
        ]
        jobs += [(range(at.theirs + lo, at.theirs + hi), 1, 3) for lo, hi in bounds[1:]]
        jobs += [(range(at.mine + lo, at.mine + hi), 1, 3) for lo, hi in bounds[2:]]
        jobs += [(range(at.mine + lead, at.mine + far), 1, 3)] if far > lead else []
        jobs.insert(0, (range(at.mine, at.mine + slots), 0, 1))
        q_own, q_early, q_late, *rest = pack(plan, x3, jobs, [kv_far])
        across += [cross(a) for a in rest[: len(bounds) - 1]]
        more = rest[len(bounds) - 1 :]
        if far > lead:
            far_own.append(lax.ppermute(more.pop(), grid_axes, onward))
        kv_more = more
        near_more = [lax.ppermute(a, grid_axes, apart) for a in kv_more]
        table = make_table(plan, at, rows_at, rows, [rest[0]])
        done = [table]
        if local:
            own_local = attend_local(plan, x3, at.order + exchanged, local, done)
            peer_local = mate(own_local)
            done = [own_local]

        near_across, far_across, guided = {}, {}, []
        (across[0],) = gate([across[0]], done)
        near_across[0] = lax.ppermute(across[0], grid_axes, onward)
        (q_early,) = gate([q_early], [across[0], *far_own])
        done = [q_early]
        q_early = cross(q_early)
        if local:
            guided = [mix(own_local, [peer_local], done)]
            done = guided
        (late,) = gate([across[0]], done)
        far_across[0] = lax.ppermute(late, grid_axes, apart)
        (across[1],) = gate([across[1]], [late, *done])
        done = [across[1]]
        for k in chunks[1:]:
            if k > 1:
                (across[k],) = gate([across[k]], done)
            done = [across[k]]
            near_across[k] = lax.ppermute(across[k], grid_axes, onward)
            if reaches[k]:
                far_across[k] = lax.ppermute(across[k], grid_axes, apart)
        (q_late,) = gate([q_late], [*done, near_across[0]])
        done = [q_late]
        q_late = cross(q_late)

        def attend_part(k, lo, hi, q, q_offset, names, bias_at, cond_at, after):
            skip = lo - bounds[k][0]
            arrays = {
                "O": (kv_more[0], skip) if k > 1 else (kv_base, lo),
                "X": (across[k], skip),
                "NO": (near_more[0], skip) if k > 1 else (near_base, lo),
                "NR": (near_across[k], skip),
                "FO": (far_own[min(k, 1)], max(lo - lead, 0)) if reaches[k] else None,
                "FR": (far_across.get(k), skip),
            }
            cut = slice(0, 5) if reaches[k] else slice(1, 4)
            sources = [arrays[name] for name in names[cut]]
            bias_at += lo * len(DISTANCES) + cut.start
            always = DISTANCES[cut].index(0)
            return attend_slots(
                table, q, q_offset, sources, always, hi - lo, bias_at, cond_at, rung == rungs[0], after
            )

        def attend_own(k, after):
            lo, hi = bounds[k]
            return attend_part(k, lo, hi, q_own, lo, OWN_SOURCES, rows_at.own, None, after)

        def attend_across(part, after):
            lo, hi, k = parts[part]
            q = q_late if part else q_early
            offset = later.index(lo) if part else 0
            return attend_part(
                k, lo, hi, q, offset, ACROSS_SOURCES, rows_at.across, rows_at.cond, after
            )

        own, kept = {}, []
        own[0] = attend_own(0, done)
        keep, send = attend_across(0, [own[0]])
        got = mate(send)
        end = mix(own[0], [mate(own[0])], [keep])
        mixed = mix(keep, [got], [end])
        kept.append(cross(mixed))
        waiting = []
        done = [mixed]
        for part in range(1, len(parts)):
            keep, send = attend_across(part, done)
            middle = send.shape[0] // 2
            pieces = [send] if part < len(parts) - 1 else [send[:middle], send[middle:]]
            waiting.append((keep, [mate(piece) for piece in pieces]))
            done = [keep]
        for keep, got in waiting:
            mixed = mix(keep, got, done)
            kept.append(cross(mixed))
            done = [mixed]
        raw = []
        for k in chunks[1:]:
            lo, hi = bounds[k]
            own[k] = attend_own(k, [mixed, kept[0]])
            middle = (hi - lo) // 2
            raw += [(lo, own[k][:middle]), (lo + middle, own[k][middle:])]
        others = [mate(a) for _, a in raw]
        arrays = [end, *[a for _, a in raw], *others, *kept, *[mate(a) for a in kept], *guided]
        places = ([0], [lo for lo, _ in raw], [lo for lo, _, _ in parts])
        sizes = tuple(len(firsts) for firsts in places)
        return pl.pallas_call(
            functools.partial(assemble_kernel, at, rows_at, sizes, slots, places),
            out_shape=pltpu.HBM((rows, per_half, seq_count * HD), BF16),
            in_specs=[whole(pl.ANY)] + [whole()] * (1 + len(arrays)),
            out_specs=whole(pltpu.HBM),
            scratch_shapes=[
                pltpu.SMEM(plan.shape, plan.dtype),
                pltpu.VMEM((heads, rows, HD), BF16),
                pltpu.VMEM((rows, per_half, seq_count * HD), BF16),
                pltpu.SemaphoreType.DMA((1,)),
                pltpu.SemaphoreType.DMA((4,)),
            ],
            compiler_params=params(),
            name="assemble",
        )(plan, table, *arrays)

    return lax.switch(
        rung[0],
        [functools.partial(attempt, rung) for rung in rungs],
        plan, x3, kv_lead, kv_base,
    )


def rungs_of(heads):
    third = heads // 3
    return ((2 * third + 2, third), (2 * third + 2, 2 * third + 2), (heads, heads))


def solution(mesh):
    sizes = dict(mesh.shape)

    def whole_body(qkv, timestep, windows, segments):
        frames_here = segments.shape[0] // sizes["frame"]
        one_frame = frames_here == sizes["seq"]
        if sizes["seq"] == 2 and sizes["cfg"] == 2 and one_frame and qkv.shape[1] % 32 == 0:
            return ranked_body(rungs_of(windows.shape[0]), qkv, timestep, windows, segments)
        return body(qkv, timestep, windows, segments)

    return jax.shard_map(
        whole_body,
        mesh=mesh,
        in_specs=(P("cfg", ("groups", "frame", "seq"), None, None), P("groups"), P(), P("groups")),
        out_specs=P(("groups", "frame", "seq"), "cfg", None),
        check_vma=False,
    )
```

```python
import functools
import math

import jax
import jax.numpy as jnp
from jax import lax
from jax.experimental import pallas as pl
from jax.experimental.pallas import tpu as pltpu
from jax.sharding import PartitionSpec as P

HD = 128
F_DEV = 2
W_MAX = 2


def padded_2(block, sides, width):
    for axis, dim in sides:
        count = lax.axis_size(axis)
        forward = [(i, i + 1) for i in range(count - 1)]
        backward = [(target, source) for source, target in forward]
        low = lax.ppermute(
            lax.slice_in_dim(block, block.shape[dim] - width, None, axis=dim), axis, forward
        )
        high = lax.ppermute(lax.slice_in_dim(block, 0, width, axis=dim), axis, backward)
        block = jnp.concatenate([low, block, high], axis=dim)
    return block


def attend(block, head_windows, seg_pad, first_frame):
    count_blocks = block.shape[0]
    branches = block.shape[1]
    rows_block = block.shape[2]
    columns = block.shape[4]
    heads_here = columns // HD
    per_frame = count_blocks // F_DEV
    reach = W_MAX * per_frame
    span = 2 * W_MAX + 1
    scale = 1.0 / math.sqrt(HD)
    pairs = block[:, :, :, 1:]
    padded = padded_2(pairs, (("frame", 0),), reach)
    queries = block[:, :, :, 0].reshape(count_blocks, branches, rows_block, heads_here, HD)
    offsets = jnp.arange(span, dtype=jnp.int32) - W_MAX
    within_reach = jnp.abs(offsets)[None, None, :] <= head_windows[:, :, None]
    results = []
    for frame_number in range(F_DEV):
        query = queries[frame_number * per_frame : (frame_number + 1) * per_frame]
        window_rows = padded[frame_number * per_frame : frame_number * per_frame + span * per_frame]
        window_rows = window_rows.reshape(span * per_frame, branches, rows_block, 2, heads_here, HD)
        key_rows = window_rows[:, :, :, 0]
        value_rows = window_rows[:, :, :, 1]
        here = first_frame + frame_number
        shots = lax.dynamic_slice_in_dim(seg_pad, here, span, 0)
        own_shot = lax.dynamic_index_in_dim(seg_pad, here + W_MAX, 0, keepdims=False)
        allowed = within_reach & (shots == own_shot)[None, None, :]
        allowed = jnp.repeat(allowed, per_frame, axis=2)
        scores = (
            jnp.einsum("sbthd,ubrhd->bhstur", query, key_rows, preferred_element_type=jnp.float32)
            * scale
        )
        scores = jnp.where(allowed[:, :, None, None, :, None], scores, -1e30)
        highest = jnp.max(scores, axis=(4, 5), keepdims=True)
        expd = jnp.exp(scores - highest)
        totals = jnp.sum(expd, axis=(4, 5))
        weights = expd.astype(jnp.bfloat16)
        mixed = jnp.einsum(
            "bhstur,ubrhd->sbthd", weights, value_rows, preferred_element_type=jnp.float32
        )
        mixed = mixed / jnp.transpose(totals, (2, 0, 3, 1))[..., None]
        results.append(mixed.astype(jnp.bfloat16))
    return jnp.concatenate(results, axis=0)


def body(qkv, timestep, windows, segments):
    first_frame = lax.axis_index("frame") * F_DEV
    fill = jnp.full((W_MAX,), -1, jnp.int32)
    seg_pad = jnp.concatenate([fill, segments, fill])
    strength = 1.0 + 4.0 * timestep[0].astype(jnp.float32) / 999.0
    seq_count = lax.axis_size("seq")
    cfg_count = lax.axis_size("cfg")
    spread = lax.all_to_all(qkv, ("seq", "cfg"), split_axis=3, concat_axis=0, tiled=True)
    columns = spread.shape[3]
    heads_here = columns // HD
    block = spread.reshape(seq_count, cfg_count, spread.shape[1], 3, columns)
    start_head = (lax.axis_index("seq") * cfg_count + lax.axis_index("cfg")) * heads_here
    head_windows = lax.dynamic_slice_in_dim(windows, start_head, heads_here, 0).reshape(
        1, heads_here
    )
    attended = attend(block, head_windows, seg_pad, first_frame)
    cond = attended[:, 0].astype(jnp.float32)
    uncond = attended[:, 1].astype(jnp.float32)
    guided = (uncond + strength * (cond - uncond)).astype(jnp.bfloat16)
    own_rows = lax.all_to_all(guided, "seq", split_axis=0, concat_axis=3, tiled=True)
    return own_rows[0]

LOG2E = 1.4426950408889634
MASKED = -1e30
UNROLLED_BLOCKS = 25
BF16 = jnp.bfloat16
F32 = jnp.float32
VMEM_BYTES = 32 * 1024 * 1024
PLAN_VMEM_BYTES = 60 * 1024 * 1024
SWAP = ((0, 1), (1, 0))
COSTS = {"pack": 1e10, "local": 3e9, "own": 3e9, "across": 3e9, "mix": 1e8, "gate": 1e9}
STEPS = {"O": 0, "X": 1, "NO": 2, "NR": -1, "FO": -2, "FR": 3}
OWN_SOURCES = ("FO", "NR", "O", "X", "NO")
ACROSS_SOURCES = ("NR", "O", "X", "NO", "FR")
DISTANCES = (2, 1, 0, 1, 2)


def whole(space=pltpu.VMEM):
    return pl.BlockSpec(memory_space=space)


def cost(kind):
    return pl.CostEstimate(flops=int(COSTS[kind]), bytes_accessed=1, transcendentals=0)


def params(limit=VMEM_BYTES):
    return pltpu.CompilerParams(vmem_limit_bytes=limit)


class Rows:
    def __init__(self, heads):
        self.strength = 0
        self.cond = 1
        self.own = 8
        self.across = self.own + heads // 2 * len(DISTANCES)
        self.size = self.across + heads // 2 * len(DISTANCES)


class Layout:
    def __init__(self, heads, outs):
        self.mine = 0
        self.theirs = heads // 2
        self.order = heads
        self.rank = 2 * heads
        self.reach = 3 * heads
        self.my_reach = 4 * heads
        self.pos = self.my_reach + heads // 2
        self.own_match = self.pos + outs
        self.across_match = self.own_match + len(DISTANCES)
        self.branch = self.across_match + len(DISTANCES)
        self.column = self.branch + 1
        self.step = self.column + 1
        self.size = self.step + 1


def plan_kernel(
    at, rungs, split, windows_in, segments_in, step_in, x_ref, plan_out, rung_out, kv_ref, own_ref,
    windows_ref, segments_ref, step_ref, plan_ref, rung_ref, in_sems, out_sems, sems,
):
    get_windows = pltpu.make_async_copy(windows_in, windows_ref, in_sems.at[0])
    get_segments = pltpu.make_async_copy(segments_in, segments_ref, in_sems.at[1])
    get_windows.start()
    get_segments.start()
    get_step = pltpu.make_async_copy(step_in, step_ref, in_sems.at[2])
    get_step.start()
    heads = windows_ref.shape[0]
    frames = segments_ref.shape[0]
    column, block, branch = (lax.axis_index(a).astype(jnp.int32) for a in ("seq", "frame", "cfg"))
    get_windows.wait()
    reach = [windows_ref[h] for h in range(heads)]
    wide = [(w >= 2).astype(jnp.int32) for w in reach]
    some = [(w >= 1).astype(jnp.int32) for w in reach]
    most = functools.reduce(lambda a, b: a + b, wide)
    many = functools.reduce(lambda a, b: a + b, some)
    next_wide, next_some, next_none = jnp.int32(0), most, many
    for h in range(heads):
        spot = jnp.where(wide[h] == 1, next_wide, jnp.where(some[h] == 1, next_some, next_none))
        next_wide = next_wide + wide[h]
        next_some = next_some + some[h] - wide[h]
        next_none = next_none + 1 - some[h]
        plan_ref[at.order + spot] = jnp.int32(h)
        plan_ref[at.rank + h] = spot
        plan_ref[at.reach + spot] = reach[h]
    copies = []
    for out_ref, side in ((kv_ref, 1 - column), (own_ref, column)):
        for j in range(out_ref.shape[0]):
            start = pl.multiple_of(plan_ref[at.order + 2 * j + side] * HD, HD)
            copies.append(
                pltpu.make_async_copy(
                    x_ref.at[1:3, :, pl.ds(start, HD)], out_ref.at[j], sems.at[len(copies)]
                )
            )
            copies[-1].start()
    for j in range(heads // 2):
        plan_ref[at.mine + j] = plan_ref[at.order + 2 * j + column]
        plan_ref[at.theirs + j] = plan_ref[at.order + 2 * j + 1 - column]
        plan_ref[at.my_reach + j] = plan_ref[at.reach + 2 * j + column]
    columns, cores = split
    per_half = heads // (columns * cores)
    for t in range(columns * per_half):
        head = (t // per_half) * (heads // columns) + branch * per_half + t % per_half
        plan_ref[at.pos + t] = plan_ref[at.rank + head]
    own_frame = 2 * block + column
    sign = 1 - 2 * column

    get_segments.wait()
    get_step.wait()
    plan_ref[at.step] = step_ref[0]

    def shot(name):
        frame = own_frame + STEPS[name] * sign
        inside = jnp.logical_and(frame >= 0, frame < frames)
        return jnp.where(inside, segments_ref[jnp.clip(frame, 0, frames - 1)], -1)

    for first, names, query in (
        (at.own_match, OWN_SOURCES, "O"),
        (at.across_match, ACROSS_SOURCES, "X"),
    ):
        for k, name in enumerate(names):
            plan_ref[first + k] = (shot(name) == shot(query)).astype(jnp.int32)
    plan_ref[at.branch] = branch
    plan_ref[at.column] = column
    index = jnp.int32(len(rungs) - 1)
    for k in reversed(range(len(rungs) - 1)):
        fits = jnp.logical_and(many <= rungs[k][0], most <= rungs[k][1])
        index = jnp.where(fits, jnp.int32(k), index)
    rung_ref[0] = index
    for k, (ref, out) in enumerate(((plan_ref, plan_out), (rung_ref, rung_out))):
        copies.append(pltpu.make_async_copy(ref, out, out_sems.at[k]))
        copies[-1].start()
    for copy in copies:
        copy.wait()


def pack_kernel(jobs, count_in, plan_ref, x_ref, *refs):
    outs, sems = refs[count_in:-1], refs[-1]
    copies = []
    for out_ref, (spots, first, last) in zip(outs, jobs):
        for j, spot in enumerate(spots):
            start = pl.multiple_of(plan_ref[spot] * HD, HD)
            copies.append(
                pltpu.make_async_copy(
                    x_ref.at[first:last, :, pl.ds(start, HD)],
                    out_ref.at[j],
                    sems.at[len(copies)],
                )
            )
    for copy in copies:
        copy.start()
    for copy in copies:
        copy.wait()


def pack(plan, x3, jobs, after):
    rows = x3.shape[1]
    return pl.pallas_call(
        functools.partial(pack_kernel, jobs, len(after)),
        out_shape=[
            jax.ShapeDtypeStruct((len(spots), last - first, rows, HD), x3.dtype)
            for spots, first, last in jobs
        ],
        in_specs=[whole(pltpu.SMEM)] + [whole(pl.ANY)] * (1 + len(after)),
        out_specs=[whole()] * len(jobs),
        scratch_shapes=[pltpu.SemaphoreType.DMA((sum(len(spots) for spots, _, _ in jobs),))],
        compiler_params=params(),
        cost_estimate=cost("pack"),
        name="pack_heads",
    )(plan, x3, *after)


def gate_kernel(*refs):
    del refs


def gate(values, after):
    count = len(values)
    return pl.pallas_call(
        gate_kernel,
        out_shape=[jax.ShapeDtypeStruct(v.shape, v.dtype) for v in values],
        in_specs=[whole(pl.ANY)] * (count + len(after)),
        out_specs=[whole(pl.ANY)] * count,
        input_output_aliases={i: i for i in range(count)},
        compiler_params=params(),
        cost_estimate=cost("gate"),
        name="gate",
    )(*values, *after)


def softmax_mix(q, keys, values, biases):
    factor = LOG2E / math.sqrt(HD)
    scores = []
    for key, bias in zip(keys, biases):
        score = lax.dot_general(q, key, (((1,), (1,)), ((), ())), preferred_element_type=F32)
        scores.append(score if bias is None else score + bias)
    top = jnp.max(functools.reduce(jnp.maximum, scores), axis=1, keepdims=True)
    expd = [jnp.exp2((score - top) * factor) for score in scores]
    total = jnp.sum(functools.reduce(jnp.add, expd), axis=1, keepdims=True)
    mixed = functools.reduce(
        jnp.add,
        [
            jnp.dot(e.astype(BF16), value, preferred_element_type=F32)
            for e, value in zip(expd, values)
        ],
    )
    return mixed / total


def table_kernel(at, rows_at, plan_ref, *refs):
    table_ref = refs[-1]
    width = table_ref.shape[1]

    def put(row, value):
        table_ref[row : row + 1, :] = jnp.full((1, width), value, F32)

    step = jnp.full((1, width), plan_ref[at.step], jnp.int32).astype(F32)
    table_ref[rows_at.strength : rows_at.strength + 1, :] = 1.0 + 4.0 * step / 999.0
    put(rows_at.cond, jnp.where(plan_ref[at.branch] == 0, 1.0, 0.0).astype(F32))
    for first, match_at in ((rows_at.own, at.own_match), (rows_at.across, at.across_match)):
        for slot in range((rows_at.across - rows_at.own) // len(DISTANCES)):
            reach = plan_ref[at.my_reach + slot]
            for k, distance in enumerate(DISTANCES):
                seen = jnp.logical_and(reach >= distance, plan_ref[match_at + k] != 0)
                put(
                    first + slot * len(DISTANCES) + k, jnp.where(seen, 0.0, MASKED).astype(F32)
                )


def make_table(plan, at, rows_at, width, after):
    return pl.pallas_call(
        functools.partial(table_kernel, at, rows_at),
        out_shape=jax.ShapeDtypeStruct((rows_at.size, width), F32),
        in_specs=[whole(pltpu.SMEM)] + [whole(pl.ANY)] * len(after),
        out_specs=whole(),
        compiler_params=params(),
        cost_estimate=cost("mix"),
        name="table",
    )(plan, *after)


def local_kernel(count, heads_at, plan_ref, x_ref, *refs):
    out_ref, held, sems = refs[-3:]
    copies = []
    for j in range(count):
        start = pl.multiple_of(plan_ref[heads_at + j] * HD, HD)
        copies.append(
            pltpu.make_async_copy(x_ref.at[:, :, pl.ds(start, HD)], held.at[j], sems.at[j])
        )
        copies[-1].start()
    for copy in copies:
        copy.wait()
    for j in range(count):
        out_ref[j] = softmax_mix(held[j, 0], [held[j, 1]], [held[j, 2]], [None]).astype(BF16)


def attend_local(plan, x3, heads_at, count, after):
    planes, rows, _ = x3.shape
    return pl.pallas_call(
        functools.partial(local_kernel, count, heads_at),
        out_shape=jax.ShapeDtypeStruct((count, rows, HD), BF16),
        in_specs=[whole(pltpu.SMEM)] + [whole(pl.ANY)] * (1 + len(after)),
        out_specs=whole(),
        scratch_shapes=[
            pltpu.VMEM((count, planes, rows, HD), BF16),
            pltpu.SemaphoreType.DMA((count,)),
        ],
        compiler_params=params(),
        cost_estimate=cost("local"),
        name="attend_local",
    )(plan, x3, *after)


def attend_kernel(count, q_offset, offsets, always, bias_at, cond_at, table_ref, q_ref, *refs):
    sources = len(offsets)
    kv_refs = refs[:sources]
    halves = cond_at is not None
    outs = refs[-2:] if halves else refs[-1:]

    def one(j):
        keys = [ref[o + j, 0] for ref, o in zip(kv_refs, offsets)]
        values = [ref[o + j, 1] for ref, o in zip(kv_refs, offsets)]
        first = bias_at + j * len(DISTANCES)
        biases = [
            None if k == always else table_ref[pl.ds(first + k, 1), :] for k in range(sources)
        ]
        out = softmax_mix(q_ref[q_offset + j, 0], keys, values, biases)
        if halves:
            half = out.shape[0] // 2
            low, high = out[:half], out[half:]
            is_first = table_ref[cond_at : cond_at + 1, :HD] > 0.0
            outs[0][j] = jnp.where(is_first, low, high).astype(BF16)
            outs[1][j] = jnp.where(is_first, high, low).astype(BF16)
        else:
            outs[0][j] = out.astype(BF16)

    pairs = 0 if count * sources <= UNROLLED_BLOCKS else count // 2

    def two(i, carry):
        one(2 * i)
        one(2 * i + 1)
        return carry

    if pairs:
        lax.fori_loop(0, pairs, two, 0)
    for j in range(2 * pairs, count):
        one(j)


def attend_slots(table, q, q_offset, sources, always, count, bias_at, cond_at, after):
    rows = q.shape[-2]
    if cond_at is None:
        out_shape = jax.ShapeDtypeStruct((count, rows, HD), BF16)
        out_specs = whole()
    else:
        out_shape = [jax.ShapeDtypeStruct((count, rows // 2, HD), BF16)] * 2
        out_specs = [whole()] * 2
    arrays = [array for array, _ in sources]
    offsets = [offset for _, offset in sources]
    return pl.pallas_call(
        functools.partial(attend_kernel, count, q_offset, offsets, always, bias_at, cond_at),
        out_shape=out_shape,
        in_specs=[whole()] * (2 + len(arrays)) + [whole(pl.ANY)] * len(after),
        out_specs=out_specs,
        compiler_params=params(),
        cost_estimate=cost("own" if cond_at is None else "across"),
        name="attend",
    )(table, q, *arrays, *after)


def blend(cond, uncond, strength):
    cond = cond.astype(F32)
    uncond = uncond.astype(F32)
    return (uncond + strength * (cond - uncond)).astype(BF16)


def mix_branches(rows_at, table_ref, mine, other):
    strength = table_ref[rows_at.strength : rows_at.strength + 1, :HD]
    is_cond = table_ref[rows_at.cond : rows_at.cond + 1, :HD] > 0.0
    mine = mine.astype(F32)
    other = other.astype(F32)
    return blend(jnp.where(is_cond, mine, other), jnp.where(is_cond, other, mine), strength)


def mix_kernel(rows_at, pieces, table_ref, mine_ref, *refs):
    out_ref = refs[-1]
    j = 0
    for other_ref in refs[:pieces]:
        for i in range(other_ref.shape[0]):
            out_ref[j] = mix_branches(rows_at, table_ref, mine_ref[j], other_ref[i])
            j += 1


def mix_cores(table, rows_at, mine, others, after):
    return pl.pallas_call(
        functools.partial(mix_kernel, rows_at, len(others)),
        out_shape=jax.ShapeDtypeStruct(mine.shape, mine.dtype),
        in_specs=[whole()] * (2 + len(others)) + [whole(pl.ANY)] * len(after),
        out_specs=whole(),
        compiler_params=params(),
        cost_estimate=cost("mix"),
        name="mix",
    )(table, mine, *others, *after)


def assemble_kernel(at, rows_at, sizes, slots, places, plan_in, table_ref, *refs):
    out_ref, plan_ref, listed, turned, plan_sem, out_sems = refs[-6:]
    get_plan = pltpu.make_async_copy(plan_in, plan_ref, plan_sem.at[0])
    get_plan.start()
    own_count, raw_count, cross_count = sizes
    refs = list(refs[:-6])

    def take(count):
        taken = refs[:count]
        del refs[:count]
        return taken

    own, raw, raw_other = take(own_count), take(raw_count), take(raw_count)
    kept, moved, local = take(cross_count), take(cross_count), refs
    for ref, first in zip(own, places[0]):
        for j in range(ref.shape[0]):
            listed[first + j] = ref[j]
    for ref in local:
        for j in range(ref.shape[0]):
            listed[2 * slots + j] = ref[j]
    for ref, other, first in zip(raw, raw_other, places[1]):
        for j in range(ref.shape[0]):
            listed[first + j] = mix_branches(rows_at, table_ref, ref[j], other[j])
    get_plan.wait()
    column, branch = plan_ref[at.column], plan_ref[at.branch]
    for ref, other, first in zip(kept, moved, places[2]):
        half = ref.shape[1]
        here = pl.multiple_of(branch * half, half)
        there = pl.multiple_of((1 - branch) * half, half)
        for j in range(ref.shape[0]):
            listed[slots + first + j, pl.ds(here, half)] = ref[j]
            listed[slots + first + j, pl.ds(there, half)] = other[j]
    per_half = turned.shape[1]
    count = turned.shape[2] // HD * per_half
    spots = []
    for t in range(count):
        p = plan_ref[at.pos + t]
        slot = lax.shift_right_logical(p, 1)
        paired = jnp.where(jnp.bitwise_and(p, 1) == column, slot, slots + slot)
        spots.append(jnp.where(p >= 2 * slots, p, paired))
    parts = out_sems.shape[0]
    size = turned.shape[0] // parts
    copies = []
    for r in range(parts):
        tokens = slice(r * size, (r + 1) * size)
        for s in range(count // per_half):
            picked = [listed[spots[s * per_half + a], tokens] for a in range(per_half)]
            turned[tokens, :, s * HD : (s + 1) * HD] = jnp.swapaxes(jnp.stack(picked), 0, 1)
        copies.append(
            pltpu.make_async_copy(turned.at[tokens], out_ref.at[tokens], out_sems.at[r])
        )
        copies[-1].start()
    for copy in copies:
        copy.wait()


def ranked_body(rungs, qkv, timestep, windows, segments):
    rows = qkv.shape[1]
    heads = windows.shape[0]
    seq_count = lax.axis_size("seq")
    frame_count = lax.axis_size("frame")
    cfg_count = lax.axis_size("cfg")
    per_half = heads // (seq_count * cfg_count)
    outs = seq_count * per_half
    at = Layout(heads, outs)
    rows_at = Rows(heads)
    x3 = pltpu.with_memory_space_constraint(jnp.transpose(qkv[0], (1, 0, 2)), pltpu.HBM)
    lead, base = rungs[0][1] // 2, rungs[0][0] // 2
    plan, rung, kv_lead, kv_base = pl.pallas_call(
        functools.partial(plan_kernel, at, rungs, (seq_count, cfg_count)),
        out_shape=[
            jax.ShapeDtypeStruct((at.size,), jnp.int32),
            jax.ShapeDtypeStruct((1,), jnp.int32),
            jax.ShapeDtypeStruct((lead, 2, rows, HD), BF16),
            jax.ShapeDtypeStruct((base, 2, rows, HD), BF16),
        ],
        in_specs=[whole(pltpu.HBM)] * 3 + [whole(pl.ANY)],
        out_specs=[whole(pl.ANY)] * 2 + [whole()] * 2,
        scratch_shapes=[
            pltpu.SMEM(windows.shape, jnp.int32),
            pltpu.SMEM(segments.shape, jnp.int32),
            pltpu.SMEM(timestep.shape, jnp.int32),
            pltpu.SMEM((at.size,), jnp.int32),
            pltpu.SMEM((1,), jnp.int32),
            pltpu.SemaphoreType.DMA((3,)),
            pltpu.SemaphoreType.DMA((2,)),
            pltpu.SemaphoreType.DMA((lead + base,)),
        ],
        compiler_params=params(PLAN_VMEM_BYTES),
        name="plan",
    )(windows, segments, timestep, x3)

    grid_axes = ("seq", "frame")
    last = frame_count - 1
    apart = [(i, i - 1) for i in range(1, frame_count)] + [
        (frame_count + i, frame_count + i + 1) for i in range(last)
    ]
    onward = [(i, i + 1) for i in range(last)] + [
        (frame_count + i, frame_count + i - 1) for i in range(1, frame_count)
    ]

    def attempt(rung, plan, x3, kv_lead, kv_base):
        exchanged, wide = rung
        slots, far = exchanged // 2, wide // 2
        local = heads - exchanged
        bounds = [(0, lead), (lead, base)]
        if slots > base:
            bounds.append((base, slots))
        chunks = range(len(bounds))
        reaches = [far >= hi for _, hi in bounds]

        def cross(a):
            return lax.ppermute(a, "seq", SWAP)

        def mate(a):
            return lax.ppermute(a, "cfg", SWAP)

        def mix(mine, others, after):
            return mix_cores(table, rows_at, mine, others, after)

        across = [cross(kv_lead)]
        near_base = lax.ppermute(kv_base, grid_axes, apart)
        (kv_far,) = pack(plan, x3, [(range(at.mine, at.mine + lead), 1, 3)], [kv_base])
        far_own = [lax.ppermute(kv_far, grid_axes, onward)]
        split = base
        cut = 0
        parts = [(lead, split, 1), (split, base, 1)]
        parts += [(lo, hi, k) for k, (lo, hi) in enumerate(bounds) if k > 1]
        parts += [(0, cut, 0), (cut, lead, 0)]
        parts = [(lo, hi, k) for lo, hi, k in parts if hi > lo]
        later = [slot for lo, hi, _ in parts[1:] for slot in range(lo, hi)]
        jobs = [
            ([at.theirs + slot for slot in slots_of], 0, 1)
            for slots_of in (range(lead, split), later)
        ]
        jobs += [(range(at.theirs + lo, at.theirs + hi), 1, 3) for lo, hi in bounds[1:]]
        jobs += [(range(at.mine + lo, at.mine + hi), 1, 3) for lo, hi in bounds[2:]]
        jobs += [(range(at.mine + lead, at.mine + far), 1, 3)] if far > lead else []
        jobs.insert(0, (range(at.mine, at.mine + slots), 0, 1))
        q_own, q_early, q_late, *rest = pack(plan, x3, jobs, [kv_far])
        across += [cross(a) for a in rest[: len(bounds) - 1]]
        more = rest[len(bounds) - 1 :]
        if far > lead:
            far_own.append(lax.ppermute(more.pop(), grid_axes, onward))
        kv_more = more
        near_more = [lax.ppermute(a, grid_axes, apart) for a in kv_more]
        table = make_table(plan, at, rows_at, rows, [rest[0]])
        done = [table]
        if local:
            own_local = attend_local(plan, x3, at.order + exchanged, local, done)
            peer_local = mate(own_local)
            done = [own_local]

        near_across, far_across, guided = {}, {}, []
        (across[0],) = gate([across[0]], done)
        near_across[0] = lax.ppermute(across[0], grid_axes, onward)
        (q_early,) = gate([q_early], [across[0], *far_own])
        done = [q_early]
        q_early = cross(q_early)
        if local:
            guided = [mix(own_local, [peer_local], done)]
            done = guided
        (late,) = gate([across[0]], done)
        far_across[0] = lax.ppermute(late, grid_axes, apart)
        (across[1],) = gate([across[1]], [late, *done])
        done = [across[1]]
        for k in chunks[1:]:
            if k > 1:
                (across[k],) = gate([across[k]], done)
            done = [across[k]]
            near_across[k] = lax.ppermute(across[k], grid_axes, onward)
            if reaches[k]:
                far_across[k] = lax.ppermute(across[k], grid_axes, apart)
        (q_late,) = gate([q_late], [*done, near_across[0]])
        done = [q_late]
        q_late = cross(q_late)

        def attend_part(k, lo, hi, q, q_offset, names, bias_at, cond_at, after):
            skip = lo - bounds[k][0]
            arrays = {
                "O": (kv_more[0], skip) if k > 1 else (kv_base, lo),
                "X": (across[k], skip),
                "NO": (near_more[0], skip) if k > 1 else (near_base, lo),
                "NR": (near_across[k], skip),
                "FO": (far_own[min(k, 1)], max(lo - lead, 0)) if reaches[k] else None,
                "FR": (far_across.get(k), skip),
            }
            cut = slice(0, 5) if reaches[k] else slice(1, 4)
            sources = [arrays[name] for name in names[cut]]
            bias_at += lo * len(DISTANCES) + cut.start
            always = DISTANCES[cut].index(0)
            return attend_slots(
                table, q, q_offset, sources, always, hi - lo, bias_at, cond_at, after
            )

        def attend_own(k, after):
            lo, hi = bounds[k]
            return attend_part(k, lo, hi, q_own, lo, OWN_SOURCES, rows_at.own, None, after)

        def attend_across(part, after):
            lo, hi, k = parts[part]
            q = q_late if part else q_early
            offset = later.index(lo) if part else 0
            return attend_part(
                k, lo, hi, q, offset, ACROSS_SOURCES, rows_at.across, rows_at.cond, after
            )

        own, kept = {}, []
        own[0] = attend_own(0, done)
        keep, send = attend_across(0, [own[0]])
        got = mate(send)
        end = mix(own[0], [mate(own[0])], [keep])
        mixed = mix(keep, [got], [end])
        kept.append(cross(mixed))
        waiting = []
        done = [mixed]
        for part in range(1, len(parts)):
            keep, send = attend_across(part, done)
            middle = send.shape[0] // 2
            pieces = [send] if part < len(parts) - 1 else [send[:middle], send[middle:]]
            waiting.append((keep, [mate(piece) for piece in pieces]))
            done = [keep]
        done.append(kept[0])
        for keep, got in waiting:
            mixed = mix(keep, got, done)
            kept.append(cross(mixed))
            done = [mixed]
        raw = []
        for k in chunks[1:]:
            lo, hi = bounds[k]
            own[k] = attend_own(k, [mixed, kept[0]])
            middle = (hi - lo) // 2
            raw += [(lo, own[k][:middle]), (lo + middle, own[k][middle:])]
        others = [mate(a) for _, a in raw]
        arrays = [end, *[a for _, a in raw], *others, *kept, *[mate(a) for a in kept], *guided]
        places = ([0], [lo for lo, _ in raw], [lo for lo, _, _ in parts])
        sizes = tuple(len(firsts) for firsts in places)
        return pl.pallas_call(
            functools.partial(assemble_kernel, at, rows_at, sizes, slots, places),
            out_shape=pltpu.HBM((rows, per_half, seq_count * HD), BF16),
            in_specs=[whole(pl.ANY)] + [whole()] * (1 + len(arrays)),
            out_specs=whole(pltpu.HBM),
            scratch_shapes=[
                pltpu.SMEM(plan.shape, plan.dtype),
                pltpu.VMEM((heads, rows, HD), BF16),
                pltpu.VMEM((rows, per_half, seq_count * HD), BF16),
                pltpu.SemaphoreType.DMA((1,)),
                pltpu.SemaphoreType.DMA((4,)),
            ],
            compiler_params=params(),
            name="assemble",
        )(plan, table, *arrays)

    return lax.switch(
        rung[0],
        [functools.partial(attempt, rung) for rung in rungs],
        plan, x3, kv_lead, kv_base,
    )


def rungs_of(heads):
    third = heads // 3
    return ((2 * third + 2, third), (2 * third + 2, 2 * third + 2), (heads, heads))


def solution(mesh):
    sizes = dict(mesh.shape)

    def whole_body(qkv, timestep, windows, segments):
        frames_here = segments.shape[0] // sizes["frame"]
        one_frame = frames_here == sizes["seq"]
        if sizes["seq"] == 2 and sizes["cfg"] == 2 and one_frame and qkv.shape[1] % 32 == 0:
            return ranked_body(rungs_of(windows.shape[0]), qkv, timestep, windows, segments)
        return body(qkv, timestep, windows, segments)

    return jax.shard_map(
        whole_body,
        mesh=mesh,
        in_specs=(P("cfg", ("groups", "frame", "seq"), None, None), P("groups"), P(), P("groups")),
        out_specs=P(("groups", "frame", "seq"), "cfg", None),
        check_vma=False,
    )
```
